32 devices in a mesh: img: 8 (over z, y), grp: 4 (over x, core).
Axes of the slice: x: 2, y: 2, z: 4, core: 2. Of those that a mesh axis runs over, the one named last changes fastest.
Arguments:
- p2: bfloat16 [8, 4, 4096, 256], P('img', 'grp'), may hold values from -6 to 6
- p3: bfloat16 [8, 4, 1024, 256], P('img', 'grp'), may hold values from -6 to 6
- p4: bfloat16 [8, 4, 256, 256], P('img', 'grp'), may hold values from -6 to 6
- p5: bfloat16 [8, 4, 64, 256], P('img', 'grp'), may hold values from -6 to 6
- roi_boxes: int32 [8, 4, 5, 16], P('img', 'grp'), may hold values from 0 to 238, as said below
- recv_index: int32 [8, 4, 8], P('img', 'grp'), may hold values from 0 to 15, as said below
- classes: int32 [8, 4, 8], P('img', 'grp'), may hold values from 0 to 79
- targets: int32 [8, 4, 8, 784], P('img', 'grp'), may hold values 0 or 1
- conv_weights: bfloat16 [4, 2304, 256], replicated, may hold values from -0.125 to 0.125
- conv_biases: bfloat16 [4, 256], replicated, may hold values from -1.5 to 1.5
- deconv_weight: bfloat16 [256, 1024], replicated, may hold values from -0.375 to 0.375
- deconv_bias: bfloat16 [256], replicated, may hold values from -1.5 to 1.5
- predictor_weight: bfloat16 [256, 80], replicated, may hold values from -0.375 to 0.375
- predictor_bias: bfloat16 [80], replicated, may hold values from -4 to 4
Outputs:
- masks: float32 [8, 4, 16, 784], P('img', 'grp')
- grad_p2: float32 [8, 4, 4096, 256], P('img', 'grp')
- grad_p3: float32 [8, 4, 1024, 256], P('img', 'grp')
- grad_p4: float32 [8, 4, 256, 256], P('img', 'grp')
- grad_p5: float32 [8, 4, 64, 256], P('img', 'grp')
- grad_conv_weights: float32 [4, 2304, 256], replicated
- grad_conv_biases: float32 [4, 256], replicated
- grad_deconv_weight: float32 [256, 1024], replicated
- grad_deconv_bias: float32 [256], replicated
- grad_predictor_weight: float32 [256, 80], replicated
- grad_predictor_bias: float32 [80], replicated
The draws below stay inside these ranges and needn't reach their ends.
Inputs may be any that keep to these rules, and one draw needn't show every extreme that they name: `roi_boxes`: level 0 to 3 means P2 to P5; steps are 1 or more; every sample stays within its level so that y0 + 13 sy <= 4 (64 >> L) - 5, likewise for x. `recv_index`: A device's 8 entries are distinct; entry e names the slot e % 2 sent to it by device e // 2 of img in its group; no slot is named by two devices; the RoIs each image has processed vary from image to image.
All inputs are finite; a program needn't handle non-finite values. No bound on the sum of `targets` on one device may be relied on, other than what follows from the above.
Results may differ from the reference program's by a relative error of at most 0.015.
Values may be sent and summed in bfloat16 or wider, within the bound.
A program may use at most 192 MiB of HBM per device.

```python
import jax
import jax.numpy as jnp
from jax import lax

C = 256
K = 80
POOL = 14
LAYERS = 4
S2 = 64
R_BAL = 8
MASK = 28
PAIR = 2
SLOTS = 16
CELLS = 5440
IMG_ROWS = 8
IMG_COLS = 4


def draw_roi_boxes(key, part):
    key = jax.random.fold_in(key, 11)
    subkeys = jax.random.split(key, 5)
    shape_one = (IMG_ROWS, IMG_COLS, SLOTS)
    first_slot = (jnp.arange(SLOTS, dtype=jnp.int32) == 0)[None, None, :]
    level_id = jax.random.randint(subkeys[0], shape_one, 0, 4)
    level_id = jnp.where(first_slot, 0, level_id).astype(jnp.int32)
    side_cells = S2 // jnp.left_shift(jnp.int32(1), level_id)
    limit_q = 4 * side_cells - 5
    most_step = limit_q // 13
    step_y = jax.random.randint(subkeys[1], shape_one, 1, most_step + 1)
    step_y = jnp.where(first_slot, 1, step_y).astype(jnp.int32)
    step_x = jax.random.randint(subkeys[2], shape_one, 1, most_step + 1)
    start_y = jax.random.randint(subkeys[3], shape_one, 0, limit_q - 13 * step_y + 1)
    start_y = jnp.where(first_slot, limit_q - 13, start_y).astype(jnp.int32)
    start_x = jax.random.randint(subkeys[4], shape_one, 0, limit_q - 13 * step_x + 1)
    return jnp.stack([level_id, start_y, start_x, step_y, step_x], axis=2).astype(jnp.int32)


def one_group(group_key):
    band = R_BAL // PAIR
    key_amount, key_flip, key_source, key_dest, key_order = jax.random.split(group_key, 5)
    device = jnp.arange(IMG_ROWS, dtype=jnp.int32)
    low_side = device % (2 * band) < band
    partner = jnp.where(low_side, device + band, device - band)
    pair_id = device // (2 * band) * band + device % band
    amounts = jax.random.randint(key_amount, (IMG_ROWS // 2,), 0, band)
    flips = jax.random.randint(key_flip, (IMG_ROWS // 2,), 0, 2)
    moved = amounts[pair_id]
    giver = low_side.astype(jnp.int32) ^ flips[pair_id] == 1
    column = jnp.arange(IMG_ROWS, dtype=jnp.int32)
    own_pos = (column[None, :] - device[:, None]) % IMG_ROWS
    partner_pos = (column[None, :] - partner[:, None]) % IMG_ROWS
    keep_own = (own_pos < band) & jnp.logical_not(giver[:, None] & (own_pos < moved[:, None]))
    taken = (partner_pos < band) & jnp.logical_not(giver)[:, None] & (partner_pos < moved[:, None])
    load = jnp.where(keep_own | taken, PAIR, 0)
    load = load[jax.random.permutation(key_source, IMG_ROWS)][:, jax.random.permutation(key_dest, IMG_ROWS)]
    live = (jnp.arange(PAIR, dtype=jnp.int32)[None, None, :] < load.T[:, :, None]).reshape(IMG_ROWS, SLOTS)
    ranks = jax.vmap(lambda order_key: jax.random.permutation(order_key, SLOTS))(jax.random.split(key_order, IMG_ROWS))
    scores = (1 - live.astype(jnp.int32)) * SLOTS + ranks
    return jnp.argsort(scores, axis=1)[:, :R_BAL].astype(jnp.int32)


def draw_recv_index(key, part):
    key = jax.random.fold_in(key, 23)
    chosen = jax.vmap(one_group)(jax.random.split(key, IMG_COLS))
    return jnp.transpose(chosen, (1, 0, 2)).astype(jnp.int32)


def plant(array, rng, smallest, top_value):
    shape = array.shape
    index_at = [jax.random.randint(jax.random.fold_in(rng, axis), (), 0, shape[axis]) for axis in range(len(shape))]
    array = array.at[tuple(index_at)].set(smallest)
    longest = shape.index(max(shape))
    index_at[longest] = (index_at[longest] + 1) % shape[longest]
    return array.at[tuple(index_at)].set(top_value)


def shard_levels(own_key, shape, cuts, low, top_value):
    def one(position, parts):
        steps = jax.random.uniform(jax.random.fold_in(jax.random.fold_in(own_key, 6), position), (parts,), jnp.float32, low / len(cuts), top_value / len(cuts))
        return jnp.repeat(jnp.exp(steps), shape[position] // parts).reshape((-1,) + (1,) * (len(shape) - position - 1))

    loudness = one(*cuts[0])
    for cut in cuts[1:]:
        loudness = loudness * one(*cut)
    return loudness


def bell_draw(own_key, dims, scale, bound, cuts=(), held_as=jnp.bfloat16):
    array = jax.random.normal(own_key, dims, jnp.float32) * scale
    if len(cuts) > 0:
        array = shard_levels(own_key, dims, cuts, -0.22, 0.18) * array
    return jnp.clip(array, min=-bound, max=bound).astype(held_as)


def setup_inputs(seed: int = 0) -> dict:
    key_list = jax.random.split(jax.random.key(seed), 15)
    return {
        "p2": bell_draw(key_list[0], (IMG_ROWS, IMG_COLS, S2 * S2, C), 1.0, 6.0, ((0, 8), (1, 4))),
        "p3": bell_draw(key_list[1], (IMG_ROWS, IMG_COLS, (S2 // 2) * (S2 // 2), C), 1.0, 6.0, ((0, 8), (1, 4))),
        "p4": bell_draw(key_list[2], (IMG_ROWS, IMG_COLS, (S2 // 4) * (S2 // 4), C), 1.0, 6.0, ((0, 8), (1, 4))),
        "p5": bell_draw(key_list[3], (IMG_ROWS, IMG_COLS, (S2 // 8) * (S2 // 8), C), 1.0, 6.0, ((0, 8), (1, 4))),
        "roi_boxes": draw_roi_boxes(jax.random.fold_in(key_list[14], 71), 0),
        "recv_index": draw_recv_index(jax.random.fold_in(key_list[14], 71), 0),
        "classes": plant(jax.random.randint(key_list[6], (IMG_ROWS, IMG_COLS, R_BAL), 0, K), jax.random.fold_in(key_list[6], 1), 0, K - 1).astype(jnp.int32),
        "targets": plant((jax.random.randint(key_list[7], (IMG_ROWS, IMG_COLS, R_BAL, MASK * MASK), 0, 2) < 1).astype(jnp.int32), jax.random.fold_in(key_list[7], 1), 0, 1),
        "conv_weights": bell_draw(key_list[8], (LAYERS, 9 * C, C), (9 * C) ** -0.5, 0.125),
        "conv_biases": bell_draw(key_list[9], (LAYERS, C), 0.3, 1.5),
        "deconv_weight": bell_draw(key_list[10], (C, 4 * C), C ** -0.5, 0.375),
        "deconv_bias": bell_draw(key_list[11], (C,), 0.3, 1.5),
        "predictor_weight": bell_draw(key_list[12], (C, K), C ** -0.5, 0.375),
        "predictor_bias": bell_draw(key_list[13], (K,), 1.0, 4.0),
    }


@jax.custom_vjp
def low(v):
    return lax.optimization_barrier(v.astype(jnp.bfloat16)).astype(jnp.float32)

@jax.custom_vjp
def low_back(v):
    return v

def low_keep(v):
    return (low(v), None)

def low_pass(kept, grad):
    return (grad,)

def back_keep(v):
    return (v, None)

def back_low(kept, grad):
    return (low(grad),)
low.defvjp(low_keep, low_pass)
low_back.defvjp(back_keep, back_low)

def level_offsets(level_id):
    first_end = S2 * S2
    second_end = first_end + S2 // 2 * (S2 // 2)
    third_end = second_end + S2 // 4 * (S2 // 4)
    return jnp.where(level_id == 0, 0, jnp.where(level_id == 1, first_end, jnp.where(level_id == 2, second_end, third_end))).astype(jnp.int32)

def sample_points(boxes):
    level_id = boxes[0]
    side_cells = (S2 // jnp.left_shift(jnp.int32(1), level_id)).astype(jnp.int32)
    sample_steps = jnp.arange(POOL, dtype=jnp.int32)
    quarter_y = boxes[1][:, None] + sample_steps[None, :] * boxes[3][:, None]
    quarter_x = boxes[2][:, None] + sample_steps[None, :] * boxes[4][:, None]
    weight_y = ((quarter_y % 4).astype(jnp.float32) * 0.25)[:, :, None]
    weight_x = ((quarter_x % 4).astype(jnp.float32) * 0.25)[:, None, :]
    stride = side_cells[:, None, None]
    base_row = level_offsets(level_id)[:, None, None] + (quarter_y // 4)[:, :, None] * stride + (quarter_x // 4)[:, None, :]
    row_index = jnp.stack([base_row, base_row + 1, base_row + stride, base_row + stride + 1]).reshape(4, -1, POOL * POOL)
    corner_weights = jnp.stack([(1.0 - weight_y) * (1.0 - weight_x), (1.0 - weight_y) * weight_x, weight_y * (1.0 - weight_x), weight_y * weight_x]).reshape(4, -1, POOL * POOL)
    return (row_index.astype(jnp.int32), corner_weights)

def pool_blocks(feature_table, boxes):
    row_index, corner_weights = sample_points(boxes)
    pooled = jnp.zeros((row_index.shape[1], POOL * POOL, feature_table.shape[1]), jnp.float32)
    for corner in range(4):
        pooled = pooled + corner_weights[corner][:, :, None] * feature_table[row_index[corner]]
    return pooled

def patches(hidden):
    padded = jnp.pad(hidden, ((0, 0), (1, 1), (1, 1), (0, 0)))
    pieces = [padded[:, row_off:row_off + POOL, col_off:col_off + POOL, :] for row_off in range(3) for col_off in range(3)]
    return jnp.concatenate(pieces, axis=-1).reshape(hidden.shape[0] * POOL * POOL, -1)

def head(blocks, class_ids, target_bits, conv_w, conv_b, dec_w, dec_b, pred_w, pred_b):
    roi_count = blocks.shape[0]
    hidden = blocks.reshape(roi_count, POOL, POOL, -1)
    for layer_idx in range(LAYERS):
        pre_act = low_back(jnp.dot(patches(hidden), conv_w[layer_idx], precision=lax.Precision.HIGHEST) + conv_b[layer_idx])
        hidden = low(jax.nn.gelu(pre_act)).reshape(roi_count, POOL, POOL, -1)
    deconv_pre = low_back(jnp.dot(hidden.reshape(roi_count * POOL * POOL, -1), dec_w, precision=lax.Precision.HIGHEST) + jnp.tile(dec_b, 4))
    upsampled = low(jax.nn.gelu(deconv_pre)).reshape(roi_count, POOL, POOL, 2, 2, -1)
    upsampled = upsampled.transpose(0, 1, 3, 2, 4, 5).reshape(roi_count, MASK * MASK, -1)
    class_weight = pred_w[:, class_ids].T
    logits = low_back(jnp.einsum('rpc,rc->rp', upsampled, class_weight, precision=lax.Precision.HIGHEST) + pred_b[class_ids][:, None])
    target_vals = target_bits.astype(jnp.float32)
    loss = jnp.sum(jax.nn.softplus(logits) - target_vals * logits) / (MASK * MASK)
    return (loss, jax.nn.sigmoid(logits))

def reference(p2, p3, p4, p5, roi_boxes, recv_index, classes, targets, conv_weights, conv_biases, deconv_weight, deconv_bias, predictor_weight, predictor_bias):
    devices_all = IMG_ROWS * IMG_COLS
    tables = jnp.concatenate([p2, p3, p4, p5], axis=2).astype(jnp.float32).reshape(devices_all, CELLS, C)
    boxes_flat = roi_boxes.reshape(devices_all, 5, SLOTS)
    dest_img = jnp.arange(IMG_ROWS, dtype=jnp.int32)[:, None, None]
    group_idx = jnp.arange(IMG_COLS, dtype=jnp.int32)[None, :, None]
    source_flat = (recv_index // PAIR * IMG_COLS + group_idx).astype(jnp.int32)
    source_slot = (dest_img * PAIR + recv_index % PAIR).astype(jnp.int32)
    classes_flat = classes.reshape(devices_all, R_BAL)
    targets_flat = targets.reshape(devices_all, R_BAL, MASK * MASK)

    def forward(table_all, conv_w, conv_b, dec_w, dec_b, pred_w, pred_b):

        def pool_item(item):
            return pool_blocks(item[0], item[1])
        pooled = lax.map(jax.checkpoint(pool_item), (table_all, boxes_flat))
        pooled = low_back(low(pooled))
        picked = pooled[source_flat, source_slot].reshape(devices_all, R_BAL, POOL * POOL, C)

        def head_item(item):
            return head(item[0], item[1], item[2], conv_w, conv_b, dec_w, dec_b, pred_w, pred_b)
        losses, mask_probs = lax.map(jax.checkpoint(head_item), (picked, classes_flat, targets_flat))
        return (jnp.sum(losses), mask_probs)
    params = (conv_weights.astype(jnp.float32), conv_biases.astype(jnp.float32), deconv_weight.astype(jnp.float32), deconv_bias.astype(jnp.float32), predictor_weight.astype(jnp.float32), predictor_bias.astype(jnp.float32))
    loss, pullback, mask_probs = jax.vjp(forward, tables, *params, has_aux=True)
    grads = pullback(jnp.ones_like(loss))
    masks = jnp.zeros((devices_all, SLOTS, MASK * MASK), jnp.float32)
    masks = masks.at[source_flat, source_slot].set(mask_probs.reshape(IMG_ROWS, IMG_COLS, R_BAL, MASK * MASK))
    masks = masks.reshape(IMG_ROWS, IMG_COLS, SLOTS, MASK * MASK)
    grad_tables = grads[0].reshape(IMG_ROWS, IMG_COLS, CELLS, C)
    first_end = S2 * S2
    second_end = first_end + S2 // 2 * (S2 // 2)
    third_end = second_end + S2 // 4 * (S2 // 4)
    return (masks, grad_tables[:, :, :first_end], grad_tables[:, :, first_end:second_end], grad_tables[:, :, second_end:third_end], grad_tables[:, :, third_end:], grads[1], grads[2], grads[3], grads[4], grads[5], grads[6])
```

```python
import functools

import jax
import jax.numpy as jnp
from jax import lax
from jax.experimental import pallas as pl
from jax.experimental.pallas import tpu as pltpu
from jax.sharding import PartitionSpec as P

MESH = pl.DeviceIdType.MESH
POOL = 14
LAYERS = 4
S2 = 64
MASK = 28
C = 256
WIDE = 16
TOK = POOL * WIDE
XROWS = 272
DROWS = 288
WIN = 128
CHUNK = 16
GA = 0.7978845608028654
GB = GA * 0.044715
BF = jnp.bfloat16
F32 = jnp.float32


def dot(a, b):
    return jnp.dot(a, b, preferred_element_type=F32)


def dot_nt(a, b):
    return lax.dot_general(a, b, (((1,), (1,)), ((), ())), preferred_element_type=F32)


def dot_tn(a, b):
    return lax.dot_general(a, b, (((0,), (0,)), ((), ())), preferred_element_type=F32)


def gelu_both(x):
    square = x * x
    gate = 0.5 + 0.5 * jnp.tanh(x * (GA + GB * square))
    value = x * gate
    slope = gate + (value - value * gate) * (2 * GA + 6 * GB * square)
    return value, slope


def exchange_kernel(n, src, dst, send_sem, recv_sem, own_sem):
    me = lax.axis_index("img")
    grp = lax.axis_index("grp")
    barrier = pltpu.get_barrier_semaphore()
    for k in range(1, n):
        pl.semaphore_signal(barrier, inc=1, device_id=(lax.rem(me + k, n), grp), device_id_type=MESH)
    own = pltpu.make_async_copy(src.at[me], dst.at[me], own_sem)
    own.start()
    pl.semaphore_wait(barrier, n - 1)
    copies = []
    for k in range(1, n):
        peer = lax.rem(me + k, n)
        copy = pltpu.make_async_remote_copy(
            src_ref=src.at[peer],
            dst_ref=dst.at[me],
            send_sem=send_sem.at[k - 1],
            recv_sem=recv_sem.at[k - 1],
            device_id=(peer, grp),
            device_id_type=MESH,
        )
        copy.start()
        copies.append(copy)
    for copy in copies:
        copy.wait()
    own.wait()


def exchange(n, blocks):
    return pl.pallas_call(
        functools.partial(exchange_kernel, n),
        out_shape=jax.ShapeDtypeStruct(blocks.shape, blocks.dtype),
        in_specs=[pl.BlockSpec(memory_space=pl.ANY)],
        out_specs=pl.BlockSpec(memory_space=pl.ANY),
        scratch_shapes=[
            pltpu.SemaphoreType.DMA((n - 1,)),
            pltpu.SemaphoreType.DMA((n - 1,)),
            pltpu.SemaphoreType.DMA,
        ],
        compiler_params=pltpu.CompilerParams(collective_id=0, has_side_effects=True),
        name="exchange",
    )(blocks)


class Sampler:
    def __init__(self, boxes, slot):
        level = boxes[0, slot]
        self.level = level
        self.y0, self.x0 = boxes[1, slot], boxes[2, slot]
        self.sy, self.sx = boxes[3, slot], boxes[4, slot]
        self.shift = 6 - level
        self.side = jnp.left_shift(1, self.shift)
        self.offset = jnp.where(level == 0, 0, jnp.where(level == 1, 4096, jnp.where(level == 2, 5120, 5376)))
        self.cell = lax.broadcasted_iota(jnp.int32, (WIDE, WIN), 1)
        self.column = (self.cell & (self.side - 1)).astype(F32)
        self.band = lax.shift_right_logical(self.cell, self.shift)

    def across(self, moved):
        j = lax.broadcasted_iota(jnp.int32, (WIDE, WIN), 0) + moved
        at = jnp.where((j >= 0) & (j < POOL), self.x0 + j * self.sx, -64).astype(F32) * 0.25
        return jnp.maximum(1.0 - jnp.abs(at - self.column), 0.0)

    def down(self, i):
        qy = self.y0 + i * self.sy
        base = self.offset + jnp.left_shift(lax.shift_right_logical(qy, 2), self.shift)
        start = pl.multiple_of(jnp.left_shift(lax.shift_right_logical(base, 4), 4), 16)
        lead = lax.shift_right_logical(base - start, self.shift)
        fraction = (qy & 3).astype(F32) * 0.25
        row = self.band - lead
        return start, jnp.where(row == 0, 1.0 - fraction, jnp.where(row == 1, fraction, 0.0))


def head_kernel(
    slots,
    classes_all,
    boxes,
    flags,
    info,
    p2,
    p3,
    p4,
    p5,
    conv_w,
    conv_b,
    dec_w,
    dec_b,
    pred_w,
    pred_b,
    probs,
    g2,
    g3,
    g4,
    g5,
    grads,
    order,
    table,
    table_grad,
    xw,
    xt,
    slope,
    dx,
    dpw,
    dx0,
    up,
    up_slope,
    dpd,
    x4t,
    acc,
    acc_dec,
    misc,
    bias2,
    bias_d,
    stage,
    in_sem,
    out_sem,
    stage_sem,
):
    chunk = min(CHUNK, slots)
    chunks = slots // chunk
    cells = p2.shape[0] + p3.shape[0] + p4.shape[0] + p5.shape[0]
    parts = []
    at = 0
    for k, part in enumerate((p2, p3, p4, p5)):
        parts.append(pltpu.make_async_copy(part, table.at[pl.ds(at, part.shape[0])], in_sem.at[k]))
        parts[-1].start()
        at += part.shape[0]

    def collect(slot, count):
        order[count] = slot
        return count + flags[slot, 1]

    count = lax.fori_loop(0, slots, collect, 0)
    order[count] = 0

    table[cells:, :] = jnp.zeros((table.shape[0] - cells, C), BF)
    table_grad[...] = jnp.zeros_like(table_grad)
    probs[...] = jnp.zeros_like(probs)
    xw[...] = jnp.zeros_like(xw)
    dpw[...] = jnp.zeros_like(dpw)
    dpd[...] = jnp.zeros_like(dpd)
    acc[...] = jnp.zeros_like(acc)
    acc_dec[...] = jnp.zeros_like(acc_dec)
    misc[...] = jnp.zeros_like(misc)
    col = lax.broadcasted_iota(jnp.int32, (TOK, C), 0) & (WIDE - 1)
    off_block = jnp.where(col < POOL, 0.0, -1e4)
    for layer in range(LAYERS):
        bias2[layer] = off_block + conv_b[layer : layer + 1, :].astype(F32)
    bias_d[...] = off_block + dec_b[...].astype(F32)
    lane_ok = (lax.broadcasted_iota(jnp.int32, (8, TOK), 1) & (WIDE - 1)) < POOL
    row_ok = lax.broadcasted_iota(jnp.int32, (8, TOK), 0) < 4
    live = (lane_ok & row_ok).astype(F32)
    for part in parts:
        part.wait()

    def spread(ref, k, value, first, last):
        ref[k, 16 : 16 + TOK, C : 2 * C] = value.astype(BF)
        ref[k, 16 : 16 + TOK, first * C : (first + 1) * C] = pltpu.roll(value, 1, 0).astype(BF)
        ref[k, 16 : 16 + TOK, last * C : (last + 1) * C] = pltpu.roll(value, TOK - 1, 0).astype(BF)

    def forward(base):
        def pair(p, _):
            for k in range(2):
                n = 2 * p + k
                slot = order[base + n]
                sampler = Sampler(boxes, slot)
                across = jnp.concatenate([sampler.across(-1), sampler.across(0), sampler.across(1)], axis=0)
                for i in range(POOL):
                    start, down = sampler.down(i)
                    weights = across * jnp.concatenate([down] * 3, axis=0)
                    sampled = dot(weights.astype(BF), table[pl.ds(start, WIN), :]).astype(BF)
                    for b in range(3):
                        xw[k, 16 * (i + 1) : 16 * (i + 2), b * C : (b + 1) * C] = sampled[b * WIDE : (b + 1) * WIDE]
            for layer in range(LAYERS):
                for k in range(2):
                    n = 2 * p + k
                    xt[layer, n] = xw[k, 16:XROWS, C : 2 * C].T
                    wide = jnp.concatenate([xw[k, 16 * ky : 16 * ky + TOK] for ky in range(3)], axis=1)
                    pre = dot(wide, conv_w[layer]) + bias2[layer]
                    value, slope_now = gelu_both(pre)
                    slope[layer, n] = slope_now.astype(BF)
                    spread(xw, k, value, 0, 2)
            for k in range(2):
                n = 2 * p + k
                index = base + n
                valid = (index < count).astype(F32)
                slot = jnp.where(index < count, order[index], slots)
                class_id = flags[order[index], 0]
                x4 = xw[k, 16 : 16 + TOK, C : 2 * C]
                x4t[k] = xw[k, 16:XROWS, C : 2 * C].T
                for ab in range(4):
                    pre = dot(x4, dec_w[:, ab * C : (ab + 1) * C]) + bias_d[...]
                    value, slope_now = gelu_both(pre)
                    up[k, :, ab * C : (ab + 1) * C] = value.astype(BF)
                    up_slope[k, :, ab * C : (ab + 1) * C] = slope_now.astype(BF)
                picks = (lax.broadcasted_iota(jnp.int32, (16, classes_all), 1) == class_id).astype(F32)
                bias = jnp.sum(picks[0:1] * pred_b[...].astype(F32), axis=1, keepdims=True)
                weight = dot_nt(picks.astype(BF), pred_w[...])
                row = lax.broadcasted_iota(jnp.int32, (16, C), 0)
                blocks = jnp.concatenate([jnp.where(row == ab, weight, 0.0) for ab in range(4)], axis=1).astype(BF)
                logit = dot_nt(blocks, up[k])[0:8] + bias
                prob = 1.0 / (1.0 + jnp.exp(-logit))
                probs[slot] = prob
                target = info[order[index], :, 0:TOK]
                d_logit = ((prob - target) * (valid / (MASK * MASK)) * live).astype(BF)
                d_logit_f = d_logit.astype(F32)
                d16 = jnp.concatenate([d_logit_f, jnp.zeros((8, TOK), F32)], axis=0).astype(BF)
                outer = dot(d16, up[k])
                gathered = jnp.zeros((16, C), F32)
                for ab in range(4):
                    gathered += jnp.where(row == ab, outer[:, ab * C : (ab + 1) * C], 0.0)
                misc[pl.ds(class_id, 1), :] += jnp.sum(gathered, axis=0, keepdims=True)
                total = jnp.sum(jnp.sum(d_logit_f, axis=1, keepdims=True), axis=0, keepdims=True)
                lane = lax.broadcasted_iota(jnp.int32, (1, C), 1)
                misc[classes_all + 8 : classes_all + 9, :] += jnp.where(lane == class_id, total, 0.0)
                grad = jnp.zeros((TOK, C), F32)
                for ab in range(4):
                    cols = slice(ab * C, (ab + 1) * C)
                    d_up = dot_tn(d16, blocks[:, cols])
                    d_pre = d_up * up_slope[k, :, cols].astype(F32)
                    misc[classes_all + 16 : classes_all + 24, :] += jnp.sum(d_pre.reshape(TOK // 8, 8, C), axis=0)
                    d_pre = d_pre.astype(BF)
                    dpd[k, 0:TOK, cols] = d_pre
                    grad += dot_nt(d_pre, dec_w[:, cols])
                dx[n] = grad
            lhs = jnp.concatenate([x4t[0], x4t[1]], axis=1)
            for ab in range(4):
                cols = slice(ab * C, (ab + 1) * C)
                rhs = jnp.concatenate([dpd[0, :, cols], dpd[1, :, cols]], axis=0)
                acc_dec[ab] += dot(lhs, rhs)
            return 0

        return pair

    def back_inputs(layer):
        def pair(p, _):
            for k in range(2):
                n = 2 * p + k
                d_pre = dx[n] * slope[layer, n].astype(F32)
                rows = slice(classes_all + 24 + 8 * layer, classes_all + 32 + 8 * layer)
                misc[rows, :] += jnp.sum(d_pre.reshape(TOK // 8, 8, C), axis=0)
                spread(dpw, n, d_pre, 2, 0)
                grad = jnp.zeros((TOK, C), F32)
                for ky in range(3):
                    for kx in range(3):
                        tap = 3 * ky + kx
                        part = dpw[n, 32 - 16 * ky : 32 - 16 * ky + TOK, kx * C : (kx + 1) * C]
                        grad += dot_nt(part, conv_w[layer, tap * C : (tap + 1) * C, :])
                if layer > 0:
                    dx[n] = grad
                else:
                    dx0[n] = grad.astype(BF)
            return 0

        return pair

    def back_weights(layer):
        kept = layer if chunks > 1 else 0

        def pair(p, _):
            lhs = jnp.concatenate([xt[layer, 2 * p], xt[layer, 2 * p + 1]], axis=1)
            for ky in range(3):
                rows = slice(32 - 16 * ky, 288 - 16 * ky)
                for kx in range(3):
                    cols = slice(kx * C, (kx + 1) * C)
                    tap = 3 * ky + kx
                    rhs = jnp.concatenate([dpw[2 * p, rows, cols], dpw[2 * p + 1, rows, cols]], axis=0)
                    acc[kept, tap * C : (tap + 1) * C, :] += dot(lhs, rhs)
            return 0

        return pair

    def scatter(base):
        def one(n, _):
            slot = order[base + n]
            sampler = Sampler(boxes, slot)
            across = sampler.across(0)

            def rows_of(size):
                def run():
                    for i in range(POOL):
                        start, down = sampler.down(i)
                        weights = (across * down).astype(BF)[:, 0:size]
                        back = dot_tn(weights, dx0[n, i * WIDE : (i + 1) * WIDE, :])
                        table_grad[pl.ds(start, size), :] += back

                return run

            pl.when(sampler.level == 0)(rows_of(128))
            pl.when(sampler.level != 0)(rows_of(128))
            return 0

        return one

    staged = [0]

    def wait_stage():
        pltpu.make_async_copy(stage.at[0], grads.at[pl.ds(0, C)], stage_sem.at[0]).wait()

    def put_rows(read, first, blocks):
        for b in range(blocks):
            kept = staged[0] % 2
            where = grads.at[pl.ds(first + b * C, C)]
            copy = pltpu.make_async_copy(stage.at[kept], where, stage_sem.at[kept])
            if staged[0] >= 2:
                copy.wait()
            stage[kept] = read(b).astype(BF)
            copy.start()
            staged[0] += 1

    def run_chunk(c, last):
        base = c * chunk
        here = jnp.minimum(count - base, chunk)
        pairs = (here + 1) // 2
        lax.fori_loop(0, pairs, forward(base), 0)
        for layer in reversed(range(LAYERS)):
            lax.fori_loop(0, pairs, back_inputs(layer), 0)
            lax.fori_loop(0, pairs, back_weights(layer), 0)
            if chunks == 1:
                put_rows(lambda b: acc[0, b * C : (b + 1) * C, :], layer * 9 * C, 9)
                if layer > 0:
                    acc[...] = jnp.zeros_like(acc)
        lax.fori_loop(0, here, scatter(base), 0)

    if chunks == 1:
        run_chunk(0, True)
    else:

        def each(c, _):
            run_chunk(c, False)
            return 0

        lax.fori_loop(0, (count + chunk - 1) // chunk, each, 0)
        for layer in range(LAYERS):
            put_rows(lambda b: acc[layer, b * C : (b + 1) * C, :], layer * 9 * C, 9)

    sides = []
    at = 0
    for k, part in enumerate((g2, g3, g4, g5)):
        sides.append(pltpu.make_async_copy(table_grad.at[pl.ds(at, part.shape[0])], part, out_sem.at[k]))
        sides[-1].start()
        at += part.shape[0]
    put_rows(lambda b: acc_dec[b], LAYERS * 9 * C, 4)
    for layer in range(LAYERS):
        rows = slice(classes_all + 24 + 8 * layer, classes_all + 32 + 8 * layer)
        misc[classes_all + layer : classes_all + layer + 1, :] = jnp.sum(misc[rows, :], axis=0, keepdims=True)
    rows = slice(classes_all + 16, classes_all + 24)
    misc[classes_all + 4 : classes_all + 5, :] = jnp.sum(misc[rows, :], axis=0, keepdims=True)
    put_rows(lambda b: misc[...], LAYERS * 9 * C + 4 * C, 1)
    for kept in range(2):
        pltpu.make_async_copy(stage.at[kept], grads.at[pl.ds(0, C)], stage_sem.at[kept]).wait()
    for side in sides:
        side.wait()


def head(slots, classes_all, boxes, flags, info, p2, p3, p4, p5, *weights):
    chunk = min(CHUNK, slots)
    kept = LAYERS if slots > chunk else 1
    cells = p2.shape[0] + p3.shape[0] + p4.shape[0] + p5.shape[0]
    any_spec = pl.BlockSpec(memory_space=pl.ANY)
    vmem = pl.BlockSpec(memory_space=pltpu.VMEM)
    smem = pl.BlockSpec(memory_space=pltpu.SMEM)
    grad_rows = LAYERS * 9 * C + 4 * C + C
    return pl.pallas_call(
        functools.partial(head_kernel, slots, classes_all),
        out_shape=(
            jax.ShapeDtypeStruct((slots + 1, 8, TOK), F32),
            *(jax.ShapeDtypeStruct(p.shape, F32) for p in (p2, p3, p4, p5)),
            jax.ShapeDtypeStruct((grad_rows, C), BF),
        ),
        in_specs=[smem, smem, vmem] + [any_spec] * 4 + [vmem] * 6,
        out_specs=[vmem] + [any_spec] * 5,
        scratch_shapes=[
            pltpu.SMEM((slots + 2,), jnp.int32),
            pltpu.VMEM((cells + WIN, C), BF),
            pltpu.VMEM((cells + WIN, C), F32),
            pltpu.VMEM((2, XROWS, 3 * C), BF),
            pltpu.VMEM((LAYERS, chunk, C, C), BF),
            pltpu.VMEM((LAYERS, chunk, TOK, C), BF),
            pltpu.VMEM((chunk, TOK, C), F32),
            pltpu.VMEM((chunk, DROWS, 3 * C), BF),
            pltpu.VMEM((chunk, TOK, C), BF),
            pltpu.VMEM((2, TOK, 4 * C), BF),
            pltpu.VMEM((2, TOK, 4 * C), BF),
            pltpu.VMEM((2, C, 4 * C), BF),
            pltpu.VMEM((2, C, C), BF),
            pltpu.VMEM((kept, 9 * C, C), F32),
            pltpu.VMEM((4, C, C), F32),
            pltpu.VMEM((C, C), F32),
            pltpu.VMEM((LAYERS, TOK, C), F32),
            pltpu.VMEM((TOK, C), F32),
            pltpu.VMEM((2, C, C), BF),
            pltpu.SemaphoreType.DMA((4,)),
            pltpu.SemaphoreType.DMA((4,)),
            pltpu.SemaphoreType.DMA((2,)),
        ],
        compiler_params=pltpu.CompilerParams(vmem_limit_bytes=62 * 2**20),
        name="head",
    )(boxes, flags, info, p2, p3, p4, p5, *weights)


def body(
    images,
    p2,
    p3,
    p4,
    p5,
    roi_boxes,
    recv_index,
    classes,
    targets,
    conv_weights,
    conv_biases,
    deconv_weight,
    deconv_bias,
    predictor_weight,
    predictor_bias,
):
    slots = roi_boxes.shape[-1]
    pair = slots // images
    picked = recv_index[0, 0]
    rois = picked.shape[0]
    classes_all = predictor_weight.shape[1]
    bits = targets[0, 0].reshape(rois, POOL, 2, POOL, 2).transpose(0, 2, 4, 1, 3).reshape(rois, 4, POOL, POOL)
    bits = jnp.pad(bits, ((0, 0), (0, 0), (0, 0), (0, WIDE - POOL))).reshape(rois, 4, TOK)
    bits = jnp.pad(bits, ((0, 0), (0, 4), (0, C - TOK)))
    lane = jnp.arange(C)[None, None, :]
    row = jnp.arange(8)[None, :, None]
    label = jnp.where(lane == 0, classes[0, 0][:, None, None], jnp.where(lane == 1, 1, 0))
    rows = jnp.where(row == 4, label, bits).astype(F32)
    chosen = (jnp.arange(slots)[:, None] == picked[None, :]).astype(F32)
    sent = jnp.dot(chosen, rows.reshape(rois, 8 * C)).reshape(images, pair * 8, C)
    info = exchange(images, sent).reshape(slots, 8, C)
    flags = info[:, 4, 0:2].astype(jnp.int32)
    probs, g2, g3, g4, g5, grads = head(
        slots,
        classes_all,
        roi_boxes[0, 0],
        flags,
        info,
        p2[0, 0],
        p3[0, 0],
        p4[0, 0],
        p5[0, 0],
        conv_weights,
        conv_biases,
        deconv_weight,
        deconv_bias[None, :],
        predictor_weight,
        predictor_bias[None, :],
    )
    masks = probs[:slots, 0:4].reshape(slots, 2, 2, POOL, WIDE)[..., :POOL].transpose(0, 3, 1, 4, 2)
    grads = lax.psum(grads, ("img", "grp")).astype(F32)
    conv_rows = LAYERS * 9 * C
    conv_grad = grads[:conv_rows].reshape(conv_weights.shape)
    dec_grad = grads[conv_rows : conv_rows + 4 * C].reshape(4, C, C).transpose(1, 0, 2).reshape(C, 4 * C)
    misc = grads[conv_rows + 4 * C :]
    return (
        masks.reshape(1, 1, slots, MASK * MASK),
        g2.reshape(p2.shape),
        g3.reshape(p3.shape),
        g4.reshape(p4.shape),
        g5.reshape(p5.shape),
        conv_grad,
        misc[classes_all : classes_all + LAYERS],
        dec_grad,
        misc[classes_all + LAYERS],
        misc[:classes_all].T,
        misc[classes_all + 8, :classes_all],
    )


def solution(mesh):
    split = P("img", "grp", None, None)
    in_specs = (split,) * 5 + (P("img", "grp", None),) * 2 + (split,) + (P(),) * 6
    out_specs = (split,) * 5 + (P(),) * 6
    return jax.shard_map(
        functools.partial(body, mesh.shape["img"]),
        mesh=mesh,
        in_specs=in_specs,
        out_specs=out_specs,
        check_vma=False,
    )
```

```python
import functools

import jax
import jax.numpy as jnp
from jax import lax
from jax.experimental import pallas as pl
from jax.experimental.pallas import tpu as pltpu
from jax.sharding import PartitionSpec as P

MESH = pl.DeviceIdType.MESH
POOL = 14
LAYERS = 4
S2 = 64
MASK = 28
C = 256
WIDE = 16
TOK = POOL * WIDE
XROWS = 272
DROWS = 288
WIN = 128
CHUNK = 16
SUM_CHUNKS = 7
SUM_GAP = 2
GA = 0.7978845608028654
GB = GA * 0.044715
BF = jnp.bfloat16
F32 = jnp.float32


def dot(a, b):
    return jnp.dot(a, b, preferred_element_type=F32)


def dot_nt(a, b):
    return lax.dot_general(a, b, (((1,), (1,)), ((), ())), preferred_element_type=F32)


def dot_tn(a, b):
    return lax.dot_general(a, b, (((0,), (0,)), ((), ())), preferred_element_type=F32)


def gelu_both(x):
    square = x * x
    gate = 0.5 + 0.5 * jnp.tanh(x * (GA + GB * square))
    value = x * gate
    slope = gate + (value - value * gate) * (2 * GA + 6 * GB * square)
    return value, slope


def exchange_kernel(n, src, dst, send_sem, recv_sem, own_sem):
    me = lax.axis_index("img")
    grp = lax.axis_index("grp")
    barrier = pltpu.get_barrier_semaphore()
    for k in range(1, n):
        pl.semaphore_signal(barrier, inc=1, device_id=(lax.rem(me + k, n), grp), device_id_type=MESH)
    own = pltpu.make_async_copy(src.at[me], dst.at[me], own_sem)
    own.start()
    pl.semaphore_wait(barrier, n - 1)
    copies = []
    for k in range(1, n):
        peer = lax.rem(me + k, n)
        copy = pltpu.make_async_remote_copy(
            src_ref=src.at[peer],
            dst_ref=dst.at[me],
            send_sem=send_sem.at[k - 1],
            recv_sem=recv_sem.at[k - 1],
            device_id=(peer, grp),
            device_id_type=MESH,
        )
        copy.start()
        copies.append(copy)
    for copy in copies:
        copy.wait()
    own.wait()


def exchange(n, blocks):
    return pl.pallas_call(
        functools.partial(exchange_kernel, n),
        out_shape=jax.ShapeDtypeStruct(blocks.shape, blocks.dtype),
        in_specs=[pl.BlockSpec(memory_space=pl.ANY)],
        out_specs=pl.BlockSpec(memory_space=pl.ANY),
        scratch_shapes=[
            pltpu.SemaphoreType.DMA((n - 1,)),
            pltpu.SemaphoreType.DMA((n - 1,)),
            pltpu.SemaphoreType.DMA,
        ],
        compiler_params=pltpu.CompilerParams(collective_id=0, has_side_effects=True),
        name="exchange",
    )(blocks)


def sum_kernel(chunks, src, out, mine, from_core, from_one, from_two, from_z, res, own_sem, send_sem, recv_sem, out_sem):
    img, grp = lax.axis_index("img"), lax.axis_index("grp")
    x, core = grp // 2, grp % 2
    z, y = img // 2, img % 2
    rows = src.shape[0] // chunks
    half, quarter, eighth = rows // 2, rows // 4, rows // 8
    shard = eighth // 4
    other_core = (img, x * 2 + 1 - core)
    other_x = (img, (1 - x) * 2 + core)
    other_y = (z * 2 + 1 - y, grp)
    others_z = [(lax.rem(z + k, 4) * 2 + y, grp) for k in range(1, 4)]
    lanes = src.shape[1] // 2
    kept_lanes = pl.ds(pl.multiple_of(core * lanes, lanes), lanes)
    sent_lanes = pl.ds(pl.multiple_of((1 - core) * lanes, lanes), lanes)

    barrier = pltpu.get_barrier_semaphore()
    peers = [other_core, other_x, other_y] + others_z
    for peer in peers:
        pl.semaphore_signal(barrier, inc=1, device_id=peer, device_id_type=MESH)
    owns = []
    for k in range(chunks):
        at = pl.ds(k * rows, rows)
        owns.append(pltpu.make_async_copy(src.at[at, kept_lanes], mine.at[at], own_sem.at[k]))
        owns[-1].start()
    pl.semaphore_wait(barrier, len(peers))

    def remote(k, lane, source, target, peer):
        copy = pltpu.make_async_remote_copy(
            src_ref=source,
            dst_ref=target,
            send_sem=send_sem.at[k, lane],
            recv_sem=recv_sem.at[k, lane],
            device_id=peer,
            device_id_type=MESH,
        )
        copy.start()
        return copy

    first_bit, second_bit = (x, y), (y, x)
    first_peer, second_peer = (other_x, other_y), (other_y, other_x)

    def place(k, s, depth, one=None, two=None, three=None):
        at = k * rows + s * half
        if depth >= 1:
            at = at + one * quarter
        if depth >= 2:
            at = at + two * eighth
        if depth >= 3:
            at = at + three * shard
        size = (half, quarter, eighth, shard)[depth]
        return pl.ds(pl.multiple_of(at, 16), size)

    flying = {}

    def stage_core(k):
        at = pl.ds(k * rows, rows)
        flying[0, k] = [remote(k, 0, src.at[at, sent_lanes], from_core.at[at], other_core)]

    def arrived(stage, k):
        for copy in flying.pop((stage, k)):
            copy.wait()

    def stage_one(k):
        arrived(0, k)
        owns[k].wait()
        at = pl.ds(k * rows, rows)
        mine[at, :] = (mine[at, :].astype(F32) + from_core[at, :].astype(F32)).astype(BF)
        flying[1, k] = [
            remote(
                k,
                1 + s,
                mine.at[place(k, s, 1, 1 - first_bit[s])],
                from_one.at[pl.ds((2 * k + s) * quarter, quarter)],
                first_peer[s],
            )
            for s in range(2)
        ]

    def stage_two(k):
        arrived(1, k)
        copies = []
        for s in range(2):
            at = place(k, s, 1, first_bit[s])
            got = from_one[pl.ds((2 * k + s) * quarter, quarter), :]
            mine[at, :] = (mine[at, :].astype(F32) + got.astype(F32)).astype(BF)
            copies.append(
                remote(
                    k,
                    3 + s,
                    mine.at[place(k, s, 2, first_bit[s], 1 - second_bit[s])],
                    from_two.at[pl.ds((2 * k + s) * eighth, eighth)],
                    second_peer[s],
                )
            )
        flying[2, k] = copies

    def stage_three(k):
        arrived(2, k)
        copies = []
        for s in range(2):
            at = place(k, s, 2, first_bit[s], second_bit[s])
            got = from_two[pl.ds((2 * k + s) * eighth, eighth), :]
            mine[at, :] = (mine[at, :].astype(F32) + got.astype(F32)).astype(BF)
            for d in range(3):
                to = lax.rem(z + 1 + d, 4)
                copies.append(
                    remote(
                        k,
                        5 + 3 * s + d,
                        mine.at[place(k, s, 3, first_bit[s], second_bit[s], to)],
                        from_z.at[pl.ds((6 * k + 3 * s + d) * shard, shard)],
                        others_z[d],
                    )
                )
        flying[3, k] = copies

    def stage_four(k):
        arrived(3, k)
        copies = []
        for s in range(2):
            at = place(k, s, 3, first_bit[s], second_bit[s], z)
            total = mine[at, :].astype(F32)
            for d in range(3):
                total += from_z[pl.ds((6 * k + 3 * s + d) * shard, shard), :].astype(F32)
            res[at, kept_lanes] = total.astype(BF)
            for d in range(3):
                block = res.at[at, kept_lanes]
                copies.append(remote(k, 11 + 3 * s + d, block, block, others_z[d]))
        flying[4, k] = copies

    def stage_five(k):
        arrived(4, k)
        copies = []
        for s in range(2):
            block = res.at[place(k, s, 2, first_bit[s], second_bit[s]), kept_lanes]
            copies.append(remote(k, 17 + s, block, block, second_peer[s]))
        flying[5, k] = copies

    def stage_six(k):
        arrived(5, k)
        copies = []
        for s in range(2):
            block = res.at[place(k, s, 1, first_bit[s]), kept_lanes]
            copies.append(remote(k, 19 + s, block, block, first_peer[s]))
        flying[6, k] = copies

    def stage_seven(k):
        arrived(6, k)
        block = res.at[pl.ds(k * rows, rows), kept_lanes]
        flying[7, k] = [remote(k, 21, block, block, other_core)]

    outs = []

    def stage_out(k):
        arrived(7, k)
        at = pl.ds(k * rows, rows)
        outs.append(pltpu.make_async_copy(res.at[at], out.at[at], out_sem.at[k]))
        outs[-1].start()

    for k in range(chunks):
        stage_core(k)
    stages = [stage_one, stage_two, stage_three, stage_four, stage_five, stage_six, stage_seven, stage_out]
    for step in range(chunks + SUM_GAP * (len(stages) - 1)):
        for s in reversed(range(len(stages))):
            if 0 <= step - SUM_GAP * s < chunks:
                stages[s](step - SUM_GAP * s)
    for copy in outs:
        copy.wait()


def sum_all(grads):
    rows, lanes = grads.shape
    chunks = SUM_CHUNKS
    any_spec = pl.BlockSpec(memory_space=pl.ANY)
    return pl.pallas_call(
        functools.partial(sum_kernel, chunks),
        out_shape=jax.ShapeDtypeStruct(grads.shape, grads.dtype),
        in_specs=[any_spec],
        out_specs=any_spec,
        scratch_shapes=[
            pltpu.VMEM((rows, lanes // 2), BF),
            pltpu.VMEM((rows, lanes // 2), BF),
            pltpu.VMEM((rows // 2, lanes // 2), BF),
            pltpu.VMEM((rows // 4, lanes // 2), BF),
            pltpu.VMEM((rows * 6 // 32, lanes // 2), BF),
            pltpu.VMEM((rows, lanes), BF),
            pltpu.SemaphoreType.DMA((chunks,)),
            pltpu.SemaphoreType.DMA((chunks, 22)),
            pltpu.SemaphoreType.DMA((chunks, 22)),
            pltpu.SemaphoreType.DMA((chunks,)),
        ],
        compiler_params=pltpu.CompilerParams(collective_id=1, has_side_effects=True, vmem_limit_bytes=48 * 2**20),
        name="sum_all",
    )(grads)


class Sampler:
    def __init__(self, boxes, slot):
        level = boxes[0, slot]
        self.level = level
        self.y0, self.x0 = boxes[1, slot], boxes[2, slot]
        self.sy, self.sx = boxes[3, slot], boxes[4, slot]
        self.shift = 6 - level
        self.side = jnp.left_shift(1, self.shift)
        self.offset = jnp.where(level == 0, 0, jnp.where(level == 1, 4096, jnp.where(level == 2, 5120, 5376)))
        self.cell = lax.broadcasted_iota(jnp.int32, (WIDE, WIN), 1)
        self.column = (self.cell & (self.side - 1)).astype(F32)
        self.band = lax.shift_right_logical(self.cell, self.shift)

    def across(self, moved):
        j = lax.broadcasted_iota(jnp.int32, (WIDE, WIN), 0) + moved
        at = jnp.where((j >= 0) & (j < POOL), self.x0 + j * self.sx, -64).astype(F32) * 0.25
        return jnp.maximum(1.0 - jnp.abs(at - self.column), 0.0)

    def down(self, i):
        qy = self.y0 + i * self.sy
        base = self.offset + jnp.left_shift(lax.shift_right_logical(qy, 2), self.shift)
        start = pl.multiple_of(jnp.left_shift(lax.shift_right_logical(base, 4), 4), 16)
        lead = lax.shift_right_logical(base - start, self.shift)
        fraction = (qy & 3).astype(F32) * 0.25
        row = self.band - lead
        return start, jnp.where(row == 0, 1.0 - fraction, jnp.where(row == 1, fraction, 0.0))


def head_kernel(
    slots,
    classes_all,
    boxes,
    flags,
    info,
    p2,
    p3,
    p4,
    p5,
    conv_w,
    conv_b,
    dec_w,
    dec_b,
    pred_w,
    pred_b,
    probs,
    g2,
    g3,
    g4,
    g5,
    grads,
    order,
    table,
    table_grad,
    xw,
    xt,
    slope,
    dx,
    dpw,
    dx0,
    up,
    up_slope,
    dpd,
    x4t,
    acc,
    acc_dec,
    misc,
    bias2,
    bias_d,
    stage,
    in_sem,
    out_sem,
    stage_sem,
):
    chunk = min(CHUNK, slots)
    chunks = slots // chunk
    cells = p2.shape[0] + p3.shape[0] + p4.shape[0] + p5.shape[0]
    parts = []
    at = 0
    for k, part in enumerate((p2, p3, p4, p5)):
        parts.append(pltpu.make_async_copy(part, table.at[pl.ds(at, part.shape[0])], in_sem.at[k]))
        parts[-1].start()
        at += part.shape[0]

    def collect(slot, count):
        order[count] = slot
        return count + flags[slot, 1]

    count = lax.fori_loop(0, slots, collect, 0)
    order[count] = 0

    table[cells:, :] = jnp.zeros((table.shape[0] - cells, C), BF)
    table_grad[...] = jnp.zeros_like(table_grad)
    probs[...] = jnp.zeros_like(probs)
    xw[...] = jnp.zeros_like(xw)
    dpw[...] = jnp.zeros_like(dpw)
    dpd[...] = jnp.zeros_like(dpd)
    acc[...] = jnp.zeros_like(acc)
    acc_dec[...] = jnp.zeros_like(acc_dec)
    misc[...] = jnp.zeros_like(misc)
    col = lax.broadcasted_iota(jnp.int32, (TOK, C), 0) & (WIDE - 1)
    off_block = jnp.where(col < POOL, 0.0, -1e4)
    for layer in range(LAYERS):
        bias2[layer] = off_block + conv_b[layer : layer + 1, :].astype(F32)
    bias_d[...] = off_block + dec_b[...].astype(F32)
    lane_ok = (lax.broadcasted_iota(jnp.int32, (8, TOK), 1) & (WIDE - 1)) < POOL
    row_ok = lax.broadcasted_iota(jnp.int32, (8, TOK), 0) < 4
    live = (lane_ok & row_ok).astype(F32)
    for part in parts:
        part.wait()

    def spread(ref, k, value, first, last):
        ref[k, 16 : 16 + TOK, C : 2 * C] = value.astype(BF)
        ref[k, 16 : 16 + TOK, first * C : (first + 1) * C] = pltpu.roll(value, 1, 0).astype(BF)
        ref[k, 16 : 16 + TOK, last * C : (last + 1) * C] = pltpu.roll(value, TOK - 1, 0).astype(BF)

    def forward(base):
        def pair(p, _):
            for k in range(2):
                n = 2 * p + k
                slot = order[base + n]
                sampler = Sampler(boxes, slot)
                across = jnp.concatenate([sampler.across(-1), sampler.across(0), sampler.across(1)], axis=0)
                for i in range(POOL):
                    start, down = sampler.down(i)
                    weights = across * jnp.concatenate([down] * 3, axis=0)
                    sampled = dot(weights.astype(BF), table[pl.ds(start, WIN), :]).astype(BF)
                    for b in range(3):
                        xw[k, 16 * (i + 1) : 16 * (i + 2), b * C : (b + 1) * C] = sampled[b * WIDE : (b + 1) * WIDE]
            for layer in range(LAYERS):
                for k in range(2):
                    n = 2 * p + k
                    xt[layer, n] = xw[k, 16:XROWS, C : 2 * C].T
                    wide = jnp.concatenate([xw[k, 16 * ky : 16 * ky + TOK] for ky in range(3)], axis=1)
                    pre = dot(wide, conv_w[layer]) + bias2[layer]
                    value, slope_now = gelu_both(pre)
                    slope[layer, n] = slope_now.astype(BF)
                    spread(xw, k, value, 0, 2)
            for k in range(2):
                n = 2 * p + k
                index = base + n
                valid = (index < count).astype(F32)
                slot = jnp.where(index < count, order[index], slots)
                class_id = flags[order[index], 0]
                x4 = xw[k, 16 : 16 + TOK, C : 2 * C]
                x4t[k] = xw[k, 16:XROWS, C : 2 * C].T
                for ab in range(4):
                    pre = dot(x4, dec_w[:, ab * C : (ab + 1) * C]) + bias_d[...]
                    value, slope_now = gelu_both(pre)
                    up[k, :, ab * C : (ab + 1) * C] = value.astype(BF)
                    up_slope[k, :, ab * C : (ab + 1) * C] = slope_now.astype(BF)
                picks = (lax.broadcasted_iota(jnp.int32, (16, classes_all), 1) == class_id).astype(F32)
                bias = jnp.sum(picks[0:1] * pred_b[...].astype(F32), axis=1, keepdims=True)
                weight = dot_nt(picks.astype(BF), pred_w[...])
                row = lax.broadcasted_iota(jnp.int32, (16, C), 0)
                blocks = jnp.concatenate([jnp.where(row == ab, weight, 0.0) for ab in range(4)], axis=1).astype(BF)
                logit = dot_nt(blocks, up[k])[0:8] + bias
                prob = 1.0 / (1.0 + jnp.exp(-logit))
                probs[slot] = prob
                target = info[order[index], :, 0:TOK]
                d_logit = ((prob - target) * (valid / (MASK * MASK)) * live).astype(BF)
                d_logit_f = d_logit.astype(F32)
                d16 = jnp.concatenate([d_logit_f, jnp.zeros((8, TOK), F32)], axis=0).astype(BF)
                outer = dot(d16, up[k])
                gathered = jnp.zeros((16, C), F32)
                for ab in range(4):
                    gathered += jnp.where(row == ab, outer[:, ab * C : (ab + 1) * C], 0.0)
                misc[pl.ds(class_id, 1), :] += jnp.sum(gathered, axis=0, keepdims=True)
                total = jnp.sum(jnp.sum(d_logit_f, axis=1, keepdims=True), axis=0, keepdims=True)
                lane = lax.broadcasted_iota(jnp.int32, (1, C), 1)
                misc[classes_all + 8 : classes_all + 9, :] += jnp.where(lane == class_id, total, 0.0)
                grad = jnp.zeros((TOK, C), F32)
                for ab in range(4):
                    cols = slice(ab * C, (ab + 1) * C)
                    d_up = dot_tn(d16, blocks[:, cols])
                    d_pre = d_up * up_slope[k, :, cols].astype(F32)
                    misc[classes_all + 16 : classes_all + 24, :] += jnp.sum(d_pre.reshape(TOK // 8, 8, C), axis=0)
                    d_pre = d_pre.astype(BF)
                    dpd[k, 0:TOK, cols] = d_pre
                    grad += dot_nt(d_pre, dec_w[:, cols])
                dx[n] = grad
            lhs = jnp.concatenate([x4t[0], x4t[1]], axis=1)
            for ab in range(4):
                cols = slice(ab * C, (ab + 1) * C)
                rhs = jnp.concatenate([dpd[0, :, cols], dpd[1, :, cols]], axis=0)
                acc_dec[ab] += dot(lhs, rhs)
            return 0

        return pair

    def back_inputs(layer):
        def pair(p, _):
            for k in range(2):
                n = 2 * p + k
                d_pre = dx[n] * slope[layer, n].astype(F32)
                rows = slice(classes_all + 24 + 8 * layer, classes_all + 32 + 8 * layer)
                misc[rows, :] += jnp.sum(d_pre.reshape(TOK // 8, 8, C), axis=0)
                spread(dpw, n, d_pre, 2, 0)
                grad = jnp.zeros((TOK, C), F32)
                for ky in range(3):
                    for kx in range(3):
                        tap = 3 * ky + kx
                        part = dpw[n, 32 - 16 * ky : 32 - 16 * ky + TOK, kx * C : (kx + 1) * C]
                        grad += dot_nt(part, conv_w[layer, tap * C : (tap + 1) * C, :])
                if layer > 0:
                    dx[n] = grad
                else:
                    dx0[n] = grad.astype(BF)
            return 0

        return pair

    def back_weights(layer):
        kept = layer if chunks > 1 else 0

        def pair(p, _):
            lhs = jnp.concatenate([xt[layer, 2 * p], xt[layer, 2 * p + 1]], axis=1)
            for ky in range(3):
                rows = slice(32 - 16 * ky, 288 - 16 * ky)
                for kx in range(3):
                    cols = slice(kx * C, (kx + 1) * C)
                    tap = 3 * ky + kx
                    rhs = jnp.concatenate([dpw[2 * p, rows, cols], dpw[2 * p + 1, rows, cols]], axis=0)
                    acc[kept, tap * C : (tap + 1) * C, :] += dot(lhs, rhs)
            return 0

        return pair

    def scatter(base):
        def one(n, _):
            slot = order[base + n]
            sampler = Sampler(boxes, slot)
            across = sampler.across(0)

            def rows_of(size):
                def run():
                    for i in range(POOL):
                        start, down = sampler.down(i)
                        weights = (across * down).astype(BF)[:, 0:size]
                        back = dot_tn(weights, dx0[n, i * WIDE : (i + 1) * WIDE, :])
                        table_grad[pl.ds(start, size), :] += back

                return run

            pl.when(sampler.level == 0)(rows_of(128))
            pl.when(sampler.level != 0)(rows_of(128))
            return 0

        return one

    staged = [0]

    def wait_stage():
        pltpu.make_async_copy(stage.at[0], grads.at[pl.ds(0, C)], stage_sem.at[0]).wait()

    def put_rows(read, first, blocks):
        for b in range(blocks):
            kept = staged[0] % 2
            where = grads.at[pl.ds(first + b * C, C)]
            copy = pltpu.make_async_copy(stage.at[kept], where, stage_sem.at[kept])
            if staged[0] >= 2:
                copy.wait()
            stage[kept] = read(b).astype(BF)
            copy.start()
            staged[0] += 1

    def run_chunk(c, last):
        base = c * chunk
        here = jnp.minimum(count - base, chunk)
        pairs = (here + 1) // 2
        lax.fori_loop(0, pairs, forward(base), 0)
        for layer in reversed(range(LAYERS)):
            lax.fori_loop(0, pairs, back_inputs(layer), 0)
            lax.fori_loop(0, pairs, back_weights(layer), 0)
            if chunks == 1:
                put_rows(lambda b: acc[0, b * C : (b + 1) * C, :], layer * 9 * C, 9)
                if layer > 0:
                    acc[...] = jnp.zeros_like(acc)
        lax.fori_loop(0, here, scatter(base), 0)

    if chunks == 1:
        run_chunk(0, True)
    else:

        def each(c, _):
            run_chunk(c, False)
            return 0

        lax.fori_loop(0, (count + chunk - 1) // chunk, each, 0)
        for layer in range(LAYERS):
            put_rows(lambda b: acc[layer, b * C : (b + 1) * C, :], layer * 9 * C, 9)

    sides = []
    at = 0
    for k, part in enumerate((g2, g3, g4, g5)):
        sides.append(pltpu.make_async_copy(table_grad.at[pl.ds(at, part.shape[0])], part, out_sem.at[k]))
        sides[-1].start()
        at += part.shape[0]
    put_rows(lambda b: acc_dec[b], LAYERS * 9 * C, 4)
    for layer in range(LAYERS):
        rows = slice(classes_all + 24 + 8 * layer, classes_all + 32 + 8 * layer)
        misc[classes_all + layer : classes_all + layer + 1, :] = jnp.sum(misc[rows, :], axis=0, keepdims=True)
    rows = slice(classes_all + 16, classes_all + 24)
    misc[classes_all + 4 : classes_all + 5, :] = jnp.sum(misc[rows, :], axis=0, keepdims=True)
    put_rows(lambda b: misc[b * C : (b + 1) * C, :], LAYERS * 9 * C + 4 * C, 2)
    for kept in range(2):
        pltpu.make_async_copy(stage.at[kept], grads.at[pl.ds(0, C)], stage_sem.at[kept]).wait()
    for side in sides:
        side.wait()


def head(slots, classes_all, boxes, flags, info, p2, p3, p4, p5, *weights):
    chunk = min(CHUNK, slots)
    kept = LAYERS if slots > chunk else 1
    cells = p2.shape[0] + p3.shape[0] + p4.shape[0] + p5.shape[0]
    any_spec = pl.BlockSpec(memory_space=pl.ANY)
    vmem = pl.BlockSpec(memory_space=pltpu.VMEM)
    smem = pl.BlockSpec(memory_space=pltpu.SMEM)
    grad_rows = LAYERS * 9 * C + 4 * C + 2 * C
    return pl.pallas_call(
        functools.partial(head_kernel, slots, classes_all),
        out_shape=(
            jax.ShapeDtypeStruct((slots + 1, 8, TOK), F32),
            *(jax.ShapeDtypeStruct(p.shape, F32) for p in (p2, p3, p4, p5)),
            jax.ShapeDtypeStruct((grad_rows, C), BF),
        ),
        in_specs=[smem, smem, vmem] + [any_spec] * 4 + [vmem] * 6,
        out_specs=[vmem] + [any_spec] * 5,
        scratch_shapes=[
            pltpu.SMEM((slots + 2,), jnp.int32),
            pltpu.VMEM((cells + WIN, C), BF),
            pltpu.VMEM((cells + WIN, C), F32),
            pltpu.VMEM((2, XROWS, 3 * C), BF),
            pltpu.VMEM((LAYERS, chunk, C, C), BF),
            pltpu.VMEM((LAYERS, chunk, TOK, C), BF),
            pltpu.VMEM((chunk, TOK, C), F32),
            pltpu.VMEM((chunk, DROWS, 3 * C), BF),
            pltpu.VMEM((chunk, TOK, C), BF),
            pltpu.VMEM((2, TOK, 4 * C), BF),
            pltpu.VMEM((2, TOK, 4 * C), BF),
            pltpu.VMEM((2, C, 4 * C), BF),
            pltpu.VMEM((2, C, C), BF),
            pltpu.VMEM((kept, 9 * C, C), F32),
            pltpu.VMEM((4, C, C), F32),
            pltpu.VMEM((2 * C, C), F32),
            pltpu.VMEM((LAYERS, TOK, C), F32),
            pltpu.VMEM((TOK, C), F32),
            pltpu.VMEM((2, C, C), BF),
            pltpu.SemaphoreType.DMA((4,)),
            pltpu.SemaphoreType.DMA((4,)),
            pltpu.SemaphoreType.DMA((2,)),
        ],
        compiler_params=pltpu.CompilerParams(vmem_limit_bytes=62 * 2**20),
        name="head",
    )(boxes, flags, info, p2, p3, p4, p5, *weights)


def body(
    images,
    groups,
    p2,
    p3,
    p4,
    p5,
    roi_boxes,
    recv_index,
    classes,
    targets,
    conv_weights,
    conv_biases,
    deconv_weight,
    deconv_bias,
    predictor_weight,
    predictor_bias,
):
    slots = roi_boxes.shape[-1]
    pair = slots // images
    picked = recv_index[0, 0]
    rois = picked.shape[0]
    classes_all = predictor_weight.shape[1]
    bits = targets[0, 0].reshape(rois, POOL, 2, POOL, 2).transpose(0, 2, 4, 1, 3).reshape(rois, 4, POOL, POOL)
    bits = jnp.pad(bits, ((0, 0), (0, 0), (0, 0), (0, WIDE - POOL))).reshape(rois, 4, TOK)
    bits = jnp.pad(bits, ((0, 0), (0, 4), (0, C - TOK)))
    lane = jnp.arange(C)[None, None, :]
    row = jnp.arange(8)[None, :, None]
    label = jnp.where(lane == 0, classes[0, 0][:, None, None], jnp.where(lane == 1, 1, 0))
    rows = jnp.where(row == 4, label, bits).astype(F32)
    chosen = (jnp.arange(slots)[:, None] == picked[None, :]).astype(F32)
    sent = jnp.dot(chosen, rows.reshape(rois, 8 * C)).reshape(images, pair * 8, C)
    info = exchange(images, sent).reshape(slots, 8, C)
    flags = info[:, 4, 0:2].astype(jnp.int32)
    probs, g2, g3, g4, g5, grads = head(
        slots,
        classes_all,
        roi_boxes[0, 0],
        flags,
        info,
        p2[0, 0],
        p3[0, 0],
        p4[0, 0],
        p5[0, 0],
        conv_weights,
        conv_biases,
        deconv_weight,
        deconv_bias[None, :],
        predictor_weight,
        predictor_bias[None, :],
    )
    masks = probs[:slots, 0:4].reshape(slots, 2, 2, POOL, WIDE)[..., :POOL].transpose(0, 3, 1, 4, 2)
    if images == 8 and groups == 4:
        grads = sum_all(grads)
    else:
        grads = lax.psum(grads, ("img", "grp"))
    grads = grads.astype(F32)
    conv_rows = LAYERS * 9 * C
    conv_grad = grads[:conv_rows].reshape(conv_weights.shape)
    dec_grad = grads[conv_rows : conv_rows + 4 * C].reshape(4, C, C).transpose(1, 0, 2).reshape(C, 4 * C)
    misc = grads[conv_rows + 4 * C :]
    return (
        masks.reshape(1, 1, slots, MASK * MASK),
        g2.reshape(p2.shape),
        g3.reshape(p3.shape),
        g4.reshape(p4.shape),
        g5.reshape(p5.shape),
        conv_grad,
        misc[classes_all : classes_all + LAYERS],
        dec_grad,
        misc[classes_all + LAYERS],
        misc[:classes_all].T,
        misc[classes_all + 8, :classes_all],
    )


def solution(mesh):
    split = P("img", "grp", None, None)
    in_specs = (split,) * 5 + (P("img", "grp", None),) * 2 + (split,) + (P(),) * 6
    out_specs = (split,) * 5 + (P(),) * 6
    return jax.shard_map(
        functools.partial(body, mesh.shape["img"], mesh.shape["grp"]),
        mesh=mesh,
        in_specs=in_specs,
        out_specs=out_specs,
        check_vma=False,
    )
```

```python
import functools

import jax
import jax.numpy as jnp
from jax import lax
from jax.experimental import pallas as pl
from jax.experimental.pallas import tpu as pltpu
from jax.sharding import PartitionSpec as P

MESH = pl.DeviceIdType.MESH
POOL = 14
LAYERS = 4
MASK = 28
PIXELS = MASK * MASK
LINE = 896
C = 256
WIDE = 16
TOK = POOL * WIDE
XROWS = 272
DROWS = 288
WIN = 128
CHUNK = 16
GROUP = 4
UNIT = 512
MISC = UNIT
DEC = 4 * C
SUM_ROWS = MISC + LAYERS * 9 * C + DEC
SUM_PARTS = tuple((units, "xy") for units in (2, 2, 2, 3, 2, 2, 3, 2, 1, 2))
SUM_GAP = 2
TAIL_GAP = 1
GA = 0.7978845608028654
GB = GA * 0.044715
BF = jnp.bfloat16
F32 = jnp.float32


def dot(a, b):
    return jnp.dot(a, b, preferred_element_type=F32)


def dot_nt(a, b):
    return lax.dot_general(a, b, (((1,), (1,)), ((), ())), preferred_element_type=F32)


def dot_tn(a, b):
    return lax.dot_general(a, b, (((0,), (0,)), ((), ())), preferred_element_type=F32)


def gelu_both(x):
    square = x * x
    gate = 0.5 + 0.5 * jnp.tanh(x * (GA + GB * square))
    value = x * gate
    slope = gate + (value - value * gate) * (2 * GA + 6 * GB * square)
    return value, slope


def exchange_kernel(
    n, pair, targets, picked, classes, conv_w, lines, tags, conv_wt, leaving, send_sem, recv_sem, own_sem
):
    me = lax.axis_index("img")
    grp = lax.axis_index("grp")
    barrier = pltpu.get_barrier_semaphore()
    for k in range(1, n):
        pl.semaphore_signal(barrier, inc=1, device_id=(lax.rem(me + k, n), grp), device_id_type=MESH)
    slots, rois = n * pair, targets.shape[0]
    chosen = (lax.broadcasted_iota(jnp.int32, (slots, rois), 0) == picked[...]).astype(F32)
    rows = dot(chosen.astype(BF), targets[...].astype(F32).astype(BF))
    label = jnp.sum(chosen * classes[...].astype(F32), axis=1, keepdims=True)
    flag = jnp.sum(chosen, axis=1, keepdims=True)
    lane = lax.broadcasted_iota(jnp.int32, (slots, 128), 1)
    mark = jnp.where(lane == PIXELS % 128, label, jnp.where(lane == PIXELS % 128 + 1, flag, 0.0))
    whole = PIXELS // 128 * 128
    last = jnp.concatenate([rows[:, whole:], jnp.zeros((slots, LINE - PIXELS), F32)], axis=1) + mark
    leaving[...] = jnp.zeros_like(leaving)
    for i in range(n):
        leaving[i, 0:pair, 0:whole] = rows[i * pair : (i + 1) * pair, 0:whole]
        leaving[i, 0:pair, whole:LINE] = last[i * pair : (i + 1) * pair]
    own = pltpu.make_async_copy(leaving.at[me], lines.at[me], own_sem)
    own.start()
    pl.semaphore_wait(barrier, n - 1)
    copies = []
    for k in range(1, n):
        peer = lax.rem(me + k, n)
        copy = pltpu.make_async_remote_copy(
            src_ref=leaving.at[peer],
            dst_ref=lines.at[me],
            send_sem=send_sem.at[k - 1],
            recv_sem=recv_sem.at[k - 1],
            device_id=(peer, grp),
            device_id_type=MESH,
        )
        copy.start()
        copies.append(copy)

    def turn(layer):
        def one(tap, _):
            at = pl.ds(pl.multiple_of(tap * C, C), C)
            conv_wt[layer, at, :] = conv_w[layer, at, :].T
            return 0

        lax.fori_loop(0, 9, one, 0)

    for layer in range(LAYERS):
        turn(layer)
    for copy in copies:
        copy.wait()
    own.wait()
    for i in range(n):
        tags[i * 8 : (i + 1) * 8, :] = lines[i, :, whole:LINE].astype(jnp.int32)


def exchange(n, pair, targets, picked, classes, conv_w):
    vmem = pl.BlockSpec(memory_space=pltpu.VMEM)
    return pl.pallas_call(
        functools.partial(exchange_kernel, n, pair),
        out_shape=(
            jax.ShapeDtypeStruct((n, 8, LINE), F32),
            jax.ShapeDtypeStruct((n * 8, 128), jnp.int32),
            jax.ShapeDtypeStruct(conv_w.shape, BF),
        ),
        in_specs=[vmem] * 4,
        out_specs=[vmem] * 3,
        scratch_shapes=[
            pltpu.VMEM((n, 8, LINE), F32),
            pltpu.SemaphoreType.DMA((n - 1,)),
            pltpu.SemaphoreType.DMA((n - 1,)),
            pltpu.SemaphoreType.DMA,
        ],
        compiler_params=pltpu.CompilerParams(collective_id=0, has_side_effects=True, vmem_limit_bytes=32 * 2**20),
        name="exchange",
    )(targets, picked, classes, conv_w)


def sum_kernel(
    classes_all,
    xt,
    slope,
    conv_wt,
    small,
    out,
    d_bottom,
    xt_v,
    slope_v,
    wt_v,
    small_v,
    sums,
    leaving,
    mine,
    from_core,
    from_one,
    from_two,
    from_z,
    res,
    in_sem,
    send_sem,
    recv_sem,
    out_sem,
    bottom_sem,
    *held,
):
    img, grp = lax.axis_index("img"), lax.axis_index("grp")
    x, core = grp // 2, grp % 2
    z, y = img // 2, img % 2
    sizes = [UNIT * units for units, kind in SUM_PARTS]
    kinds = [kind for units, kind in SUM_PARTS]
    starts = [SUM_ROWS - sum(sizes[: k + 1]) for k in range(len(sizes))]
    chunks = len(sizes)
    spans = [slice(start, start + size) for start, size in zip(starts, sizes)]
    other_core = (img, x * 2 + 1 - core)
    other_x = (img, (1 - x) * 2 + core)
    other_y = (z * 2 + 1 - y, grp)
    others_z = [(lax.rem(z + k, 4) * 2 + y, grp) for k in range(1, 4)]
    lanes = C // 2
    kept_lanes = pl.ds(pl.multiple_of(core * lanes, lanes), lanes)

    barrier = pltpu.get_barrier_semaphore()
    peers = [other_core, other_x, other_y] + others_z
    for peer in peers:
        pl.semaphore_signal(barrier, inc=1, device_id=peer, device_id_type=MESH)
    load_small = pltpu.make_async_copy(small, small_v, in_sem.at[3 * LAYERS])
    load_slope, load_wt, load_xt = {}, {}, {}
    for layer in range(LAYERS):
        load_slope[layer] = pltpu.make_async_copy(slope.at[layer], slope_v.at[layer], in_sem.at[3 * layer])
        load_wt[layer] = pltpu.make_async_copy(conv_wt.at[layer], wt_v.at[layer], in_sem.at[3 * layer + 1])
        load_xt[layer] = pltpu.make_async_copy(xt.at[layer], xt_v.at[layer], in_sem.at[3 * layer + 2])

    def load_layer(layer):
        load_slope[layer].start()
        load_wt[layer].start()
        load_xt[layer].start()

    load_small.start()
    load_layer(LAYERS - 1)
    frames, dx = held[:GROUP], held[GROUP:]
    blocks = xt.shape[1]
    each = blocks // GROUP
    for frame in frames:
        frame[:, 0:16, :] = jnp.zeros((each, 16, 3 * C), BF)
        frame[:, 16 + TOK : DROWS, :] = jnp.zeros((each, DROWS - 16 - TOK, 3 * C), BF)
    sums[...] = jnp.zeros_like(sums)
    pl.semaphore_wait(barrier, len(peers))

    def remote(k, lane, source, target, peer):
        copy = pltpu.make_async_remote_copy(
            src_ref=source,
            dst_ref=target,
            send_sem=send_sem.at[k, lane],
            recv_sem=recv_sem.at[k, lane],
            device_id=peer,
            device_id_type=MESH,
        )
        copy.start()
        return copy

    bits, across = {"x": (x, y), "y": (y, x)}, {"x": (other_x, other_y), "y": (other_y, other_x)}

    def place(k, s, depth):
        size = sizes[k] // len(kinds[k])
        at = starts[k] + s * size
        for level in range(abs(depth)):
            size = size // 2
            bit = bits[kinds[k][s]][level]
            at = at + (1 - bit if level + 1 == -depth else bit) * size
        return at, size

    def rows_at(k, s, depth):
        at, size = place(k, s, depth)
        return pl.ds(pl.multiple_of(at, 16), size)

    def shard_at(k, s, owner):
        at, size = place(k, s, 2)
        return pl.ds(pl.multiple_of(at + owner * (size // 4), 16), size // 4)

    def landing(k, s, cut, d=0):
        size = sizes[k] // (len(kinds[k]) * cut)
        per = 3 if cut == 16 else 1
        first = starts[k] // cut * per + (per * s + d) * size
        return slice(first, first + size)

    flying = {}

    def arrived(stage, k):
        for copy in flying.pop((stage, k)):
            copy.wait()

    def put(at, value):
        low, high = value[:, :lanes], value[:, lanes:]
        first = core == 0
        mine[at, :] = jnp.where(first, low, high).astype(BF)
        leaving[at, :] = jnp.where(first, high, low).astype(BF)

    def spread(layer, k, q):
        value = slope_v[layer, k * each + q].astype(F32)
        if layer < LAYERS - 1:
            value = dx[k][q] * value
        frames[k][q, 16 : 16 + TOK, 0:C] = pltpu.roll(value, TOK - 1, 0).astype(BF)
        frames[k][q, 16 : 16 + TOK, C : 2 * C] = value.astype(BF)
        frames[k][q, 16 : 16 + TOK, 2 * C : 3 * C] = pltpu.roll(value, 1, 0).astype(BF)
        return jnp.sum(value.reshape(TOK // 8, 8, C), axis=0)

    def back(layer, k, q):
        wide = jnp.concatenate([frames[k][q, 32 - 16 * ky : 32 - 16 * ky + TOK] for ky in range(3)], axis=1)
        return dot(wide, wt_v[layer])

    def inputs(layer, part):
        def four(q, _):
            total = jnp.zeros((8, C), F32)
            for k in range(GROUP):
                if layer > 0:
                    total += spread(layer, k, q)
                    dx[k][q] = back(layer, k, q)
                else:
                    slope_v[0, k * each + q] = back(0, k, q).astype(BF)
            if layer > 0:
                sums[layer] += total
            return 0

        if part == 0 and layer > 0:
            load_slope[layer].wait()
        if part == 0:
            load_wt[layer].wait()
        if part == 0 and layer > 0:
            load_layer(layer - 1)
        lax.fori_loop(part * each // 2, (part + 1) * each // 2, four, 0)

    def lowest():
        load_slope[0].wait()

        def four(q, _):
            total = jnp.zeros((8, C), F32)
            for k in range(GROUP):
                total += spread(0, k, q)
            sums[0] += total
            return 0

        lax.fori_loop(0, each, four, 0)
        put(slice(0, MISC), small_v[0:MISC, :].astype(F32))
        row = lax.broadcasted_iota(jnp.int32, (16, C), 0)
        biases = jnp.zeros((16, C), F32)
        for layer in range(LAYERS):
            biases += jnp.where(row == layer, jnp.sum(sums[layer], axis=0, keepdims=True), 0.0)
        first = bias_rows(classes_all)
        put(slice(first, first + 16), biases)

    def weights(layer, taps):
        for tap in taps:
            if tap == 8:
                load_xt[layer].wait()
            ky, kx = tap // 3, tap % 3
            lhs = jnp.concatenate([xt_v[layer, n] for n in range(blocks)], axis=1)
            rhs = jnp.concatenate(
                [
                    frames[n // each][n % each, 32 - 16 * ky : 288 - 16 * ky, kx * C : (kx + 1) * C]
                    for n in range(blocks)
                ],
                axis=0,
            )
            at = MISC + (9 * layer + tap) * C
            put(slice(at, at + C), dot(lhs, rhs))

    def stage_core(k):
        flying[0, k] = [remote(k, 0, leaving.at[spans[k]], from_core.at[spans[k]], other_core)]

    def parts(k):
        return range(len(kinds[k]))

    def stage_one(k):
        arrived(0, k)
        at = spans[k]
        mine[at, :] = (mine[at, :].astype(F32) + from_core[at, :].astype(F32)).astype(BF)
        flying[1, k] = [
            remote(k, 1 + s, mine.at[rows_at(k, s, -1)], from_one.at[landing(k, s, 2)], across[kinds[k][s]][0])
            for s in parts(k)
        ]

    def stage_two(k):
        arrived(1, k)
        copies = []
        for s in parts(k):
            at = rows_at(k, s, 1)
            mine[at, :] = (mine[at, :].astype(F32) + from_one[landing(k, s, 2), :].astype(F32)).astype(BF)
            leave = mine.at[rows_at(k, s, -2)]
            copies.append(remote(k, 3 + s, leave, from_two.at[landing(k, s, 4)], across[kinds[k][s]][1]))
        flying[2, k] = copies

    def stage_three(k):
        arrived(2, k)
        copies = []
        for s in parts(k):
            at = rows_at(k, s, 2)
            mine[at, :] = (mine[at, :].astype(F32) + from_two[landing(k, s, 4), :].astype(F32)).astype(BF)
            for d in range(3):
                leave = mine.at[shard_at(k, s, lax.rem(z + 1 + d, 4))]
                copies.append(remote(k, 5 + 3 * s + d, leave, from_z.at[landing(k, s, 16, d)], others_z[d]))
        flying[3, k] = copies

    def stage_four(k):
        arrived(3, k)
        copies = []
        for s in parts(k):
            at = shard_at(k, s, z)
            total = mine[at, :].astype(F32)
            for d in range(3):
                total += from_z[landing(k, s, 16, d), :].astype(F32)
            res[at, kept_lanes] = total.astype(BF)
            for d in range(3):
                block = res.at[at, kept_lanes]
                copies.append(remote(k, 11 + 3 * s + d, block, block, others_z[d]))
        flying[4, k] = copies

    def stage_five(k):
        arrived(4, k)
        blocks = [res.at[rows_at(k, s, 2), kept_lanes] for s in parts(k)]
        flying[5, k] = [remote(k, 17 + s, blocks[s], blocks[s], across[kinds[k][s]][1]) for s in parts(k)]

    def stage_six(k):
        arrived(5, k)
        blocks = [res.at[rows_at(k, s, 1), kept_lanes] for s in parts(k)]
        flying[6, k] = [remote(k, 19 + s, blocks[s], blocks[s], across[kinds[k][s]][0]) for s in parts(k)]

    def stage_seven(k):
        arrived(6, k)
        block = res.at[spans[k], kept_lanes]
        flying[7, k] = [remote(k, 21, block, block, other_core)]

    outs = []

    def stage_out(k):
        arrived(7, k)
        outs.append(pltpu.make_async_copy(res.at[spans[k]], out.at[spans[k]], out_sem.at[k]))
        outs[-1].start()

    stages = [stage_one, stage_two, stage_three, stage_four, stage_five, stage_six, stage_seven, stage_out]
    work = []
    for layer in reversed(range(LAYERS)):
        top = MISC + 9 * layer * C
        if layer > 0:
            for part in range(2):
                work.append((functools.partial(inputs, layer, part), None))
        else:
            work.append((lowest, None))
        for taps in ((8, 7), (6, 5), (4, 3), (2, 1, 0)):
            work.append((functools.partial(weights, layer, taps), top + taps[-1] * C))
    work[-1] = (work[-1][0], 0)
    for part in range(2):
        work.append((functools.partial(inputs, 0, part), None))

    load_small.wait()
    put(slice(SUM_ROWS - DEC, SUM_ROWS), small_v[MISC:, :].astype(F32))
    ready = SUM_ROWS - DEC
    due = {}
    step, first = 0, 0
    while len(outs) < chunks or step < len(work):
        gap = SUM_GAP if step < len(work) else TAIL_GAP
        for k in range(chunks):
            if k in due and due[k][1] <= step and due[k][0] < len(stages):
                stages[due[k][0]](k)
                due[k] = (due[k][0] + 1, step + gap)
        while first < chunks and starts[first] >= ready:
            due[first] = (0, step + gap)
            stage_core(first)
            first += 1
        if step < len(work):
            run, now = work[step]
            run()
            ready = ready if now is None else now
            if step == len(work) - 1:
                bottom = pltpu.make_async_copy(slope_v.at[0], d_bottom, bottom_sem)
                bottom.start()
        step += 1
    bottom.wait()
    for copy in outs:
        copy.wait()


def bias_rows(classes_all):
    return (classes_all + 7) // 8 * 8 + 16


def sum_all(classes_all, xt, slope, conv_w, conv_wt, small):
    blocks = xt.shape[1]
    chunks = len(SUM_PARTS)
    any_spec = pl.BlockSpec(memory_space=pl.ANY)
    return pl.pallas_call(
        functools.partial(sum_kernel, classes_all),
        out_shape=(jax.ShapeDtypeStruct((SUM_ROWS, C), BF), jax.ShapeDtypeStruct(slope.shape[1:], BF)),
        in_specs=[any_spec] * 4,
        out_specs=[any_spec] * 2,
        scratch_shapes=[
            pltpu.VMEM(xt.shape, BF),
            pltpu.VMEM(slope.shape, BF),
            pltpu.VMEM(conv_wt.shape, BF),
            pltpu.VMEM(small.shape, BF),
            pltpu.VMEM((LAYERS, 8, C), F32),
            pltpu.VMEM((SUM_ROWS, C // 2), BF),
            pltpu.VMEM((SUM_ROWS, C // 2), BF),
            pltpu.VMEM((SUM_ROWS, C // 2), BF),
            pltpu.VMEM((SUM_ROWS // 2, C // 2), BF),
            pltpu.VMEM((SUM_ROWS // 4, C // 2), BF),
            pltpu.VMEM((SUM_ROWS // 16 * 3, C // 2), BF),
            pltpu.VMEM((SUM_ROWS, C), BF),
            pltpu.SemaphoreType.DMA((3 * LAYERS + 1,)),
            pltpu.SemaphoreType.DMA((chunks, 22)),
            pltpu.SemaphoreType.DMA((chunks, 22)),
            pltpu.SemaphoreType.DMA((chunks,)),
            pltpu.SemaphoreType.DMA,
        ]
        + [pltpu.VMEM((blocks // GROUP, DROWS, 3 * C), BF)] * GROUP
        + [pltpu.VMEM((blocks // GROUP, TOK, C), F32)] * GROUP,
        compiler_params=pltpu.CompilerParams(collective_id=1, has_side_effects=True, vmem_limit_bytes=60 * 2**20),
        name="sum_all",
    )(xt, slope, conv_wt, small)


def sum_plain(classes_all, xt, slope, conv_w, conv_wt, small):
    slots = slope.shape[1]
    chunk = min(CHUNK, slots)

    def some(c, carry):
        weights, biases, bottom = carry
        grad = 1.0
        parts, sums = [], []
        for layer in reversed(range(LAYERS)):
            d_pre = grad * lax.dynamic_slice_in_dim(slope[layer], c * chunk, chunk).astype(F32)
            sums.insert(0, jnp.sum(d_pre, axis=(0, 1)))
            padded = jnp.pad(d_pre.astype(BF), ((0, 0), (17, 49), (0, 0)))
            held = lax.dynamic_slice_in_dim(xt[layer], c * chunk, chunk)
            grad = 0.0
            taps = []
            for tap in range(9):
                at = 17 - 16 * (tap // 3 - 1) - (tap % 3 - 1)
                moved = padded[:, at : at + C]
                taps.append(jnp.einsum("nct,ntd->cd", held, moved, preferred_element_type=F32))
                kernel = conv_w[layer, tap * C : (tap + 1) * C]
                grad += jnp.einsum("ntd,cd->ntc", moved[:, :TOK], kernel, preferred_element_type=F32)
            parts = taps + parts
        bottom = lax.dynamic_update_slice_in_dim(bottom, grad.astype(BF), c * chunk, 0)
        return weights + jnp.concatenate(parts), biases + jnp.stack(sums), bottom

    carry = (jnp.zeros((LAYERS * 9 * C, C), F32), jnp.zeros((LAYERS, C), F32), jnp.zeros(slope.shape[1:], BF))
    weights, biases, bottom = lax.fori_loop(0, slots // chunk, some, carry)
    first = bias_rows(classes_all)
    misc = small[:MISC].astype(F32).at[first : first + LAYERS].set(biases)
    total = jnp.concatenate([misc, weights, small[MISC:].astype(F32)])
    return lax.psum(total.astype(BF), ("img", "grp")), bottom


class Sampler:
    def __init__(self, boxes, slot):
        level = boxes[0, 0, slot]
        self.level = level
        self.y0, self.x0 = boxes[1, 0, slot], boxes[2, 0, slot]
        self.sy, self.sx = boxes[3, 0, slot], boxes[4, 0, slot]
        self.shift = 6 - level
        self.side = jnp.left_shift(1, self.shift)
        self.offset = jnp.where(level == 0, 0, jnp.where(level == 1, 4096, jnp.where(level == 2, 5120, 5376)))
        self.cell = lax.broadcasted_iota(jnp.int32, (WIDE, WIN), 1)
        self.column = (self.cell & (self.side - 1)).astype(F32)
        self.band = lax.shift_right_logical(self.cell, self.shift)

    def across(self, moved):
        j = lax.broadcasted_iota(jnp.int32, (WIDE, WIN), 0) + moved
        at = jnp.where((j >= 0) & (j < POOL), self.x0 + j * self.sx, -64).astype(F32) * 0.25
        return jnp.maximum(1.0 - jnp.abs(at - self.column), 0.0)

    def down(self, i):
        qy = self.y0 + i * self.sy
        base = self.offset + jnp.left_shift(lax.shift_right_logical(qy, 2), self.shift)
        start = pl.multiple_of(jnp.left_shift(lax.shift_right_logical(base, 4), 4), 16)
        lead = lax.shift_right_logical(base - start, self.shift)
        fraction = (qy & 3).astype(F32) * 0.25
        row = self.band - lead
        return start, jnp.where(row == 0, 1.0 - fraction, jnp.where(row == 1, fraction, 0.0))


def head_kernel(
    slots,
    classes_all,
    images,
    boxes,
    tags,
    lines,
    p2,
    p3,
    p4,
    p5,
    conv_w_h,
    conv_b,
    dec_w,
    dec_b,
    pred_wt,
    pred_b,
    masks,
    xt_out,
    slope_out,
    small,
    order,
    table,
    xt,
    slope,
    up,
    up_slope,
    dpd,
    x4t,
    acc_dec,
    misc,
    dec_sum,
    bias2,
    bias_d,
    small_v,
    conv_w,
    moves,
    wanted,
    probs,
    in_sem,
    w_sem,
    out_sem,
    small_sem,
    *xw,
):
    chunk = min(CHUNK, slots)
    chunks = slots // chunk
    pair = slots // images
    cells = p2.shape[0] + p3.shape[0] + p4.shape[0] + p5.shape[0]
    parts = []
    at = 0
    for k, part in enumerate((p2, p3, p4, p5)):
        parts.append(pltpu.make_async_copy(part, table.at[pl.ds(at, part.shape[0])], in_sem.at[k]))
        at += part.shape[0]
    for layer in range(LAYERS):
        parts.append(pltpu.make_async_copy(conv_w_h.at[layer], conv_w.at[layer], w_sem.at[layer]))
    for part in parts:
        part.start()

    count = processed(slots, pair, tags, order)
    table[cells:, :] = jnp.zeros((table.shape[0] - cells, C), BF)
    probs[...] = jnp.zeros_like(probs)
    for frame in xw:
        frame[...] = jnp.zeros_like(frame)
    dpd[...] = jnp.zeros_like(dpd)
    acc_dec[...] = jnp.zeros_like(acc_dec)
    misc[...] = jnp.zeros_like(misc)
    dec_sum[...] = jnp.zeros_like(dec_sum)
    col = lax.broadcasted_iota(jnp.int32, (TOK, C), 0) & (WIDE - 1)
    off_block = jnp.where(col < POOL, 0.0, -1e4)
    for layer in range(LAYERS):
        bias2[layer] = off_block + conv_b[layer : layer + 1, :].astype(F32)
    bias_d[...] = off_block + jnp.concatenate([dec_b[0:1, :], dec_b[1:2, :]], axis=1).astype(F32)
    lane_ok = (lax.broadcasted_iota(jnp.int32, (8, TOK), 1) & (WIDE - 1)) < POOL
    row_ok = lax.broadcasted_iota(jnp.int32, (8, TOK), 0) < 4
    live = (lane_ok & row_ok).astype(F32)
    token = lax.broadcasted_iota(jnp.int32, (TOK, LINE), 0)
    pixel = lax.broadcasted_iota(jnp.int32, (TOK, LINE), 1)
    inside = (token & (WIDE - 1)) < POOL
    corner = lax.shift_right_logical(token, 4) * (2 * MASK) + (token & (WIDE - 1)) * 2
    all_lines = lines[...].reshape(images * 8, LINE).astype(BF)
    for ab in range(4):
        moves[ab] = (inside & (pixel == corner + (ab // 2 * MASK + ab % 2))).astype(F32).astype(BF)
        wanted[ab] = dot_nt(all_lines, moves[ab])
    for part in parts:
        part.wait()

    def spread(ref, value, first, last):
        ref[16 : 16 + TOK, C : 2 * C] = value.astype(BF)
        ref[16 : 16 + TOK, first * C : (first + 1) * C] = pltpu.roll(value, 1, 0).astype(BF)
        ref[16 : 16 + TOK, last * C : (last + 1) * C] = pltpu.roll(value, TOK - 1, 0).astype(BF)

    def sends(base, n):
        where = pl.ds(base + n, 1)
        return (
            pltpu.make_async_copy(xt.at[:, pl.ds(n, 1)], xt_out.at[:, where], out_sem.at[n, 0]),
            pltpu.make_async_copy(slope.at[:, pl.ds(n, 1)], slope_out.at[:, where], out_sem.at[n, 1]),
        )

    pred_row = (classes_all + 7) // 8 * 8

    def forward(base, first, group):
        def run(q, _):
            at = [first + group * q + k for k in range(group)]
            for k, n in enumerate(at):
                slot = order[base + n]
                sampler = Sampler(boxes, slot)
                across = jnp.concatenate([sampler.across(-1), sampler.across(0), sampler.across(1)], axis=0)
                for i in range(POOL):
                    start, down = sampler.down(i)
                    weights = across * jnp.concatenate([down] * 3, axis=0)
                    sampled = dot(weights.astype(BF), table[pl.ds(start, WIN), :]).astype(BF)
                    for b in range(3):
                        xw[k][16 * (i + 1) : 16 * (i + 2), b * C : (b + 1) * C] = sampled[b * WIDE : (b + 1) * WIDE]
            for layer in range(LAYERS):
                for k, n in enumerate(at):
                    xt[layer, n] = xw[k][16:XROWS, C : 2 * C].T
                    wide = jnp.concatenate([xw[k][16 * ky : 16 * ky + TOK] for ky in range(3)], axis=1)
                    pre = dot(wide, conv_w[layer]) + bias2[layer]
                    value, slope_now = gelu_both(pre)
                    slope[layer, n] = slope_now.astype(BF)
                    spread(xw[k], value, 0, 2)
            for k, n in enumerate(at):
                index = base + n
                valid = (index < count).astype(F32)
                slot = jnp.where(index < count, order[index], slots)
                line = line_of(order[index], pair)
                class_id = tags[line, PIXELS % 128]
                x4 = xw[k][16 : 16 + TOK, C : 2 * C]
                x4t[k] = xw[k][16:XROWS, C : 2 * C].T
                for ab in range(4):
                    pre = dot(x4, dec_w[:, ab * C : (ab + 1) * C]) + bias_d[...]
                    value, slope_now = gelu_both(pre)
                    up[k, :, ab * C : (ab + 1) * C] = value.astype(BF)
                    up_slope[k, :, ab * C : (ab + 1) * C] = slope_now.astype(BF)
                picks = (lax.broadcasted_iota(jnp.int32, (16, classes_all), 1) == class_id).astype(F32)
                bias = jnp.sum(picks[0:1] * pred_b[...].astype(F32), axis=1, keepdims=True)
                weight = dot(picks.astype(BF), pred_wt[...])
                row = lax.broadcasted_iota(jnp.int32, (16, C), 0)
                blocks = jnp.concatenate([jnp.where(row == ab, weight, 0.0) for ab in range(4)], axis=1).astype(BF)
                logit = dot_nt(blocks, up[k])[0:8] + bias
                prob = 1.0 / (1.0 + jnp.exp(-logit))
                rows = []
                for ab in range(4):
                    probs[ab, pl.ds(slot, 1), :] = prob[ab : ab + 1]
                    rows.append(wanted[ab, pl.ds(line, 1), :])
                target = jnp.concatenate(rows + [jnp.zeros((4, TOK), F32)], axis=0)
                d_logit = ((prob - target) * (valid / (MASK * MASK)) * live).astype(BF)
                d_logit_f = d_logit.astype(F32)
                d16 = jnp.concatenate([d_logit_f, jnp.zeros((8, TOK), F32)], axis=0).astype(BF)
                outer = dot(d16, up[k])
                gathered = jnp.zeros((16, C), F32)
                for ab in range(4):
                    gathered += jnp.where(row == ab, outer[:, ab * C : (ab + 1) * C], 0.0)
                misc[pl.ds(class_id, 1), :] += jnp.sum(gathered, axis=0, keepdims=True)
                total = jnp.sum(jnp.sum(d_logit_f, axis=1, keepdims=True), axis=0, keepdims=True)
                lane = lax.broadcasted_iota(jnp.int32, (1, C), 1)
                misc[pred_row : pred_row + 1, :] += jnp.where(lane == class_id, total, 0.0)
                grad = jnp.zeros((TOK, C), F32)
                for ab in range(4):
                    cols = slice(ab * C, (ab + 1) * C)
                    d_up = dot_tn(d16, blocks[:, cols])
                    d_pre = d_up * up_slope[k, :, cols].astype(F32)
                    dec_sum[...] += jnp.sum(d_pre.reshape(TOK // 8, 8, C), axis=0)
                    d_pre = d_pre.astype(BF)
                    dpd[k, 0:TOK, cols] = d_pre
                    grad += dot_nt(d_pre, dec_w[:, cols])
                last = LAYERS - 1
                slope[last, n] = (grad * slope[last, n].astype(F32)).astype(BF)
            lhs = jnp.concatenate([x4t[k] for k in range(group)], axis=1)
            for ab in range(4):
                cols = slice(ab * C, (ab + 1) * C)
                rhs = jnp.concatenate([dpd[k, :, cols] for k in range(group)], axis=0)
                acc_dec[ab] += dot(lhs, rhs)
            for n in at:
                for copy in sends(base, n):
                    copy.start()
            return 0

        return run

    def clear(base):
        def one(n, _):
            for layer in range(LAYERS):
                xt[layer, n] = jnp.zeros((C, C), BF)
                slope[layer, n] = jnp.zeros((TOK, C), BF)
            for copy in sends(base, n):
                copy.start()
            return 0

        return one

    def wait_for(n, _):
        for copy in sends(0, n):
            copy.wait()
        return 0

    def run_chunk(c, _):
        base = c * chunk
        here = jnp.clip(count - base, 0, chunk)
        wide = here // GROUP
        pairs = (here - wide * GROUP + 1) // 2
        lax.fori_loop(wide * GROUP + 2 * pairs, chunk, clear(base), 0)
        lax.fori_loop(0, wide, forward(base, 0, GROUP), 0)
        lax.fori_loop(0, pairs, forward(base, wide * GROUP, 2), 0)
        lax.fori_loop(0, chunk, wait_for, 0)
        return 0

    if chunks == 1:
        run_chunk(0, 0)
    else:
        lax.fori_loop(0, chunks, run_chunk, 0)

    misc[pred_row + 8 : pred_row + 9, :] = jnp.sum(dec_sum[...], axis=0, keepdims=True)
    small_v[0:MISC, :] = misc[...].astype(BF)
    for ab in range(4):
        small_v[MISC + ab * C : MISC + (ab + 1) * C, :] = acc_dec[ab].astype(BF)
    send_small = pltpu.make_async_copy(small_v, small, small_sem)
    send_small.start()
    image = jnp.zeros((slots, LINE), F32)
    for ab in range(4):
        prob = probs[ab, 0:slots, :]
        high = prob.astype(BF)
        low = (prob - high.astype(F32)).astype(BF)
        image += dot(high, moves[ab]) + dot(low, moves[ab])
    masks[...] = image[:, 0:PIXELS]
    send_small.wait()


def processed(slots, pair, tags, order):
    def collect(slot, count):
        order[count] = slot
        return count + tags[line_of(slot, pair), PIXELS % 128 + 1]

    count = lax.fori_loop(0, slots, collect, 0)
    order[count] = 0
    return count


def line_of(slot, pair):
    return slot // pair * 8 + slot % pair


def head(slots, classes_all, boxes, tags, lines, p2, p3, p4, p5, conv_w, *weights):
    chunk = min(CHUNK, slots)
    images = lines.shape[0]
    cells = p2.shape[0] + p3.shape[0] + p4.shape[0] + p5.shape[0]
    any_spec = pl.BlockSpec(memory_space=pl.ANY)
    vmem = pl.BlockSpec(memory_space=pltpu.VMEM)
    smem = pl.BlockSpec(memory_space=pltpu.SMEM)
    return pl.pallas_call(
        functools.partial(head_kernel, slots, classes_all, images),
        out_shape=(
            jax.ShapeDtypeStruct((slots, PIXELS), F32),
            jax.ShapeDtypeStruct((LAYERS, slots, C, C), BF),
            jax.ShapeDtypeStruct((LAYERS, slots, TOK, C), BF),
            jax.ShapeDtypeStruct((MISC + DEC, C), BF),
        ),
        in_specs=[smem, smem, vmem] + [any_spec] * 5 + [vmem] * 5,
        out_specs=[vmem] + [any_spec] * 3,
        scratch_shapes=[
            pltpu.SMEM((slots + 2,), jnp.int32),
            pltpu.VMEM((cells + WIN, C), BF),
            pltpu.VMEM((LAYERS, chunk, C, C), BF),
            pltpu.VMEM((LAYERS, chunk, TOK, C), BF),
            pltpu.VMEM((GROUP, TOK, 4 * C), BF),
            pltpu.VMEM((GROUP, TOK, 4 * C), BF),
            pltpu.VMEM((GROUP, C, 4 * C), BF),
            pltpu.VMEM((GROUP, C, C), BF),
            pltpu.VMEM((4, C, C), F32),
            pltpu.VMEM((MISC, C), F32),
            pltpu.VMEM((8, C), F32),
            pltpu.VMEM((LAYERS, TOK, C), F32),
            pltpu.VMEM((TOK, C), F32),
            pltpu.VMEM((MISC + DEC, C), BF),
            pltpu.VMEM(conv_w.shape, BF),
            pltpu.VMEM((4, TOK, LINE), BF),
            pltpu.VMEM((4, images * 8, TOK), F32),
            pltpu.VMEM((4, slots + 8, TOK), F32),
            pltpu.SemaphoreType.DMA((4,)),
            pltpu.SemaphoreType.DMA((LAYERS,)),
            pltpu.SemaphoreType.DMA((chunk, 2)),
            pltpu.SemaphoreType.DMA,
        ]
        + [pltpu.VMEM((XROWS, 3 * C), BF)] * GROUP,
        compiler_params=pltpu.CompilerParams(vmem_limit_bytes=60 * 2**20),
        name="head",
    )(boxes, tags, lines, p2, p3, p4, p5, conv_w, *weights)


def finish_kernel(
    slots,
    classes_all,
    images,
    boxes,
    tags,
    dx0,
    summed,
    g2,
    g3,
    g4,
    g5,
    conv_g,
    conv_bg,
    dec_g,
    dec_bg,
    pred_g,
    pred_bg,
    order,
    table_grad,
    sum_v,
    conv_v,
    in_sem,
    conv_sem,
    out_sem,
):
    pieces = LAYERS
    size = 9 * C
    loads = []
    for k in range(pieces):
        at = pl.ds(MISC + k * size, size)
        loads.append(pltpu.make_async_copy(summed.at[at], sum_v.at[at], in_sem.at[k]))
    for k, at in enumerate((pl.ds(0, MISC), pl.ds(SUM_ROWS - DEC, DEC))):
        loads.append(pltpu.make_async_copy(summed.at[at], sum_v.at[at], in_sem.at[pieces + k]))
    for load in loads:
        load.start()
    pair = slots // images
    count = processed(slots, pair, tags, order)
    table_grad[...] = jnp.zeros_like(table_grad)
    stores = []
    for k in range(pieces):
        loads[k].wait()
        conv_v[k] = sum_v[MISC + k * size : MISC + (k + 1) * size, :].astype(F32)
        stores.append(pltpu.make_async_copy(conv_v.at[k], conv_g.at[k], conv_sem.at[k]))
        stores[-1].start()

    def scatter(n, _):
        sampler = Sampler(boxes, order[n])
        across = sampler.across(0)

        def rows_of(cells):
            def run():
                for i in range(POOL):
                    start, down = sampler.down(i)
                    weights = (across * down).astype(BF)[:, 0:cells]
                    table_grad[pl.ds(start, cells), :] += dot_tn(weights, dx0[n, i * WIDE : (i + 1) * WIDE, :])

            return run

        pl.when(sampler.level == 0)(rows_of(128))
        pl.when(sampler.level == 1)(rows_of(64))
        pl.when(sampler.level >= 2)(rows_of(32))
        return 0

    lax.fori_loop(0, count, scatter, 0)
    at = 0
    for k, part in enumerate((g2, g3, g4, g5)):
        stores.append(pltpu.make_async_copy(table_grad.at[pl.ds(at, part.shape[0])], part, out_sem.at[k]))
        stores[-1].start()
        at += part.shape[0]
    for load in loads[pieces:]:
        load.wait()
    for ab in range(4):
        first = SUM_ROWS - DEC + ab * C
        dec_g[:, ab * C : (ab + 1) * C] = sum_v[first : first + C, :].astype(F32)
    misc = sum_v[0:MISC, :].astype(F32)
    pred_row = (classes_all + 7) // 8 * 8
    bias_row = bias_rows(classes_all)
    pred_g[...] = misc[0:classes_all]
    pred_bg[...] = misc[pred_row : pred_row + 1, 0:classes_all]
    dec_bg[...] = misc[pred_row + 8 : pred_row + 9]
    conv_bg[...] = misc[bias_row : bias_row + LAYERS]
    for store in stores:
        store.wait()


def finish(slots, classes_all, images, boxes, tags, dx0, summed, levels):
    cells = sum(levels)
    any_spec = pl.BlockSpec(memory_space=pl.ANY)
    vmem = pl.BlockSpec(memory_space=pltpu.VMEM)
    smem = pl.BlockSpec(memory_space=pltpu.SMEM)
    return pl.pallas_call(
        functools.partial(finish_kernel, slots, classes_all, images),
        out_shape=(
            *(jax.ShapeDtypeStruct((level, C), F32) for level in levels),
            jax.ShapeDtypeStruct((LAYERS, 9 * C, C), F32),
            jax.ShapeDtypeStruct((LAYERS, C), F32),
            jax.ShapeDtypeStruct((C, 4 * C), F32),
            jax.ShapeDtypeStruct((1, C), F32),
            jax.ShapeDtypeStruct((classes_all, C), F32),
            jax.ShapeDtypeStruct((1, classes_all), F32),
        ),
        in_specs=[smem, smem, vmem, any_spec],
        out_specs=[any_spec] * 5 + [vmem] * 5,
        scratch_shapes=[
            pltpu.SMEM((slots + 2,), jnp.int32),
            pltpu.VMEM((cells + WIN, C), F32),
            pltpu.VMEM((SUM_ROWS, C), BF),
            pltpu.VMEM((LAYERS, 9 * C, C), F32),
            pltpu.SemaphoreType.DMA((LAYERS + 2,)),
            pltpu.SemaphoreType.DMA((LAYERS,)),
            pltpu.SemaphoreType.DMA((4,)),
        ],
        compiler_params=pltpu.CompilerParams(vmem_limit_bytes=60 * 2**20),
        name="finish",
    )(boxes, tags, dx0, summed)


def body(
    images,
    groups,
    p2,
    p3,
    p4,
    p5,
    roi_boxes,
    recv_index,
    classes,
    targets,
    conv_weights,
    conv_biases,
    deconv_weight,
    deconv_bias,
    predictor_weight,
    predictor_bias,
):
    slots = roi_boxes.shape[-1]
    classes_all = predictor_weight.shape[1]
    boxes = roi_boxes[0].transpose(1, 0, 2)
    lines, tags, conv_wt = exchange(
        images, slots // images, targets[0, 0], recv_index[0], classes[0], conv_weights
    )
    masks, xt, slope, small = head(
        slots,
        classes_all,
        boxes,
        tags,
        lines,
        p2[0, 0],
        p3[0, 0],
        p4[0, 0],
        p5[0, 0],
        conv_weights,
        conv_biases,
        deconv_weight,
        deconv_bias.reshape(2, C // 2),
        predictor_weight.T,
        predictor_bias[None, :],
    )
    total = sum_all if images == 8 and groups == 4 else sum_plain
    summed, dx0 = total(classes_all, xt, slope, conv_weights, conv_wt, small)
    levels = [p.shape[2] for p in (p2, p3, p4, p5)]
    g2, g3, g4, g5, conv_g, conv_bg, dec_g, dec_bg, pred_g, pred_bg = finish(
        slots, classes_all, images, boxes, tags, dx0, summed, levels
    )
    return (
        masks[None, None],
        g2[None, None],
        g3[None, None],
        g4[None, None],
        g5[None, None],
        conv_g,
        conv_bg,
        dec_g,
        dec_bg[0],
        pred_g.T,
        pred_bg[0],
    )


def solution(mesh):
    split = P("img", "grp", None, None)
    in_specs = (split,) * 5 + (P("img", "grp", None),) * 2 + (split,) + (P(),) * 6
    out_specs = (split,) * 5 + (P(),) * 6
    return jax.shard_map(
        functools.partial(body, mesh.shape["img"], mesh.shape["grp"]),
        mesh=mesh,
        in_specs=in_specs,
        out_specs=out_specs,
        check_vma=False,
    )
```

```python
import functools

import jax
import jax.numpy as jnp
from jax import lax
from jax.experimental import pallas as pl
from jax.experimental.pallas import tpu as pltpu
from jax.sharding import PartitionSpec as P

MESH = pl.DeviceIdType.MESH
POOL = 14
LAYERS = 4
MASK = 28
PIXELS = MASK * MASK
LINE = 896
C = 256
WIDE = 16
TOK = POOL * WIDE
XROWS = 272
DROWS = 288
WIN = 128
CHUNK = 16
GROUP = 4
UNIT = 512
MISC = UNIT
DEC = 4 * C
TOP = LAYERS - 1
HEAD_ROWS = 9 * C + DEC
SUM_ROWS = MISC + LAYERS * 9 * C + DEC
SUM_PARTS = tuple((units, "xy") for units in (2, 2, 2, 3, 2, 2, 3, 2, 1, 2))
SUM_GAP = 3
TAIL_GAP = 2
SUM_ENTER = 3
GA = 0.7978845608028654
GB = GA * 0.044715
BF = jnp.bfloat16
F32 = jnp.float32


def dot(a, b):
    return jnp.dot(a, b, preferred_element_type=F32)


def dot_nt(a, b):
    return lax.dot_general(a, b, (((1,), (1,)), ((), ())), preferred_element_type=F32)


def dot_tn(a, b):
    return lax.dot_general(a, b, (((0,), (0,)), ((), ())), preferred_element_type=F32)


def gelu_both(x):
    square = x * x
    gate = 0.5 + 0.5 * jnp.tanh(x * (GA + GB * square))
    value = x * gate
    slope = gate + (value - value * gate) * (2 * GA + 6 * GB * square)
    return value, slope


def exchange_kernel(
    n,
    pair,
    targets,
    picked,
    classes,
    conv_w,
    lines,
    tags,
    conv_wt,
    targets_v,
    picked_v,
    classes_v,
    lines_v,
    tags_v,
    conv_v,
    turned,
    leaving,
    send_sem,
    recv_sem,
    own_sem,
    in_sem,
    w_sem,
    out_sem,
):
    me = lax.axis_index("img")
    grp = lax.axis_index("grp")
    barrier = pltpu.get_barrier_semaphore()
    for k in range(1, n):
        pl.semaphore_signal(barrier, inc=1, device_id=(lax.rem(me + k, n), grp), device_id_type=MESH)
    loads = []
    for k, (source, target) in enumerate(((targets, targets_v), (picked, picked_v), (classes, classes_v))):
        loads.append(pltpu.make_async_copy(source, target, in_sem.at[k]))
    for layer in range(LAYERS):
        loads.append(pltpu.make_async_copy(conv_w.at[layer], conv_v.at[layer], w_sem.at[layer]))
    for load in loads:
        load.start()
    leaving[...] = jnp.zeros_like(leaving)
    for load in loads[:3]:
        load.wait()
    slots, rois = n * pair, targets.shape[0]
    chosen = (lax.broadcasted_iota(jnp.int32, (slots, rois), 0) == picked_v[...]).astype(F32)
    rows = dot(chosen.astype(BF), targets_v[...].astype(F32).astype(BF))
    label = jnp.sum(chosen * classes_v[...].astype(F32), axis=1, keepdims=True)
    flag = jnp.sum(chosen, axis=1, keepdims=True)
    lane = lax.broadcasted_iota(jnp.int32, (slots, 128), 1)
    mark = jnp.where(lane == PIXELS % 128, label, jnp.where(lane == PIXELS % 128 + 1, flag, 0.0))
    whole = PIXELS // 128 * 128
    last = jnp.concatenate([rows[:, whole:], jnp.zeros((slots, LINE - PIXELS), F32)], axis=1) + mark
    for i in range(n):
        leaving[i, 0:pair, 0:whole] = rows[i * pair : (i + 1) * pair, 0:whole]
        leaving[i, 0:pair, whole:LINE] = last[i * pair : (i + 1) * pair]
    own = pltpu.make_async_copy(leaving.at[me], lines_v.at[me], own_sem)
    own.start()
    pl.semaphore_wait(barrier, n - 1)
    copies = []
    for k in range(1, n):
        peer = lax.rem(me + k, n)
        copy = pltpu.make_async_remote_copy(
            src_ref=leaving.at[peer],
            dst_ref=lines_v.at[me],
            send_sem=send_sem.at[k - 1],
            recv_sem=recv_sem.at[k - 1],
            device_id=(peer, grp),
            device_id_type=MESH,
        )
        copy.start()
        copies.append(copy)

    def turn(layer):
        def one(tap, _):
            at = pl.ds(pl.multiple_of(tap * C, C), C)
            turned[layer, at, :] = conv_v[layer, at, :].T
            return 0

        lax.fori_loop(0, 9, one, 0)

    stores = []
    for layer in range(LAYERS):
        loads[3 + layer].wait()
        turn(layer)
        stores.append(pltpu.make_async_copy(turned.at[layer], conv_wt.at[layer], w_sem.at[layer]))
        stores[-1].start()
    own.wait()
    for copy in copies:
        copy.wait()
    for i in range(n):
        tags_v[i * 8 : (i + 1) * 8, :] = lines_v[i, :, whole:LINE].astype(jnp.int32)
    stores.append(pltpu.make_async_copy(lines_v, lines, out_sem.at[0]))
    stores.append(pltpu.make_async_copy(tags_v, tags, out_sem.at[1]))
    for store in stores[LAYERS:]:
        store.start()
    for store in stores:
        store.wait()


def exchange(n, pair, targets, picked, classes, conv_w):
    any_spec = pl.BlockSpec(memory_space=pl.ANY)
    return pl.pallas_call(
        functools.partial(exchange_kernel, n, pair),
        out_shape=(
            jax.ShapeDtypeStruct((n, 8, LINE), F32),
            jax.ShapeDtypeStruct((n * 8, 128), jnp.int32),
            jax.ShapeDtypeStruct(conv_w.shape, BF),
        ),
        in_specs=[any_spec] * 4,
        out_specs=[any_spec] * 3,
        scratch_shapes=[
            pltpu.VMEM(targets.shape, jnp.int32),
            pltpu.VMEM(picked.shape, jnp.int32),
            pltpu.VMEM(classes.shape, jnp.int32),
            pltpu.VMEM((n, 8, LINE), F32),
            pltpu.VMEM((n * 8, 128), jnp.int32),
            pltpu.VMEM(conv_w.shape, BF),
            pltpu.VMEM(conv_w.shape, BF),
            pltpu.VMEM((n, 8, LINE), F32),
            pltpu.SemaphoreType.DMA((n - 1,)),
            pltpu.SemaphoreType.DMA((n - 1,)),
            pltpu.SemaphoreType.DMA,
            pltpu.SemaphoreType.DMA((3,)),
            pltpu.SemaphoreType.DMA((LAYERS,)),
            pltpu.SemaphoreType.DMA((2,)),
        ],
        compiler_params=pltpu.CompilerParams(collective_id=0, has_side_effects=True, vmem_limit_bytes=60 * 2**20),
        name="exchange",
    )(targets, picked, classes, conv_w)


def sum_kernel(
    classes_all,
    xt,
    slope,
    conv_wt,
    small,
    out,
    d_bottom,
    xt_v,
    slope_v,
    wt_v,
    small_v,
    sums,
    leaving,
    mine,
    from_core,
    from_one,
    from_two,
    from_z,
    res,
    in_sem,
    send_sem,
    recv_sem,
    out_sem,
    bottom_sem,
    *held,
):
    img, grp = lax.axis_index("img"), lax.axis_index("grp")
    x, core = grp // 2, grp % 2
    z, y = img // 2, img % 2
    sizes = [UNIT * units for units, kind in SUM_PARTS]
    kinds = [kind for units, kind in SUM_PARTS]
    starts = [SUM_ROWS - sum(sizes[: k + 1]) for k in range(len(sizes))]
    chunks = len(sizes)
    spans = [slice(start, start + size) for start, size in zip(starts, sizes)]
    other_core = (img, x * 2 + 1 - core)
    other_x = (img, (1 - x) * 2 + core)
    other_y = (z * 2 + 1 - y, grp)
    others_z = [(lax.rem(z + k, 4) * 2 + y, grp) for k in range(1, 4)]
    lanes = C // 2
    kept_lanes = pl.ds(pl.multiple_of(core * lanes, lanes), lanes)

    barrier = pltpu.get_barrier_semaphore()
    peers = [other_core, other_x, other_y] + others_z
    for peer in peers:
        pl.semaphore_signal(barrier, inc=1, device_id=peer, device_id_type=MESH)
    load_small = pltpu.make_async_copy(small, small_v, in_sem.at[3 * TOP])
    load_slope, load_wt, load_xt = {}, {}, {}
    for layer in range(TOP):
        load_slope[layer] = pltpu.make_async_copy(slope.at[layer], slope_v.at[layer], in_sem.at[3 * layer])
        load_wt[layer] = pltpu.make_async_copy(conv_wt.at[layer], wt_v.at[layer], in_sem.at[3 * layer + 1])
        load_xt[layer] = pltpu.make_async_copy(xt.at[layer], xt_v.at[layer], in_sem.at[3 * layer + 2])

    def load_layer(layer):
        load_slope[layer].start()
        load_wt[layer].start()
        load_xt[layer].start()

    load_small.start()
    load_layer(TOP - 1)
    frames, dx = held[:GROUP], held[GROUP:]
    blocks = xt.shape[1]
    each = blocks // GROUP
    for frame in frames:
        frame[:, 0:16, :] = jnp.zeros((each, 16, 3 * C), BF)
        frame[:, 16 + TOK : DROWS, :] = jnp.zeros((each, DROWS - 16 - TOK, 3 * C), BF)
    sums[...] = jnp.zeros_like(sums)
    pl.semaphore_wait(barrier, len(peers))

    def remote(k, lane, source, target, peer):
        copy = pltpu.make_async_remote_copy(
            src_ref=source,
            dst_ref=target,
            send_sem=send_sem.at[k, lane],
            recv_sem=recv_sem.at[k, lane],
            device_id=peer,
            device_id_type=MESH,
        )
        copy.start()
        return copy

    bits, across = {"x": (x, y), "y": (y, x)}, {"x": (other_x, other_y), "y": (other_y, other_x)}

    def place(k, s, depth):
        size = sizes[k] // len(kinds[k])
        at = starts[k] + s * size
        for level in range(abs(depth)):
            size = size // 2
            bit = bits[kinds[k][s]][level]
            at = at + (1 - bit if level + 1 == -depth else bit) * size
        return at, size

    def rows_at(k, s, depth):
        at, size = place(k, s, depth)
        return pl.ds(pl.multiple_of(at, 16), size)

    def shard_at(k, s, owner):
        at, size = place(k, s, 2)
        return pl.ds(pl.multiple_of(at + owner * (size // 4), 16), size // 4)

    def landing(k, s, cut, d=0):
        size = sizes[k] // (len(kinds[k]) * cut)
        per = 3 if cut == 16 else 1
        first = starts[k] // cut * per + (per * s + d) * size
        return slice(first, first + size)

    flying = {}

    def arrived(stage, k):
        for copy in flying.pop((stage, k)):
            copy.wait()

    def put(at, value):
        low, high = value[:, :lanes], value[:, lanes:]
        first = core == 0
        mine[at, :] = jnp.where(first, low, high).astype(BF)
        leaving[at, :] = jnp.where(first, high, low).astype(BF)

    def spread(layer, k, q):
        value = slope_v[layer, k * each + q].astype(F32)
        if layer < TOP - 1:
            value = dx[k][q] * value
        frames[k][q, 16 : 16 + TOK, 0:C] = pltpu.roll(value, TOK - 1, 0).astype(BF)
        frames[k][q, 16 : 16 + TOK, C : 2 * C] = value.astype(BF)
        frames[k][q, 16 : 16 + TOK, 2 * C : 3 * C] = pltpu.roll(value, 1, 0).astype(BF)
        return jnp.sum(value.reshape(TOK // 8, 8, C), axis=0)

    def back(layer, k, q):
        wide = jnp.concatenate([frames[k][q, 32 - 16 * ky : 32 - 16 * ky + TOK] for ky in range(3)], axis=1)
        return dot(wide, wt_v[layer])

    def inputs(layer, part):
        def four(q, _):
            total = jnp.zeros((8, C), F32)
            for k in range(GROUP):
                if layer > 0:
                    total += spread(layer, k, q)
                    dx[k][q] = back(layer, k, q)
                else:
                    slope_v[0, k * each + q] = back(0, k, q).astype(BF)
            if layer > 0:
                sums[layer] += total
            return 0

        if part == 0 and layer > 0:
            load_slope[layer].wait()
        if part == 0:
            load_wt[layer].wait()
        if part == 0 and layer > 0:
            load_layer(layer - 1)
        lax.fori_loop(part * each // 2, (part + 1) * each // 2, four, 0)

    def lowest():
        load_slope[0].wait()

        def four(q, _):
            total = jnp.zeros((8, C), F32)
            for k in range(GROUP):
                total += spread(0, k, q)
            sums[0] += total
            return 0

        lax.fori_loop(0, each, four, 0)
        put(slice(0, MISC), small_v[0:MISC, :].astype(F32))
        row = lax.broadcasted_iota(jnp.int32, (16, C), 0)
        first = bias_rows(classes_all)
        biases = small_v[first : first + 16, :].astype(F32)
        for layer in range(TOP):
            biases += jnp.where(row == layer, jnp.sum(sums[layer], axis=0, keepdims=True), 0.0)
        put(slice(first, first + 16), biases)

    def weights(layer, taps):
        for tap in taps:
            if tap == 8:
                load_xt[layer].wait()
            ky, kx = tap // 3, tap % 3
            lhs = jnp.concatenate([xt_v[layer, n] for n in range(blocks)], axis=1)
            rhs = jnp.concatenate(
                [
                    frames[n // each][n % each, 32 - 16 * ky : 288 - 16 * ky, kx * C : (kx + 1) * C]
                    for n in range(blocks)
                ],
                axis=0,
            )
            at = MISC + (9 * layer + tap) * C
            put(slice(at, at + C), dot(lhs, rhs))

    def stage_core(k):
        flying[0, k] = [remote(k, 0, leaving.at[spans[k]], from_core.at[spans[k]], other_core)]

    def parts(k):
        return range(len(kinds[k]))

    def stage_one(k):
        arrived(0, k)
        at = spans[k]
        mine[at, :] = (mine[at, :].astype(F32) + from_core[at, :].astype(F32)).astype(BF)
        flying[1, k] = [
            remote(k, 1 + s, mine.at[rows_at(k, s, -1)], from_one.at[landing(k, s, 2)], across[kinds[k][s]][0])
            for s in parts(k)
        ]

    def stage_two(k):
        arrived(1, k)
        copies = []
        for s in parts(k):
            at = rows_at(k, s, 1)
            mine[at, :] = (mine[at, :].astype(F32) + from_one[landing(k, s, 2), :].astype(F32)).astype(BF)
            leave = mine.at[rows_at(k, s, -2)]
            copies.append(remote(k, 3 + s, leave, from_two.at[landing(k, s, 4)], across[kinds[k][s]][1]))
        flying[2, k] = copies

    def stage_three(k):
        arrived(2, k)
        copies = []
        for s in parts(k):
            at = rows_at(k, s, 2)
            mine[at, :] = (mine[at, :].astype(F32) + from_two[landing(k, s, 4), :].astype(F32)).astype(BF)
            for d in range(3):
                leave = mine.at[shard_at(k, s, lax.rem(z + 1 + d, 4))]
                copies.append(remote(k, 5 + 3 * s + d, leave, from_z.at[landing(k, s, 16, d)], others_z[d]))
        flying[3, k] = copies

    def stage_four(k):
        arrived(3, k)
        copies = []
        for s in parts(k):
            at = shard_at(k, s, z)
            total = mine[at, :].astype(F32)
            for d in range(3):
                total += from_z[landing(k, s, 16, d), :].astype(F32)
            res[at, kept_lanes] = total.astype(BF)
            for d in range(3):
                block = res.at[at, kept_lanes]
                copies.append(remote(k, 11 + 3 * s + d, block, block, others_z[d]))
        flying[4, k] = copies

    def stage_five(k):
        arrived(4, k)
        blocks = [res.at[rows_at(k, s, 2), kept_lanes] for s in parts(k)]
        flying[5, k] = [remote(k, 17 + s, blocks[s], blocks[s], across[kinds[k][s]][1]) for s in parts(k)]

    def stage_six(k):
        arrived(5, k)
        blocks = [res.at[rows_at(k, s, 1), kept_lanes] for s in parts(k)]
        flying[6, k] = [remote(k, 19 + s, blocks[s], blocks[s], across[kinds[k][s]][0]) for s in parts(k)]

    def stage_seven(k):
        arrived(6, k)
        block = res.at[spans[k], kept_lanes]
        flying[7, k] = [remote(k, 21, block, block, other_core)]

    outs = []

    def stage_out(k):
        arrived(7, k)
        outs.append(pltpu.make_async_copy(res.at[spans[k]], out.at[spans[k]], out_sem.at[k]))
        outs[-1].start()

    stages = [stage_one, stage_two, stage_three, stage_four, stage_five, stage_six, stage_seven, stage_out]
    work = []
    for layer in reversed(range(TOP)):
        top = MISC + 9 * layer * C
        if layer > 0:
            for part in range(2):
                work.append((functools.partial(inputs, layer, part), None))
        else:
            work.append((lowest, None))
        for taps in ((8, 7), (6, 5), (4, 3), (2, 1, 0)):
            work.append((functools.partial(weights, layer, taps), top + taps[-1] * C))
    work[-1] = (work[-1][0], 0)
    for part in range(2):
        work.append((functools.partial(inputs, 0, part), None))

    load_small.wait()
    put(slice(SUM_ROWS - HEAD_ROWS, SUM_ROWS), small_v[MISC:, :].astype(F32))
    ready = SUM_ROWS - HEAD_ROWS
    due = {}
    step, first = 0, 0
    while len(outs) < chunks or step < len(work):
        gap = SUM_GAP if step < len(work) else TAIL_GAP
        for k in range(chunks):
            if k in due and due[k][1] <= step and due[k][0] < len(stages):
                stages[due[k][0]](k)
                due[k] = (due[k][0] + 1, step + gap)
        for _ in range(SUM_ENTER):
            if first == chunks or starts[first] < ready:
                break
            due[first] = (0, step + gap)
            stage_core(first)
            first += 1
        if step < len(work):
            run, now = work[step]
            run()
            ready = ready if now is None else now
            if step == len(work) - 1:
                bottom = pltpu.make_async_copy(slope_v.at[0], d_bottom, bottom_sem)
                bottom.start()
        step += 1
    bottom.wait()
    for copy in outs:
        copy.wait()


def bias_rows(classes_all):
    return (classes_all + 7) // 8 * 8 + 16


def sum_all(classes_all, xt, slope, conv_w, conv_wt, small):
    blocks = xt.shape[1]
    chunks = len(SUM_PARTS)
    any_spec = pl.BlockSpec(memory_space=pl.ANY)
    return pl.pallas_call(
        functools.partial(sum_kernel, classes_all),
        out_shape=(jax.ShapeDtypeStruct((SUM_ROWS, C), BF), jax.ShapeDtypeStruct(slope.shape[1:], BF)),
        in_specs=[any_spec] * 4,
        out_specs=[any_spec] * 2,
        scratch_shapes=[
            pltpu.VMEM(xt.shape, BF),
            pltpu.VMEM(slope.shape, BF),
            pltpu.VMEM((TOP, 9 * C, C), BF),
            pltpu.VMEM(small.shape, BF),
            pltpu.VMEM((TOP, 8, C), F32),
            pltpu.VMEM((SUM_ROWS, C // 2), BF),
            pltpu.VMEM((SUM_ROWS, C // 2), BF),
            pltpu.VMEM((SUM_ROWS, C // 2), BF),
            pltpu.VMEM((SUM_ROWS // 2, C // 2), BF),
            pltpu.VMEM((SUM_ROWS // 4, C // 2), BF),
            pltpu.VMEM((SUM_ROWS // 16 * 3, C // 2), BF),
            pltpu.VMEM((SUM_ROWS, C), BF),
            pltpu.SemaphoreType.DMA((3 * TOP + 1,)),
            pltpu.SemaphoreType.DMA((chunks, 22)),
            pltpu.SemaphoreType.DMA((chunks, 22)),
            pltpu.SemaphoreType.DMA((chunks,)),
            pltpu.SemaphoreType.DMA,
        ]
        + [pltpu.VMEM((blocks // GROUP, DROWS, 3 * C), BF)] * GROUP
        + [pltpu.VMEM((blocks // GROUP, TOK, C), F32)] * GROUP,
        compiler_params=pltpu.CompilerParams(collective_id=1, has_side_effects=True, vmem_limit_bytes=60 * 2**20),
        name="sum_all",
    )(xt, slope, conv_wt, small)


def sum_plain(classes_all, xt, slope, conv_w, conv_wt, small):
    slots = slope.shape[1]
    chunk = min(CHUNK, slots)

    def some(c, carry):
        weights, biases, bottom = carry
        grad = 1.0
        parts, sums = [], []
        for layer in reversed(range(TOP)):
            d_pre = grad * lax.dynamic_slice_in_dim(slope[layer], c * chunk, chunk).astype(F32)
            sums.insert(0, jnp.sum(d_pre, axis=(0, 1)))
            padded = jnp.pad(d_pre.astype(BF), ((0, 0), (17, 49), (0, 0)))
            held = lax.dynamic_slice_in_dim(xt[layer], c * chunk, chunk)
            grad = 0.0
            taps = []
            for tap in range(9):
                at = 17 - 16 * (tap // 3 - 1) - (tap % 3 - 1)
                moved = padded[:, at : at + C]
                taps.append(jnp.einsum("nct,ntd->cd", held, moved, preferred_element_type=F32))
                kernel = conv_w[layer, tap * C : (tap + 1) * C]
                grad += jnp.einsum("ntd,cd->ntc", moved[:, :TOK], kernel, preferred_element_type=F32)
            parts = taps + parts
        bottom = lax.dynamic_update_slice_in_dim(bottom, grad.astype(BF), c * chunk, 0)
        return weights + jnp.concatenate(parts), biases + jnp.stack(sums), bottom

    carry = (jnp.zeros((TOP * 9 * C, C), F32), jnp.zeros((TOP, C), F32), jnp.zeros(slope.shape[1:], BF))
    weights, biases, bottom = lax.fori_loop(0, slots // chunk, some, carry)
    first = bias_rows(classes_all)
    misc = small[:MISC].astype(F32).at[first : first + TOP].set(biases)
    total = jnp.concatenate([misc, weights, small[MISC:].astype(F32)])
    return lax.psum(total.astype(BF), ("img", "grp")), bottom


class Sampler:
    def __init__(self, boxes, slot):
        level = boxes[0, 0, slot]
        self.level = level
        self.y0, self.x0 = boxes[1, 0, slot], boxes[2, 0, slot]
        self.sy, self.sx = boxes[3, 0, slot], boxes[4, 0, slot]
        self.shift = 6 - level
        self.side = jnp.left_shift(1, self.shift)
        self.offset = jnp.where(level == 0, 0, jnp.where(level == 1, 4096, jnp.where(level == 2, 5120, 5376)))
        self.cell = lax.broadcasted_iota(jnp.int32, (WIDE, WIN), 1)
        self.column = (self.cell & (self.side - 1)).astype(F32)
        self.band = lax.shift_right_logical(self.cell, self.shift)

    def across(self, moved):
        j = lax.broadcasted_iota(jnp.int32, (WIDE, WIN), 0) + moved
        at = jnp.where((j >= 0) & (j < POOL), self.x0 + j * self.sx, -64).astype(F32) * 0.25
        return jnp.maximum(1.0 - jnp.abs(at - self.column), 0.0)

    def down(self, i):
        qy = self.y0 + i * self.sy
        base = self.offset + jnp.left_shift(lax.shift_right_logical(qy, 2), self.shift)
        start = pl.multiple_of(jnp.left_shift(lax.shift_right_logical(base, 4), 4), 16)
        lead = lax.shift_right_logical(base - start, self.shift)
        fraction = (qy & 3).astype(F32) * 0.25
        row = self.band - lead
        return start, jnp.where(row == 0, 1.0 - fraction, jnp.where(row == 1, fraction, 0.0))


def head_kernel(
    slots,
    classes_all,
    images,
    boxes,
    tags,
    lines,
    p2,
    p3,
    p4,
    p5,
    conv_w_h,
    conv_wt_h,
    conv_b,
    dec_w,
    dec_b,
    pred_wt,
    pred_b,
    masks,
    xt_out,
    slope_out,
    small,
    order,
    table,
    xt,
    slope,
    up,
    up_slope,
    dpd,
    x4t,
    acc_dec,
    acc,
    misc,
    dec_sum,
    top_sum,
    bias2,
    bias_d,
    small_v,
    conv_w,
    top_wt,
    moves,
    wanted,
    probs,
    in_sem,
    w_sem,
    out_sem,
    small_sem,
    *frames,
):
    chunk = min(CHUNK, slots)
    chunks = slots // chunk
    pair = slots // images
    cells = p2.shape[0] + p3.shape[0] + p4.shape[0] + p5.shape[0]
    parts = []
    at = 0
    for k, part in enumerate((p2, p3, p4, p5)):
        parts.append(pltpu.make_async_copy(part, table.at[pl.ds(at, part.shape[0])], in_sem.at[k]))
        at += part.shape[0]
    for layer in range(LAYERS):
        parts.append(pltpu.make_async_copy(conv_w_h.at[layer], conv_w.at[layer], w_sem.at[layer]))
    parts.append(pltpu.make_async_copy(conv_wt_h.at[TOP], top_wt, w_sem.at[LAYERS]))
    xw, dpw = frames[:GROUP], frames[GROUP:]
    for part in parts:
        part.start()

    count = processed(slots, pair, tags, order)
    table[cells:, :] = jnp.zeros((table.shape[0] - cells, C), BF)
    probs[...] = jnp.zeros_like(probs)
    for frame in frames:
        frame[...] = jnp.zeros_like(frame)
    dpd[...] = jnp.zeros_like(dpd)
    acc_dec[...] = jnp.zeros_like(acc_dec)
    acc[...] = jnp.zeros_like(acc)
    top_sum[...] = jnp.zeros_like(top_sum)
    misc[...] = jnp.zeros_like(misc)
    dec_sum[...] = jnp.zeros_like(dec_sum)
    col = lax.broadcasted_iota(jnp.int32, (TOK, C), 0) & (WIDE - 1)
    off_block = jnp.where(col < POOL, 0.0, -1e4)
    for layer in range(LAYERS):
        bias2[layer] = off_block + conv_b[layer : layer + 1, :].astype(F32)
    bias_d[...] = off_block + jnp.concatenate([dec_b[0:1, :], dec_b[1:2, :]], axis=1).astype(F32)
    lane_ok = (lax.broadcasted_iota(jnp.int32, (8, TOK), 1) & (WIDE - 1)) < POOL
    row_ok = lax.broadcasted_iota(jnp.int32, (8, TOK), 0) < 4
    live = (lane_ok & row_ok).astype(F32)
    token = lax.broadcasted_iota(jnp.int32, (TOK, LINE), 0)
    pixel = lax.broadcasted_iota(jnp.int32, (TOK, LINE), 1)
    inside = (token & (WIDE - 1)) < POOL
    corner = lax.shift_right_logical(token, 4) * (2 * MASK) + (token & (WIDE - 1)) * 2
    all_lines = lines[...].reshape(images * 8, LINE).astype(BF)
    for ab in range(4):
        moves[ab] = (inside & (pixel == corner + (ab // 2 * MASK + ab % 2))).astype(F32).astype(BF)
        wanted[ab] = dot_nt(all_lines, moves[ab])
    for part in parts:
        part.wait()

    def spread(ref, value, first, last):
        ref[16 : 16 + TOK, C : 2 * C] = value.astype(BF)
        ref[16 : 16 + TOK, first * C : (first + 1) * C] = pltpu.roll(value, 1, 0).astype(BF)
        ref[16 : 16 + TOK, last * C : (last + 1) * C] = pltpu.roll(value, TOK - 1, 0).astype(BF)

    def sends(base, n):
        where = pl.ds(base + n, 1)
        return (
            pltpu.make_async_copy(xt.at[0:TOP, pl.ds(n, 1)], xt_out.at[:, where], out_sem.at[n, 0]),
            pltpu.make_async_copy(slope.at[0:TOP, pl.ds(n, 1)], slope_out.at[:, where], out_sem.at[n, 1]),
        )

    pred_row = (classes_all + 7) // 8 * 8

    def forward(base, first, group):
        def run(q, _):
            at = [first + group * q + k for k in range(group)]
            for k, n in enumerate(at):
                slot = order[base + n]
                sampler = Sampler(boxes, slot)
                across = jnp.concatenate([sampler.across(-1), sampler.across(0), sampler.across(1)], axis=0)
                for i in range(POOL):
                    start, down = sampler.down(i)
                    weights = across * jnp.concatenate([down] * 3, axis=0)
                    sampled = dot(weights.astype(BF), table[pl.ds(start, WIN), :]).astype(BF)
                    for b in range(3):
                        xw[k][16 * (i + 1) : 16 * (i + 2), b * C : (b + 1) * C] = sampled[b * WIDE : (b + 1) * WIDE]
            for layer in range(LAYERS):
                for k, n in enumerate(at):
                    xt[layer, n] = xw[k][16:XROWS, C : 2 * C].T
                    wide = jnp.concatenate([xw[k][16 * ky : 16 * ky + TOK] for ky in range(3)], axis=1)
                    pre = dot(wide, conv_w[layer]) + bias2[layer]
                    value, slope_now = gelu_both(pre)
                    slope[layer, n] = slope_now.astype(BF)
                    spread(xw[k], value, 0, 2)
            for k in range(group):
                x4 = xw[k][16 : 16 + TOK, C : 2 * C]
                x4t[k] = xw[k][16:XROWS, C : 2 * C].T
                for ab in range(4):
                    pre = dot(x4, dec_w[:, ab * C : (ab + 1) * C]) + bias_d[...]
                    value, slope_now = gelu_both(pre)
                    up[k, :, ab * C : (ab + 1) * C] = value.astype(BF)
                    up_slope[k, :, ab * C : (ab + 1) * C] = slope_now.astype(BF)
            row = lax.broadcasted_iota(jnp.int32, (16, C), 0)
            lane = lax.broadcasted_iota(jnp.int32, (1, C), 1)
            class_ids = [tags[line_of(order[base + n], pair), PIXELS % 128] for n in at]
            heads, d_logits = [], []
            for k, n in enumerate(at):
                picks = (lax.broadcasted_iota(jnp.int32, (16, classes_all), 1) == class_ids[k]).astype(F32)
                bias = jnp.sum(picks[0:1] * pred_b[...].astype(F32), axis=1, keepdims=True)
                weight = dot(picks.astype(BF), pred_wt[...])
                blocks = jnp.concatenate([jnp.where(row == ab, weight, 0.0) for ab in range(4)], axis=1).astype(BF)
                heads.append((blocks, bias))
            for k, n in enumerate(at):
                blocks, bias = heads[k]
                index = base + n
                valid = (index < count).astype(F32)
                slot = jnp.where(index < count, order[index], slots)
                line = line_of(order[index], pair)
                logit = dot_nt(blocks, up[k])[0:8] + bias
                prob = 1.0 / (1.0 + jnp.exp(-logit))
                rows = []
                for ab in range(4):
                    probs[ab, pl.ds(slot, 1), :] = prob[ab : ab + 1]
                    rows.append(wanted[ab, pl.ds(line, 1), :])
                target = jnp.concatenate(rows + [jnp.zeros((4, TOK), F32)], axis=0)
                d_logit = ((prob - target) * (valid / (MASK * MASK)) * live).astype(BF)
                d_logits.append(d_logit.astype(F32))
            sixteens = [jnp.concatenate([d, jnp.zeros((8, TOK), F32)], axis=0).astype(BF) for d in d_logits]
            outers = [dot(sixteens[k], up[k]) for k in range(group)]
            dec_total = jnp.zeros((8, C), F32)
            grads = []
            for k in range(group):
                grad = jnp.zeros((TOK, C), F32)
                for ab in range(4):
                    cols = slice(ab * C, (ab + 1) * C)
                    d_up = dot_tn(sixteens[k], heads[k][0][:, cols])
                    d_pre = d_up * up_slope[k, :, cols].astype(F32)
                    dec_total += jnp.sum(d_pre.reshape(TOK // 8, 8, C), axis=0)
                    d_pre = d_pre.astype(BF)
                    dpd[k, 0:TOK, cols] = d_pre
                    grad += dot_nt(d_pre, dec_w[:, cols])
                grads.append(grad)
            dec_sum[...] += dec_total
            top_total = jnp.zeros((8, C), F32)
            for k, n in enumerate(at):
                d_pre = grads[k] * slope[TOP, n].astype(F32)
                top_total += jnp.sum(d_pre.reshape(TOK // 8, 8, C), axis=0)
                spread(dpw[k], d_pre, 2, 0)
                wide = jnp.concatenate([dpw[k][32 - 16 * ky : 32 - 16 * ky + TOK] for ky in range(3)], axis=1)
                slope[TOP - 1, n] = (dot(wide, top_wt[...]) * slope[TOP - 1, n].astype(F32)).astype(BF)
            top_sum[...] += top_total
            for k in range(group):
                gathered = jnp.zeros((16, C), F32)
                for ab in range(4):
                    gathered += jnp.where(row == ab, outers[k][:, ab * C : (ab + 1) * C], 0.0)
                total = jnp.sum(jnp.sum(d_logits[k], axis=1, keepdims=True), axis=0, keepdims=True)
                misc[pl.ds(class_ids[k], 1), :] += jnp.sum(gathered, axis=0, keepdims=True)
                misc[pred_row : pred_row + 1, :] += jnp.where(lane == class_ids[k], total, 0.0)
            lhs = jnp.concatenate([x4t[k] for k in range(group)], axis=1)
            for ab in range(4):
                cols = slice(ab * C, (ab + 1) * C)
                rhs = jnp.concatenate([dpd[k, :, cols] for k in range(group)], axis=0)
                acc_dec[ab] += dot(lhs, rhs)
            lhs = jnp.concatenate([xt[TOP, n] for n in at], axis=1)
            for tap in range(9):
                rows = slice(32 - 16 * (tap // 3), 288 - 16 * (tap // 3))
                cols = slice(tap % 3 * C, (tap % 3 + 1) * C)
                rhs = jnp.concatenate([dpw[k][rows, cols] for k in range(group)], axis=0)
                acc[tap * C : (tap + 1) * C, :] += dot(lhs, rhs)
            for n in at:
                for copy in sends(base, n):
                    copy.start()
            return 0

        return run

    def clear(base):
        def one(n, _):
            for layer in range(TOP):
                xt[layer, n] = jnp.zeros((C, C), BF)
                slope[layer, n] = jnp.zeros((TOK, C), BF)
            for copy in sends(base, n):
                copy.start()
            return 0

        return one

    def wait_for(n, _):
        for copy in sends(0, n):
            copy.wait()
        return 0

    def run_chunk(c, _):
        base = c * chunk
        here = jnp.clip(count - base, 0, chunk)
        wide = here // GROUP
        pairs = (here - wide * GROUP + 1) // 2
        lax.fori_loop(wide * GROUP + 2 * pairs, chunk, clear(base), 0)
        lax.fori_loop(0, wide, forward(base, 0, GROUP), 0)
        lax.fori_loop(0, pairs, forward(base, wide * GROUP, 2), 0)
        lax.fori_loop(0, chunk, wait_for, 0)
        return 0

    if chunks == 1:
        run_chunk(0, 0)
    else:
        lax.fori_loop(0, chunks, run_chunk, 0)

    misc[pred_row + 8 : pred_row + 9, :] = jnp.sum(dec_sum[...], axis=0, keepdims=True)
    first = bias_rows(classes_all) + TOP
    misc[first : first + 1, :] = jnp.sum(top_sum[...], axis=0, keepdims=True)
    small_v[0:MISC, :] = misc[...].astype(BF)
    small_v[MISC : MISC + 9 * C, :] = acc[...].astype(BF)
    for ab in range(4):
        first = MISC + 9 * C + ab * C
        small_v[first : first + C, :] = acc_dec[ab].astype(BF)
    send_small = pltpu.make_async_copy(small_v, small, small_sem)
    send_small.start()
    image = jnp.zeros((slots, LINE), F32)
    for ab in range(4):
        prob = probs[ab, 0:slots, :]
        high = prob.astype(BF)
        low = (prob - high.astype(F32)).astype(BF)
        image += dot(high, moves[ab]) + dot(low, moves[ab])
    masks[...] = image[:, 0:PIXELS]
    send_small.wait()


def processed(slots, pair, tags, order):
    def collect(slot, count):
        order[count] = slot
        return count + tags[line_of(slot, pair), PIXELS % 128 + 1]

    count = lax.fori_loop(0, slots, collect, 0)
    order[count] = 0
    return count


def line_of(slot, pair):
    return slot // pair * 8 + slot % pair


def head(slots, classes_all, boxes, tags, lines, p2, p3, p4, p5, conv_w, conv_wt, *weights):
    chunk = min(CHUNK, slots)
    images = lines.shape[0]
    cells = p2.shape[0] + p3.shape[0] + p4.shape[0] + p5.shape[0]
    any_spec = pl.BlockSpec(memory_space=pl.ANY)
    vmem = pl.BlockSpec(memory_space=pltpu.VMEM)
    smem = pl.BlockSpec(memory_space=pltpu.SMEM)
    return pl.pallas_call(
        functools.partial(head_kernel, slots, classes_all, images),
        out_shape=(
            jax.ShapeDtypeStruct((slots, PIXELS), F32),
            jax.ShapeDtypeStruct((TOP, slots, C, C), BF),
            jax.ShapeDtypeStruct((TOP, slots, TOK, C), BF),
            jax.ShapeDtypeStruct((MISC + HEAD_ROWS, C), BF),
        ),
        in_specs=[smem, smem, vmem] + [any_spec] * 6 + [vmem] * 5,
        out_specs=[vmem] + [any_spec] * 3,
        scratch_shapes=[
            pltpu.SMEM((slots + 2,), jnp.int32),
            pltpu.VMEM((cells + WIN, C), BF),
            pltpu.VMEM((LAYERS, chunk, C, C), BF),
            pltpu.VMEM((LAYERS, chunk, TOK, C), BF),
            pltpu.VMEM((GROUP, TOK, 4 * C), BF),
            pltpu.VMEM((GROUP, TOK, 4 * C), BF),
            pltpu.VMEM((GROUP, C, 4 * C), BF),
            pltpu.VMEM((GROUP, C, C), BF),
            pltpu.VMEM((4, C, C), F32),
            pltpu.VMEM((9 * C, C), F32),
            pltpu.VMEM((MISC, C), F32),
            pltpu.VMEM((8, C), F32),
            pltpu.VMEM((8, C), F32),
            pltpu.VMEM((LAYERS, TOK, C), F32),
            pltpu.VMEM((TOK, C), F32),
            pltpu.VMEM((MISC + HEAD_ROWS, C), BF),
            pltpu.VMEM(conv_w.shape, BF),
            pltpu.VMEM((9 * C, C), BF),
            pltpu.VMEM((4, TOK, LINE), BF),
            pltpu.VMEM((4, images * 8, TOK), F32),
            pltpu.VMEM((4, slots + 8, TOK), F32),
            pltpu.SemaphoreType.DMA((4,)),
            pltpu.SemaphoreType.DMA((LAYERS + 1,)),
            pltpu.SemaphoreType.DMA((chunk, 2)),
            pltpu.SemaphoreType.DMA,
        ]
        + [pltpu.VMEM((XROWS, 3 * C), BF)] * GROUP
        + [pltpu.VMEM((DROWS, 3 * C), BF)] * GROUP,
        compiler_params=pltpu.CompilerParams(vmem_limit_bytes=60 * 2**20),
        name="head",
    )(boxes, tags, lines, p2, p3, p4, p5, conv_w, conv_wt, *weights)


def finish_kernel(
    slots,
    classes_all,
    images,
    boxes,
    tags,
    dx0,
    summed,
    g2,
    g3,
    g4,
    g5,
    conv_g,
    conv_bg,
    dec_g,
    dec_bg,
    pred_g,
    pred_bg,
    order,
    table_grad,
    sum_v,
    conv_v,
    in_sem,
    conv_sem,
    out_sem,
):
    pieces = LAYERS
    size = 9 * C
    loads = []
    for k in range(pieces):
        at = pl.ds(MISC + k * size, size)
        loads.append(pltpu.make_async_copy(summed.at[at], sum_v.at[at], in_sem.at[k]))
    for k, at in enumerate((pl.ds(0, MISC), pl.ds(SUM_ROWS - DEC, DEC))):
        loads.append(pltpu.make_async_copy(summed.at[at], sum_v.at[at], in_sem.at[pieces + k]))
    for load in loads:
        load.start()
    pair = slots // images
    count = processed(slots, pair, tags, order)
    table_grad[...] = jnp.zeros_like(table_grad)
    stores = []
    for k in range(pieces):
        loads[k].wait()
        conv_v[k] = sum_v[MISC + k * size : MISC + (k + 1) * size, :].astype(F32)
        stores.append(pltpu.make_async_copy(conv_v.at[k], conv_g.at[k], conv_sem.at[k]))
        stores[-1].start()

    def scatter(n, _):
        sampler = Sampler(boxes, order[n])
        across = sampler.across(0)

        def rows_of(cells):
            def run():
                for i in range(POOL):
                    start, down = sampler.down(i)
                    weights = (across * down).astype(BF)[:, 0:cells]
                    table_grad[pl.ds(start, cells), :] += dot_tn(weights, dx0[n, i * WIDE : (i + 1) * WIDE, :])

            return run

        pl.when(sampler.level == 0)(rows_of(128))
        pl.when(sampler.level == 1)(rows_of(64))
        pl.when(sampler.level >= 2)(rows_of(32))
        return 0

    lax.fori_loop(0, count, scatter, 0)
    at = 0
    for k, part in enumerate((g2, g3, g4, g5)):
        stores.append(pltpu.make_async_copy(table_grad.at[pl.ds(at, part.shape[0])], part, out_sem.at[k]))
        stores[-1].start()
        at += part.shape[0]
    for load in loads[pieces:]:
        load.wait()
    for ab in range(4):
        first = SUM_ROWS - DEC + ab * C
        dec_g[:, ab * C : (ab + 1) * C] = sum_v[first : first + C, :].astype(F32)
    misc = sum_v[0:MISC, :].astype(F32)
    pred_row = (classes_all + 7) // 8 * 8
    bias_row = bias_rows(classes_all)
    pred_g[...] = misc[0:classes_all]
    pred_bg[...] = misc[pred_row : pred_row + 1, 0:classes_all]
    dec_bg[...] = misc[pred_row + 8 : pred_row + 9]
    conv_bg[...] = misc[bias_row : bias_row + LAYERS]
    for store in stores:
        store.wait()


def finish(slots, classes_all, images, boxes, tags, dx0, summed, levels):
    cells = sum(levels)
    any_spec = pl.BlockSpec(memory_space=pl.ANY)
    vmem = pl.BlockSpec(memory_space=pltpu.VMEM)
    smem = pl.BlockSpec(memory_space=pltpu.SMEM)
    return pl.pallas_call(
        functools.partial(finish_kernel, slots, classes_all, images),
        out_shape=(
            *(jax.ShapeDtypeStruct((level, C), F32) for level in levels),
            jax.ShapeDtypeStruct((LAYERS, 9 * C, C), F32),
            jax.ShapeDtypeStruct((LAYERS, C), F32),
            jax.ShapeDtypeStruct((C, 4 * C), F32),
            jax.ShapeDtypeStruct((1, C), F32),
            jax.ShapeDtypeStruct((classes_all, C), F32),
            jax.ShapeDtypeStruct((1, classes_all), F32),
        ),
        in_specs=[smem, smem, vmem, any_spec],
        out_specs=[any_spec] * 5 + [vmem] * 5,
        scratch_shapes=[
            pltpu.SMEM((slots + 2,), jnp.int32),
            pltpu.VMEM((cells + WIN, C), F32),
            pltpu.VMEM((SUM_ROWS, C), BF),
            pltpu.VMEM((LAYERS, 9 * C, C), F32),
            pltpu.SemaphoreType.DMA((LAYERS + 2,)),
            pltpu.SemaphoreType.DMA((LAYERS,)),
            pltpu.SemaphoreType.DMA((4,)),
        ],
        compiler_params=pltpu.CompilerParams(vmem_limit_bytes=60 * 2**20),
        name="finish",
    )(boxes, tags, dx0, summed)


def body(
    images,
    groups,
    p2,
    p3,
    p4,
    p5,
    roi_boxes,
    recv_index,
    classes,
    targets,
    conv_weights,
    conv_biases,
    deconv_weight,
    deconv_bias,
    predictor_weight,
    predictor_bias,
):
    slots = roi_boxes.shape[-1]
    classes_all = predictor_weight.shape[1]
    boxes = roi_boxes[0].transpose(1, 0, 2)
    lines, tags, conv_wt = exchange(
        images, slots // images, targets[0, 0], recv_index[0], classes[0], conv_weights
    )
    masks, xt, slope, small = head(
        slots,
        classes_all,
        boxes,
        tags,
        lines,
        p2[0, 0],
        p3[0, 0],
        p4[0, 0],
        p5[0, 0],
        conv_weights,
        conv_wt,
        conv_biases,
        deconv_weight,
        deconv_bias.reshape(2, C // 2),
        predictor_weight.T,
        predictor_bias[None, :],
    )
    total = sum_all if images == 8 and groups == 4 else sum_plain
    summed, dx0 = total(classes_all, xt, slope, conv_weights, conv_wt, small)
    levels = [p.shape[2] for p in (p2, p3, p4, p5)]
    g2, g3, g4, g5, conv_g, conv_bg, dec_g, dec_bg, pred_g, pred_bg = finish(
        slots, classes_all, images, boxes, tags, dx0, summed, levels
    )
    return (
        masks[None, None],
        g2[None, None],
        g3[None, None],
        g4[None, None],
        g5[None, None],
        conv_g,
        conv_bg,
        dec_g,
        dec_bg[0],
        pred_g.T,
        pred_bg[0],
    )


def solution(mesh):
    split = P("img", "grp", None, None)
    in_specs = (split,) * 5 + (P("img", "grp", None),) * 2 + (split,) + (P(),) * 6
    out_specs = (split,) * 5 + (P(),) * 6
    return jax.shard_map(
        functools.partial(body, mesh.shape["img"], mesh.shape["grp"]),
        mesh=mesh,
        in_specs=in_specs,
        out_specs=out_specs,
        check_vma=False,
    )
```

```python
import functools

import jax
import jax.numpy as jnp
from jax import lax
from jax.experimental import pallas as pl
from jax.experimental.pallas import tpu as pltpu
from jax.sharding import PartitionSpec as P

MESH = pl.DeviceIdType.MESH
POOL = 14
LAYERS = 4
MASK = 28
PIXELS = MASK * MASK
LINE = 896
C = 256
WIDE = 16
TOK = POOL * WIDE
XROWS = 272
DROWS = 288
WIN = 128
CHUNK = 16
GROUP = 4
UNIT = 512
MISC = UNIT
DEC = 4 * C
TOP = LAYERS - 1
HEAD_ROWS = 9 * C + DEC
SUM_ROWS = MISC + LAYERS * 9 * C + DEC
SUM_PARTS = tuple((units, "xy") for units in (2, 2, 2, 3, 2, 2, 3, 2, 1, 2))
SUM_GAP = 3
TAIL_GAP = 2
SUM_ENTER = 3
GA = 0.7978845608028654
GB = GA * 0.044715
BF = jnp.bfloat16
F32 = jnp.float32


def dot(a, b):
    return jnp.dot(a, b, preferred_element_type=F32)


def dot_nt(a, b):
    return lax.dot_general(a, b, (((1,), (1,)), ((), ())), preferred_element_type=F32)


def dot_tn(a, b):
    return lax.dot_general(a, b, (((0,), (0,)), ((), ())), preferred_element_type=F32)


def gelu_both(x):
    square = x * x
    gate = 0.5 + 0.5 * jnp.tanh(x * (GA + GB * square))
    value = x * gate
    slope = gate + (value - value * gate) * (2 * GA + 6 * GB * square)
    return value, slope


def exchange_kernel(
    n,
    pair,
    targets,
    picked,
    classes,
    conv_w,
    lines,
    tags,
    conv_wt,
    targets_v,
    picked_v,
    classes_v,
    lines_v,
    tags_v,
    conv_v,
    turned,
    leaving,
    send_sem,
    recv_sem,
    own_sem,
    in_sem,
    w_sem,
    out_sem,
):
    me = lax.axis_index("img")
    grp = lax.axis_index("grp")
    barrier = pltpu.get_barrier_semaphore()
    for k in range(1, n):
        pl.semaphore_signal(barrier, inc=1, device_id=(lax.rem(me + k, n), grp), device_id_type=MESH)
    loads = []
    for k, (source, target) in enumerate(((targets, targets_v), (picked, picked_v), (classes, classes_v))):
        loads.append(pltpu.make_async_copy(source, target, in_sem.at[k]))
    for layer in range(LAYERS):
        loads.append(pltpu.make_async_copy(conv_w.at[layer], conv_v.at[layer], w_sem.at[layer]))
    for load in loads:
        load.start()
    leaving[...] = jnp.zeros_like(leaving)
    for load in loads[:3]:
        load.wait()
    slots, rois = n * pair, targets.shape[0]
    chosen = (lax.broadcasted_iota(jnp.int32, (slots, rois), 0) == picked_v[...]).astype(F32)
    rows = dot(chosen.astype(BF), targets_v[...].astype(F32).astype(BF))
    label = jnp.sum(chosen * classes_v[...].astype(F32), axis=1, keepdims=True)
    flag = jnp.sum(chosen, axis=1, keepdims=True)
    lane = lax.broadcasted_iota(jnp.int32, (slots, 128), 1)
    mark = jnp.where(lane == PIXELS % 128, label, jnp.where(lane == PIXELS % 128 + 1, flag, 0.0))
    whole = PIXELS // 128 * 128
    last = jnp.concatenate([rows[:, whole:], jnp.zeros((slots, LINE - PIXELS), F32)], axis=1) + mark
    for i in range(n):
        leaving[i, 0:pair, 0:whole] = rows[i * pair : (i + 1) * pair, 0:whole]
        leaving[i, 0:pair, whole:LINE] = last[i * pair : (i + 1) * pair]
    own = pltpu.make_async_copy(leaving.at[me], lines_v.at[me], own_sem)
    own.start()
    pl.semaphore_wait(barrier, n - 1)
    copies = []
    for k in range(1, n):
        peer = lax.rem(me + k, n)
        copy = pltpu.make_async_remote_copy(
            src_ref=leaving.at[peer],
            dst_ref=lines_v.at[me],
            send_sem=send_sem.at[k - 1],
            recv_sem=recv_sem.at[k - 1],
            device_id=(peer, grp),
            device_id_type=MESH,
        )
        copy.start()
        copies.append(copy)

    def turn(layer):
        def one(tap, _):
            at = pl.ds(pl.multiple_of(tap * C, C), C)
            turned[layer, at, :] = conv_v[layer, at, :].T
            return 0

        lax.fori_loop(0, 9, one, 0)

    stores = []
    for layer in range(LAYERS):
        loads[3 + layer].wait()
        turn(layer)
        stores.append(pltpu.make_async_copy(turned.at[layer], conv_wt.at[layer], w_sem.at[layer]))
        stores[-1].start()
    own.wait()
    for copy in copies:
        copy.wait()
    for i in range(n):
        tags_v[i * 8 : (i + 1) * 8, :] = lines_v[i, :, whole:LINE].astype(jnp.int32)
    stores.append(pltpu.make_async_copy(lines_v, lines, out_sem.at[0]))
    stores.append(pltpu.make_async_copy(tags_v, tags, out_sem.at[1]))
    for store in stores[LAYERS:]:
        store.start()
    for store in stores:
        store.wait()


def exchange(n, pair, targets, picked, classes, conv_w):
    any_spec = pl.BlockSpec(memory_space=pl.ANY)
    return pl.pallas_call(
        functools.partial(exchange_kernel, n, pair),
        out_shape=(
            jax.ShapeDtypeStruct((n, 8, LINE), F32),
            jax.ShapeDtypeStruct((n * 8, 128), jnp.int32),
            jax.ShapeDtypeStruct(conv_w.shape, BF),
        ),
        in_specs=[any_spec] * 4,
        out_specs=[any_spec] * 3,
        scratch_shapes=[
            pltpu.VMEM(targets.shape, jnp.int32),
            pltpu.VMEM(picked.shape, jnp.int32),
            pltpu.VMEM(classes.shape, jnp.int32),
            pltpu.VMEM((n, 8, LINE), F32),
            pltpu.VMEM((n * 8, 128), jnp.int32),
            pltpu.VMEM(conv_w.shape, BF),
            pltpu.VMEM(conv_w.shape, BF),
            pltpu.VMEM((n, 8, LINE), F32),
            pltpu.SemaphoreType.DMA((n - 1,)),
            pltpu.SemaphoreType.DMA((n - 1,)),
            pltpu.SemaphoreType.DMA,
            pltpu.SemaphoreType.DMA((3,)),
            pltpu.SemaphoreType.DMA((LAYERS,)),
            pltpu.SemaphoreType.DMA((2,)),
        ],
        compiler_params=pltpu.CompilerParams(collective_id=0, has_side_effects=True, vmem_limit_bytes=60 * 2**20),
        name="exchange",
    )(targets, picked, classes, conv_w)


def sum_kernel(
    classes_all,
    xt,
    slope,
    conv_wt,
    small,
    out,
    d_bottom,
    xt_v,
    slope_v,
    wt_v,
    small_v,
    sums,
    leaving,
    mine,
    from_core,
    from_one,
    from_two,
    from_z,
    res,
    in_sem,
    send_sem,
    recv_sem,
    out_sem,
    bottom_sem,
    *held,
):
    img, grp = lax.axis_index("img"), lax.axis_index("grp")
    x, core = grp // 2, grp % 2
    z, y = img // 2, img % 2
    sizes = [UNIT * units for units, kind in SUM_PARTS]
    kinds = [kind for units, kind in SUM_PARTS]
    starts = [SUM_ROWS - sum(sizes[: k + 1]) for k in range(len(sizes))]
    chunks = len(sizes)
    spans = [slice(start, start + size) for start, size in zip(starts, sizes)]
    other_core = (img, x * 2 + 1 - core)
    other_x = (img, (1 - x) * 2 + core)
    other_y = (z * 2 + 1 - y, grp)
    others_z = [(lax.rem(z + k, 4) * 2 + y, grp) for k in range(1, 4)]
    lanes = C // 2
    kept_lanes = pl.ds(pl.multiple_of(core * lanes, lanes), lanes)

    barrier = pltpu.get_barrier_semaphore()
    peers = [other_core, other_x, other_y] + others_z
    for peer in peers:
        pl.semaphore_signal(barrier, inc=1, device_id=peer, device_id_type=MESH)
    load_small = pltpu.make_async_copy(small, small_v, in_sem.at[3 * TOP])
    load_slope, load_wt, load_xt = {}, {}, {}
    for layer in range(TOP):
        load_slope[layer] = pltpu.make_async_copy(slope.at[layer], slope_v.at[layer], in_sem.at[3 * layer])
        load_wt[layer] = pltpu.make_async_copy(conv_wt.at[layer], wt_v.at[layer], in_sem.at[3 * layer + 1])
        load_xt[layer] = pltpu.make_async_copy(xt.at[layer], xt_v.at[layer], in_sem.at[3 * layer + 2])

    def load_layer(layer):
        load_slope[layer].start()
        load_wt[layer].start()
        load_xt[layer].start()

    load_small.start()
    load_layer(TOP - 1)
    frames, dx = held[:GROUP], held[GROUP:]
    blocks = xt.shape[1]
    each = blocks // GROUP
    for frame in frames:
        frame[:, 0:16, :] = jnp.zeros((each, 16, 3 * C), BF)
        frame[:, 16 + TOK : DROWS, :] = jnp.zeros((each, DROWS - 16 - TOK, 3 * C), BF)
    sums[...] = jnp.zeros_like(sums)
    pl.semaphore_wait(barrier, len(peers))

    def remote(k, lane, source, target, peer):
        copy = pltpu.make_async_remote_copy(
            src_ref=source,
            dst_ref=target,
            send_sem=send_sem.at[k, lane],
            recv_sem=recv_sem.at[k, lane],
            device_id=peer,
            device_id_type=MESH,
        )
        copy.start()
        return copy

    bits, across = {"x": (x, y), "y": (y, x)}, {"x": (other_x, other_y), "y": (other_y, other_x)}

    def place(k, s, depth):
        size = sizes[k] // len(kinds[k])
        at = starts[k] + s * size
        for level in range(abs(depth)):
            size = size // 2
            bit = bits[kinds[k][s]][level]
            at = at + (1 - bit if level + 1 == -depth else bit) * size
        return at, size

    def rows_at(k, s, depth):
        at, size = place(k, s, depth)
        return pl.ds(pl.multiple_of(at, 16), size)

    def shard_at(k, s, owner):
        at, size = place(k, s, 2)
        return pl.ds(pl.multiple_of(at + owner * (size // 4), 16), size // 4)

    def landing(k, s, cut, d=0):
        size = sizes[k] // (len(kinds[k]) * cut)
        per = 3 if cut == 16 else 1
        first = starts[k] // cut * per + (per * s + d) * size
        return slice(first, first + size)

    flying = {}

    def arrived(stage, k):
        for copy in flying.pop((stage, k)):
            copy.wait()

    def put(at, value):
        low, high = value[:, :lanes], value[:, lanes:]
        first = core == 0
        mine[at, :] = jnp.where(first, low, high).astype(BF)
        leaving[at, :] = jnp.where(first, high, low).astype(BF)

    def spread(layer, k, q):
        value = slope_v[layer, k * each + q].astype(F32)
        if layer < TOP - 1:
            value = dx[k][q] * value
        frames[k][q, 16 : 16 + TOK, 0:C] = pltpu.roll(value, TOK - 1, 0).astype(BF)
        frames[k][q, 16 : 16 + TOK, C : 2 * C] = value.astype(BF)
        frames[k][q, 16 : 16 + TOK, 2 * C : 3 * C] = pltpu.roll(value, 1, 0).astype(BF)
        return jnp.sum(value.reshape(TOK // 8, 8, C), axis=0)

    def back(layer, k, q):
        wide = jnp.concatenate([frames[k][q, 32 - 16 * ky : 32 - 16 * ky + TOK] for ky in range(3)], axis=1)
        return dot(wide, wt_v[layer])

    def inputs(layer, part):
        def four(q, _):
            total = jnp.zeros((8, C), F32)
            for k in range(GROUP):
                if layer > 0:
                    total += spread(layer, k, q)
                    dx[k][q] = back(layer, k, q)
                else:
                    slope_v[0, k * each + q] = back(0, k, q).astype(BF)
            if layer > 0:
                sums[layer] += total
            return 0

        if part == 0 and layer > 0:
            load_slope[layer].wait()
        if part == 0:
            load_wt[layer].wait()
        if part == 0 and layer > 0:
            load_layer(layer - 1)
        lax.fori_loop(part * each // 2, (part + 1) * each // 2, four, 0)

    def lowest():
        load_slope[0].wait()

        def four(q, _):
            total = jnp.zeros((8, C), F32)
            for k in range(GROUP):
                total += spread(0, k, q)
            sums[0] += total
            return 0

        lax.fori_loop(0, each, four, 0)
        put(slice(0, MISC), small_v[0:MISC, :].astype(F32))
        row = lax.broadcasted_iota(jnp.int32, (16, C), 0)
        first = bias_rows(classes_all)
        biases = small_v[first : first + 16, :].astype(F32)
        for layer in range(TOP):
            biases += jnp.where(row == layer, jnp.sum(sums[layer], axis=0, keepdims=True), 0.0)
        put(slice(first, first + 16), biases)

    def weights(layer, taps):
        for tap in taps:
            if tap == 8:
                load_xt[layer].wait()
            ky, kx = tap // 3, tap % 3
            lhs = jnp.concatenate([xt_v[layer, n] for n in range(blocks)], axis=1)
            rhs = jnp.concatenate(
                [
                    frames[n // each][n % each, 32 - 16 * ky : 288 - 16 * ky, kx * C : (kx + 1) * C]
                    for n in range(blocks)
                ],
                axis=0,
            )
            at = MISC + (9 * layer + tap) * C
            put(slice(at, at + C), dot(lhs, rhs))

    def stage_core(k):
        flying[0, k] = [remote(k, 0, leaving.at[spans[k]], from_core.at[spans[k]], other_core)]

    def parts(k):
        return range(len(kinds[k]))

    def stage_one(k):
        arrived(0, k)
        at = spans[k]
        mine[at, :] = (mine[at, :].astype(F32) + from_core[at, :].astype(F32)).astype(BF)
        flying[1, k] = [
            remote(k, 1 + s, mine.at[rows_at(k, s, -1)], from_one.at[landing(k, s, 2)], across[kinds[k][s]][0])
            for s in parts(k)
        ]

    def stage_two(k):
        arrived(1, k)
        copies = []
        for s in parts(k):
            at = rows_at(k, s, 1)
            mine[at, :] = (mine[at, :].astype(F32) + from_one[landing(k, s, 2), :].astype(F32)).astype(BF)
            leave = mine.at[rows_at(k, s, -2)]
            copies.append(remote(k, 3 + s, leave, from_two.at[landing(k, s, 4)], across[kinds[k][s]][1]))
        flying[2, k] = copies

    def stage_three(k):
        arrived(2, k)
        copies = []
        for s in parts(k):
            at = rows_at(k, s, 2)
            mine[at, :] = (mine[at, :].astype(F32) + from_two[landing(k, s, 4), :].astype(F32)).astype(BF)
            for d in range(3):
                leave = mine.at[shard_at(k, s, lax.rem(z + 1 + d, 4))]
                copies.append(remote(k, 5 + 3 * s + d, leave, from_z.at[landing(k, s, 16, d)], others_z[d]))
        flying[3, k] = copies

    def stage_four(k):
        arrived(3, k)
        copies = []
        for s in parts(k):
            at = shard_at(k, s, z)
            total = mine[at, :].astype(F32)
            for d in range(3):
                total += from_z[landing(k, s, 16, d), :].astype(F32)
            res[at, kept_lanes] = total.astype(BF)
            for d in range(3):
                block = res.at[at, kept_lanes]
                copies.append(remote(k, 11 + 3 * s + d, block, block, others_z[d]))
        flying[4, k] = copies

    def stage_five(k):
        arrived(4, k)
        blocks = [res.at[rows_at(k, s, 2), kept_lanes] for s in parts(k)]
        flying[5, k] = [remote(k, 17 + s, blocks[s], blocks[s], across[kinds[k][s]][1]) for s in parts(k)]

    def stage_six(k):
        arrived(5, k)
        blocks = [res.at[rows_at(k, s, 1), kept_lanes] for s in parts(k)]
        flying[6, k] = [remote(k, 19 + s, blocks[s], blocks[s], across[kinds[k][s]][0]) for s in parts(k)]

    def stage_seven(k):
        arrived(6, k)
        block = res.at[spans[k], kept_lanes]
        flying[7, k] = [remote(k, 21, block, block, other_core)]

    outs = []

    def stage_out(k):
        arrived(7, k)
        outs.append(pltpu.make_async_copy(res.at[spans[k]], out.at[spans[k]], out_sem.at[k]))
        outs[-1].start()

    stages = [stage_one, stage_two, stage_three, stage_four, stage_five, stage_six, stage_seven, stage_out]
    work = []
    for layer in reversed(range(TOP)):
        top = MISC + 9 * layer * C
        if layer > 0:
            for part in range(2):
                work.append((functools.partial(inputs, layer, part), None))
        else:
            work.append((lowest, None))
        for taps in ((8, 7), (6, 5), (4, 3), (2, 1, 0)):
            work.append((functools.partial(weights, layer, taps), top + taps[-1] * C))
    work[-1] = (work[-1][0], 0)
    for part in range(2):
        work.append((functools.partial(inputs, 0, part), None))

    load_small.wait()
    put(slice(SUM_ROWS - HEAD_ROWS, SUM_ROWS), small_v[MISC:, :].astype(F32))
    ready = SUM_ROWS - HEAD_ROWS
    due = {}
    step, first = 0, 0
    while len(outs) < chunks or step < len(work):
        gap = SUM_GAP if step < len(work) else TAIL_GAP
        for k in range(chunks):
            if k in due and due[k][1] <= step and due[k][0] < len(stages):
                stages[due[k][0]](k)
                due[k] = (due[k][0] + 1, step + gap)
        for _ in range(SUM_ENTER):
            if first == chunks or starts[first] < ready:
                break
            due[first] = (0, step + gap)
            stage_core(first)
            first += 1
        if step < len(work):
            run, now = work[step]
            run()
            ready = ready if now is None else now
            if step == len(work) - 1:
                bottom = pltpu.make_async_copy(slope_v.at[0], d_bottom, bottom_sem)
                bottom.start()
        step += 1
    bottom.wait()
    for copy in outs:
        copy.wait()


def bias_rows(classes_all):
    return (classes_all + 7) // 8 * 8 + 16


def sum_all(classes_all, xt, slope, conv_w, conv_wt, small):
    blocks = xt.shape[1]
    chunks = len(SUM_PARTS)
    any_spec = pl.BlockSpec(memory_space=pl.ANY)
    return pl.pallas_call(
        functools.partial(sum_kernel, classes_all),
        out_shape=(jax.ShapeDtypeStruct((SUM_ROWS, C), BF), jax.ShapeDtypeStruct(slope.shape[1:], BF)),
        in_specs=[any_spec] * 4,
        out_specs=[any_spec] * 2,
        scratch_shapes=[
            pltpu.VMEM(xt.shape, BF),
            pltpu.VMEM(slope.shape, BF),
            pltpu.VMEM((TOP, 9 * C, C), BF),
            pltpu.VMEM(small.shape, BF),
            pltpu.VMEM((TOP, 8, C), F32),
            pltpu.VMEM((SUM_ROWS, C // 2), BF),
            pltpu.VMEM((SUM_ROWS, C // 2), BF),
            pltpu.VMEM((SUM_ROWS, C // 2), BF),
            pltpu.VMEM((SUM_ROWS // 2, C // 2), BF),
            pltpu.VMEM((SUM_ROWS // 4, C // 2), BF),
            pltpu.VMEM((SUM_ROWS // 16 * 3, C // 2), BF),
            pltpu.VMEM((SUM_ROWS, C), BF),
            pltpu.SemaphoreType.DMA((3 * TOP + 1,)),
            pltpu.SemaphoreType.DMA((chunks, 22)),
            pltpu.SemaphoreType.DMA((chunks, 22)),
            pltpu.SemaphoreType.DMA((chunks,)),
            pltpu.SemaphoreType.DMA,
        ]
        + [pltpu.VMEM((blocks // GROUP, DROWS, 3 * C), BF)] * GROUP
        + [pltpu.VMEM((blocks // GROUP, TOK, C), F32)] * GROUP,
        compiler_params=pltpu.CompilerParams(collective_id=1, has_side_effects=True, vmem_limit_bytes=60 * 2**20),
        name="sum_all",
    )(xt, slope, conv_wt, small)


def sum_plain(classes_all, xt, slope, conv_w, conv_wt, small):
    slots = slope.shape[1]
    chunk = min(CHUNK, slots)

    def some(c, carry):
        weights, biases, bottom = carry
        grad = 1.0
        parts, sums = [], []
        for layer in reversed(range(TOP)):
            d_pre = grad * lax.dynamic_slice_in_dim(slope[layer], c * chunk, chunk).astype(F32)
            sums.insert(0, jnp.sum(d_pre, axis=(0, 1)))
            padded = jnp.pad(d_pre.astype(BF), ((0, 0), (17, 49), (0, 0)))
            held = lax.dynamic_slice_in_dim(xt[layer], c * chunk, chunk)
            grad = 0.0
            taps = []
            for tap in range(9):
                at = 17 - 16 * (tap // 3 - 1) - (tap % 3 - 1)
                moved = padded[:, at : at + C]
                taps.append(jnp.einsum("nct,ntd->cd", held, moved, preferred_element_type=F32))
                kernel = conv_w[layer, tap * C : (tap + 1) * C]
                grad += jnp.einsum("ntd,cd->ntc", moved[:, :TOK], kernel, preferred_element_type=F32)
            parts = taps + parts
        bottom = lax.dynamic_update_slice_in_dim(bottom, grad.astype(BF), c * chunk, 0)
        return weights + jnp.concatenate(parts), biases + jnp.stack(sums), bottom

    carry = (jnp.zeros((TOP * 9 * C, C), F32), jnp.zeros((TOP, C), F32), jnp.zeros(slope.shape[1:], BF))
    weights, biases, bottom = lax.fori_loop(0, slots // chunk, some, carry)
    first = bias_rows(classes_all)
    misc = small[:MISC].astype(F32).at[first : first + TOP].set(biases)
    total = jnp.concatenate([misc, weights, small[MISC:].astype(F32)])
    return lax.psum(total.astype(BF), ("img", "grp")), bottom


class Sampler:
    def __init__(self, boxes, slot):
        level = boxes[0, 0, slot]
        self.level = level
        self.y0, self.x0 = boxes[1, 0, slot], boxes[2, 0, slot]
        self.sy, self.sx = boxes[3, 0, slot], boxes[4, 0, slot]
        self.shift = 6 - level
        self.side = jnp.left_shift(1, self.shift)
        self.offset = jnp.where(level == 0, 0, jnp.where(level == 1, 4096, jnp.where(level == 2, 5120, 5376)))
        self.cell = lax.broadcasted_iota(jnp.int32, (WIDE, WIN), 1)
        self.column = (self.cell & (self.side - 1)).astype(F32)
        self.band = lax.shift_right_logical(self.cell, self.shift)

    def across(self, moved):
        j = lax.broadcasted_iota(jnp.int32, (WIDE, WIN), 0) + moved
        at = jnp.where((j >= 0) & (j < POOL), self.x0 + j * self.sx, -64).astype(F32) * 0.25
        return jnp.maximum(1.0 - jnp.abs(at - self.column), 0.0)

    def down(self, i):
        qy = self.y0 + i * self.sy
        base = self.offset + jnp.left_shift(lax.shift_right_logical(qy, 2), self.shift)
        start = pl.multiple_of(jnp.left_shift(lax.shift_right_logical(base, 4), 4), 16)
        lead = lax.shift_right_logical(base - start, self.shift)
        fraction = (qy & 3).astype(F32) * 0.25
        row = self.band - lead
        return start, jnp.where(row == 0, 1.0 - fraction, jnp.where(row == 1, fraction, 0.0))


def head_kernel(
    slots,
    classes_all,
    images,
    boxes,
    tags,
    lines,
    p2,
    p3,
    p4,
    p5,
    conv_w_h,
    conv_wt_h,
    conv_b,
    dec_w,
    dec_b,
    pred_wt,
    pred_b,
    masks,
    xt_out,
    slope_out,
    small,
    order,
    table,
    xt,
    slope,
    up,
    up_slope,
    dpd,
    x4t,
    acc_dec,
    acc,
    misc,
    dec_sum,
    top_sum,
    bias2,
    bias_d,
    small_v,
    conv_w,
    top_wt,
    moves,
    wanted,
    probs,
    in_sem,
    w_sem,
    out_sem,
    small_sem,
    *frames,
):
    chunk = min(CHUNK, slots)
    chunks = slots // chunk
    pair = slots // images
    cells = p2.shape[0] + p3.shape[0] + p4.shape[0] + p5.shape[0]
    parts = []
    at = 0
    for k, part in enumerate((p2, p3, p4, p5)):
        parts.append(pltpu.make_async_copy(part, table.at[pl.ds(at, part.shape[0])], in_sem.at[k]))
        at += part.shape[0]
    for layer in range(LAYERS):
        parts.append(pltpu.make_async_copy(conv_w_h.at[layer], conv_w.at[layer], w_sem.at[layer]))
    parts.append(pltpu.make_async_copy(conv_wt_h.at[TOP], top_wt, w_sem.at[LAYERS]))
    xw, dpw = frames[:GROUP], frames[GROUP:]
    for part in parts:
        part.start()

    count = processed(slots, pair, tags, order)
    table[cells:, :] = jnp.zeros((table.shape[0] - cells, C), BF)
    probs[...] = jnp.zeros_like(probs)
    for frame in frames:
        frame[...] = jnp.zeros_like(frame)
    dpd[...] = jnp.zeros_like(dpd)
    acc_dec[...] = jnp.zeros_like(acc_dec)
    acc[...] = jnp.zeros_like(acc)
    top_sum[...] = jnp.zeros_like(top_sum)
    misc[...] = jnp.zeros_like(misc)
    dec_sum[...] = jnp.zeros_like(dec_sum)
    col = lax.broadcasted_iota(jnp.int32, (TOK, C), 0) & (WIDE - 1)
    off_block = jnp.where(col < POOL, 0.0, -1e4)
    for layer in range(LAYERS):
        bias2[layer] = off_block + conv_b[layer : layer + 1, :].astype(F32)
    bias_d[...] = off_block + jnp.concatenate([dec_b[0:1, :], dec_b[1:2, :]], axis=1).astype(F32)
    lane_ok = (lax.broadcasted_iota(jnp.int32, (8, TOK), 1) & (WIDE - 1)) < POOL
    row_ok = lax.broadcasted_iota(jnp.int32, (8, TOK), 0) < 4
    live = (lane_ok & row_ok).astype(F32)
    token = lax.broadcasted_iota(jnp.int32, (TOK, LINE), 0)
    pixel = lax.broadcasted_iota(jnp.int32, (TOK, LINE), 1)
    inside = (token & (WIDE - 1)) < POOL
    corner = lax.shift_right_logical(token, 4) * (2 * MASK) + (token & (WIDE - 1)) * 2
    all_lines = lines[...].reshape(images * 8, LINE).astype(BF)
    for ab in range(4):
        moves[ab] = (inside & (pixel == corner + (ab // 2 * MASK + ab % 2))).astype(F32).astype(BF)
        wanted[ab] = dot_nt(all_lines, moves[ab])
    for part in parts:
        part.wait()

    def spread(ref, value, first, last):
        ref[16 : 16 + TOK, C : 2 * C] = value.astype(BF)
        ref[16 : 16 + TOK, first * C : (first + 1) * C] = pltpu.roll(value, 1, 0).astype(BF)
        ref[16 : 16 + TOK, last * C : (last + 1) * C] = pltpu.roll(value, TOK - 1, 0).astype(BF)

    def sends(base, n):
        where = pl.ds(base + n, 1)
        return (
            pltpu.make_async_copy(xt.at[0:TOP, pl.ds(n, 1)], xt_out.at[:, where], out_sem.at[n, 0]),
            pltpu.make_async_copy(slope.at[0:TOP, pl.ds(n, 1)], slope_out.at[:, where], out_sem.at[n, 1]),
        )

    pred_row = (classes_all + 7) // 8 * 8

    def forward(base, first, group):
        def run(q, _):
            at = [first + group * q + k for k in range(group)]
            for k, n in enumerate(at):
                slot = order[base + n]
                sampler = Sampler(boxes, slot)
                across = jnp.concatenate([sampler.across(-1), sampler.across(0), sampler.across(1)], axis=0)
                for i in range(POOL):
                    start, down = sampler.down(i)
                    weights = across * jnp.concatenate([down] * 3, axis=0)
                    sampled = dot(weights.astype(BF), table[pl.ds(start, WIN), :]).astype(BF)
                    for b in range(3):
                        xw[k][16 * (i + 1) : 16 * (i + 2), b * C : (b + 1) * C] = sampled[b * WIDE : (b + 1) * WIDE]
            for layer in range(LAYERS):
                for k, n in enumerate(at):
                    xt[layer, n] = xw[k][16:XROWS, C : 2 * C].T
                    wide = jnp.concatenate([xw[k][16 * ky : 16 * ky + TOK] for ky in range(3)], axis=1)
                    pre = dot(wide, conv_w[layer]) + bias2[layer]
                    value, slope_now = gelu_both(pre)
                    slope[layer, n] = slope_now.astype(BF)
                    spread(xw[k], value, 0, 2)
            for k in range(group):
                x4 = xw[k][16 : 16 + TOK, C : 2 * C]
                x4t[k] = xw[k][16:XROWS, C : 2 * C].T
                for ab in range(4):
                    pre = dot(x4, dec_w[:, ab * C : (ab + 1) * C]) + bias_d[...]
                    value, slope_now = gelu_both(pre)
                    up[k, :, ab * C : (ab + 1) * C] = value.astype(BF)
                    up_slope[k, :, ab * C : (ab + 1) * C] = slope_now.astype(BF)
            row = lax.broadcasted_iota(jnp.int32, (16, C), 0)
            lane = lax.broadcasted_iota(jnp.int32, (1, C), 1)
            class_ids = [tags[line_of(order[base + n], pair), PIXELS % 128] for n in at]
            heads, d_logits = [], []
            for k, n in enumerate(at):
                picks = (lax.broadcasted_iota(jnp.int32, (16, classes_all), 1) == class_ids[k]).astype(F32)
                bias = jnp.sum(picks[0:1] * pred_b[...].astype(F32), axis=1, keepdims=True)
                weight = dot(picks.astype(BF), pred_wt[...])
                blocks = jnp.concatenate([jnp.where(row == ab, weight, 0.0) for ab in range(4)], axis=1).astype(BF)
                heads.append((blocks, bias))
            for k, n in enumerate(at):
                blocks, bias = heads[k]
                index = base + n
                valid = (index < count).astype(F32)
                slot = jnp.where(index < count, order[index], slots)
                line = line_of(order[index], pair)
                logit = dot_nt(blocks, up[k])[0:8] + bias
                prob = 1.0 / (1.0 + jnp.exp(-logit))
                rows = []
                for ab in range(4):
                    probs[ab, pl.ds(slot, 1), :] = prob[ab : ab + 1]
                    rows.append(wanted[ab, pl.ds(line, 1), :])
                target = jnp.concatenate(rows + [jnp.zeros((4, TOK), F32)], axis=0)
                d_logit = ((prob - target) * (valid / (MASK * MASK)) * live).astype(BF)
                d_logits.append(d_logit.astype(F32))
            sixteens = [jnp.concatenate([d, jnp.zeros((8, TOK), F32)], axis=0).astype(BF) for d in d_logits]
            outers = [dot(sixteens[k], up[k]) for k in range(group)]
            dec_total = jnp.zeros((8, C), F32)
            grads = []
            for k in range(group):
                grad = jnp.zeros((TOK, C), F32)
                for ab in range(4):
                    cols = slice(ab * C, (ab + 1) * C)
                    d_up = dot_tn(sixteens[k], heads[k][0][:, cols])
                    d_pre = d_up * up_slope[k, :, cols].astype(F32)
                    dec_total += jnp.sum(d_pre.reshape(TOK // 8, 8, C), axis=0)
                    d_pre = d_pre.astype(BF)
                    dpd[k, 0:TOK, cols] = d_pre
                    grad += dot_nt(d_pre, dec_w[:, cols])
                grads.append(grad)
            dec_sum[...] += dec_total
            top_total = jnp.zeros((8, C), F32)
            for k, n in enumerate(at):
                d_pre = grads[k] * slope[TOP, n].astype(F32)
                top_total += jnp.sum(d_pre.reshape(TOK // 8, 8, C), axis=0)
                spread(dpw[k], d_pre, 2, 0)
                wide = jnp.concatenate([dpw[k][32 - 16 * ky : 32 - 16 * ky + TOK] for ky in range(3)], axis=1)
                slope[TOP - 1, n] = (dot(wide, top_wt[...]) * slope[TOP - 1, n].astype(F32)).astype(BF)
            top_sum[...] += top_total
            for k in range(group):
                gathered = jnp.zeros((16, C), F32)
                for ab in range(4):
                    gathered += jnp.where(row == ab, outers[k][:, ab * C : (ab + 1) * C], 0.0)
                total = jnp.sum(jnp.sum(d_logits[k], axis=1, keepdims=True), axis=0, keepdims=True)
                misc[pl.ds(class_ids[k], 1), :] += jnp.sum(gathered, axis=0, keepdims=True)
                misc[pred_row : pred_row + 1, :] += jnp.where(lane == class_ids[k], total, 0.0)
            lhs = jnp.concatenate([x4t[k] for k in range(group)], axis=1)
            for ab in range(4):
                cols = slice(ab * C, (ab + 1) * C)
                rhs = jnp.concatenate([dpd[k, :, cols] for k in range(group)], axis=0)
                acc_dec[ab] += dot(lhs, rhs)
            lhs = jnp.concatenate([xt[TOP, n] for n in at], axis=1)
            for tap in range(9):
                rows = slice(32 - 16 * (tap // 3), 288 - 16 * (tap // 3))
                cols = slice(tap % 3 * C, (tap % 3 + 1) * C)
                rhs = jnp.concatenate([dpw[k][rows, cols] for k in range(group)], axis=0)
                acc[tap * C : (tap + 1) * C, :] += dot(lhs, rhs)
            for n in at:
                for copy in sends(base, n):
                    copy.start()
            return 0

        return run

    def clear(base):
        def one(n, _):
            for layer in range(TOP):
                xt[layer, n] = jnp.zeros((C, C), BF)
                slope[layer, n] = jnp.zeros((TOK, C), BF)
            for copy in sends(base, n):
                copy.start()
            return 0

        return one

    def wait_for(n, _):
        for copy in sends(0, n):
            copy.wait()
        return 0

    def run_chunk(c, _):
        base = c * chunk
        here = jnp.clip(count - base, 0, chunk)
        wide = here // GROUP
        pairs = (here - wide * GROUP + 1) // 2
        lax.fori_loop(wide * GROUP + 2 * pairs, chunk, clear(base), 0)
        lax.fori_loop(0, wide, forward(base, 0, GROUP), 0)
        lax.fori_loop(0, pairs, forward(base, wide * GROUP, 2), 0)
        lax.fori_loop(0, chunk, wait_for, 0)
        return 0

    if chunks == 1:
        run_chunk(0, 0)
    else:
        lax.fori_loop(0, chunks, run_chunk, 0)

    misc[pred_row + 8 : pred_row + 9, :] = jnp.sum(dec_sum[...], axis=0, keepdims=True)
    first = bias_rows(classes_all) + TOP
    misc[first : first + 1, :] = jnp.sum(top_sum[...], axis=0, keepdims=True)
    small_v[0:MISC, :] = misc[...].astype(BF)
    small_v[MISC : MISC + 9 * C, :] = acc[...].astype(BF)
    for ab in range(4):
        first = MISC + 9 * C + ab * C
        small_v[first : first + C, :] = acc_dec[ab].astype(BF)
    send_small = pltpu.make_async_copy(small_v, small, small_sem)
    send_small.start()
    image = jnp.zeros((slots, LINE), F32)
    for ab in range(4):
        prob = probs[ab, 0:slots, :]
        high = prob.astype(BF)
        low = (prob - high.astype(F32)).astype(BF)
        image += dot(high, moves[ab]) + dot(low, moves[ab])
    masks[...] = image[:, 0:PIXELS]
    send_small.wait()


def processed(slots, pair, tags, order):
    def collect(slot, count):
        order[count] = slot
        return count + tags[line_of(slot, pair), PIXELS % 128 + 1]

    count = lax.fori_loop(0, slots, collect, 0)
    order[count] = 0
    return count


def line_of(slot, pair):
    return slot // pair * 8 + slot % pair


def head(slots, classes_all, boxes, tags, lines, p2, p3, p4, p5, conv_w, conv_wt, *weights):
    chunk = min(CHUNK, slots)
    images = lines.shape[0]
    cells = p2.shape[0] + p3.shape[0] + p4.shape[0] + p5.shape[0]
    any_spec = pl.BlockSpec(memory_space=pl.ANY)
    vmem = pl.BlockSpec(memory_space=pltpu.VMEM)
    smem = pl.BlockSpec(memory_space=pltpu.SMEM)
    return pl.pallas_call(
        functools.partial(head_kernel, slots, classes_all, images),
        out_shape=(
            jax.ShapeDtypeStruct((slots, PIXELS), F32),
            jax.ShapeDtypeStruct((TOP, slots, C, C), BF),
            jax.ShapeDtypeStruct((TOP, slots, TOK, C), BF),
            jax.ShapeDtypeStruct((MISC + HEAD_ROWS, C), BF),
        ),
        in_specs=[smem, smem, vmem] + [any_spec] * 6 + [vmem] * 5,
        out_specs=[vmem] + [any_spec] * 3,
        scratch_shapes=[
            pltpu.SMEM((slots + 2,), jnp.int32),
            pltpu.VMEM((cells + WIN, C), BF),
            pltpu.VMEM((LAYERS, chunk, C, C), BF),
            pltpu.VMEM((LAYERS, chunk, TOK, C), BF),
            pltpu.VMEM((GROUP, TOK, 4 * C), BF),
            pltpu.VMEM((GROUP, TOK, 4 * C), BF),
            pltpu.VMEM((GROUP, C, 4 * C), BF),
            pltpu.VMEM((GROUP, C, C), BF),
            pltpu.VMEM((4, C, C), F32),
            pltpu.VMEM((9 * C, C), F32),
            pltpu.VMEM((MISC, C), F32),
            pltpu.VMEM((8, C), F32),
            pltpu.VMEM((8, C), F32),
            pltpu.VMEM((LAYERS, TOK, C), F32),
            pltpu.VMEM((TOK, C), F32),
            pltpu.VMEM((MISC + HEAD_ROWS, C), BF),
            pltpu.VMEM(conv_w.shape, BF),
            pltpu.VMEM((9 * C, C), BF),
            pltpu.VMEM((4, TOK, LINE), BF),
            pltpu.VMEM((4, images * 8, TOK), F32),
            pltpu.VMEM((4, slots + 8, TOK), F32),
            pltpu.SemaphoreType.DMA((4,)),
            pltpu.SemaphoreType.DMA((LAYERS + 1,)),
            pltpu.SemaphoreType.DMA((chunk, 2)),
            pltpu.SemaphoreType.DMA,
        ]
        + [pltpu.VMEM((XROWS, 3 * C), BF)] * GROUP
        + [pltpu.VMEM((DROWS, 3 * C), BF)] * GROUP,
        compiler_params=pltpu.CompilerParams(vmem_limit_bytes=60 * 2**20),
        name="head",
    )(boxes, tags, lines, p2, p3, p4, p5, conv_w, conv_wt, *weights)


def finish_kernel(
    slots,
    classes_all,
    images,
    boxes,
    tags,
    dx0,
    summed,
    g2,
    g3,
    g4,
    g5,
    conv_g,
    conv_bg,
    dec_g,
    dec_bg,
    pred_g,
    pred_bg,
    order,
    table_grad,
    sum_v,
    conv_v,
    dec_v,
    in_sem,
    conv_sem,
    out_sem,
):
    pieces = LAYERS
    size = 9 * C
    loads = []
    for k in range(pieces):
        at = pl.ds(MISC + k * size, size)
        loads.append(pltpu.make_async_copy(summed.at[at], sum_v.at[at], in_sem.at[k]))
    for k, at in enumerate((pl.ds(0, MISC), pl.ds(SUM_ROWS - DEC, DEC))):
        loads.append(pltpu.make_async_copy(summed.at[at], sum_v.at[at], in_sem.at[pieces + k]))
    for load in loads:
        load.start()
    pair = slots // images
    count = processed(slots, pair, tags, order)
    table_grad[...] = jnp.zeros_like(table_grad)
    stores = []
    for k in range(pieces):
        loads[k].wait()
        conv_v[k] = sum_v[MISC + k * size : MISC + (k + 1) * size, :].astype(F32)
        stores.append(pltpu.make_async_copy(conv_v.at[k], conv_g.at[k], conv_sem.at[k]))
        stores[-1].start()

    for load in loads[pieces:]:
        load.wait()
    for ab in range(4):
        first = SUM_ROWS - DEC + ab * C
        dec_v[:, ab * C : (ab + 1) * C] = sum_v[first : first + C, :].astype(F32)
    stores.append(pltpu.make_async_copy(dec_v, dec_g, conv_sem.at[pieces]))
    stores[-1].start()

    def scatter(n, _):
        sampler = Sampler(boxes, order[n])
        across = sampler.across(0)

        def rows_of(cells):
            def run():
                for i in range(POOL):
                    start, down = sampler.down(i)
                    weights = (across * down).astype(BF)[:, 0:cells]
                    table_grad[pl.ds(start, cells), :] += dot_tn(weights, dx0[n, i * WIDE : (i + 1) * WIDE, :])

            return run

        pl.when(sampler.level == 0)(rows_of(128))
        pl.when(sampler.level == 1)(rows_of(64))
        pl.when(sampler.level >= 2)(rows_of(32))
        return 0

    lax.fori_loop(0, count, scatter, 0)
    at = 0
    for k, part in enumerate((g2, g3, g4, g5)):
        stores.append(pltpu.make_async_copy(table_grad.at[pl.ds(at, part.shape[0])], part, out_sem.at[k]))
        stores[-1].start()
        at += part.shape[0]
    misc = sum_v[0:MISC, :].astype(F32)
    pred_row = (classes_all + 7) // 8 * 8
    bias_row = bias_rows(classes_all)
    pred_g[...] = misc[0:classes_all]
    pred_bg[...] = misc[pred_row : pred_row + 1]
    dec_bg[...] = misc[pred_row + 8 : pred_row + 9]
    conv_bg[...] = misc[bias_row : bias_row + LAYERS]
    for store in stores:
        store.wait()


def finish(slots, classes_all, images, boxes, tags, dx0, summed, levels):
    cells = sum(levels)
    any_spec = pl.BlockSpec(memory_space=pl.ANY)
    vmem = pl.BlockSpec(memory_space=pltpu.VMEM)
    smem = pl.BlockSpec(memory_space=pltpu.SMEM)
    return pl.pallas_call(
        functools.partial(finish_kernel, slots, classes_all, images),
        out_shape=(
            *(jax.ShapeDtypeStruct((level, C), F32) for level in levels),
            jax.ShapeDtypeStruct((LAYERS, 9 * C, C), F32),
            jax.ShapeDtypeStruct((LAYERS, C), F32),
            jax.ShapeDtypeStruct((C, 4 * C), F32),
            jax.ShapeDtypeStruct((1, C), F32),
            jax.ShapeDtypeStruct((classes_all, C), F32),
            jax.ShapeDtypeStruct((1, C), F32),
        ),
        in_specs=[smem, smem, vmem, any_spec],
        out_specs=[any_spec] * 5 + [vmem, any_spec, vmem, vmem, vmem],
        scratch_shapes=[
            pltpu.SMEM((slots + 2,), jnp.int32),
            pltpu.VMEM((cells + WIN, C), F32),
            pltpu.VMEM((SUM_ROWS, C), BF),
            pltpu.VMEM((LAYERS, 9 * C, C), F32),
            pltpu.VMEM((C, 4 * C), F32),
            pltpu.SemaphoreType.DMA((LAYERS + 2,)),
            pltpu.SemaphoreType.DMA((LAYERS + 1,)),
            pltpu.SemaphoreType.DMA((4,)),
        ],
        compiler_params=pltpu.CompilerParams(vmem_limit_bytes=60 * 2**20),
        name="finish",
    )(boxes, tags, dx0, summed)


def body(
    images,
    groups,
    p2,
    p3,
    p4,
    p5,
    roi_boxes,
    recv_index,
    classes,
    targets,
    conv_weights,
    conv_biases,
    deconv_weight,
    deconv_bias,
    predictor_weight,
    predictor_bias,
):
    slots = roi_boxes.shape[-1]
    classes_all = predictor_weight.shape[1]
    boxes = roi_boxes[0].transpose(1, 0, 2)
    lines, tags, conv_wt = exchange(
        images, slots // images, targets[0, 0], recv_index[0], classes[0], conv_weights
    )
    masks, xt, slope, small = head(
        slots,
        classes_all,
        boxes,
        tags,
        lines,
        p2[0, 0],
        p3[0, 0],
        p4[0, 0],
        p5[0, 0],
        conv_weights,
        conv_wt,
        conv_biases,
        deconv_weight,
        deconv_bias.reshape(2, C // 2),
        predictor_weight.T,
        predictor_bias[None, :],
    )
    total = sum_all if images == 8 and groups == 4 else sum_plain
    summed, dx0 = total(classes_all, xt, slope, conv_weights, conv_wt, small)
    levels = [p.shape[2] for p in (p2, p3, p4, p5)]
    g2, g3, g4, g5, conv_g, conv_bg, dec_g, dec_bg, pred_g, pred_bg = finish(
        slots, classes_all, images, boxes, tags, dx0, summed, levels
    )
    return (
        masks[None, None],
        g2[None, None],
        g3[None, None],
        g4[None, None],
        g5[None, None],
        conv_g,
        conv_bg,
        dec_g,
        dec_bg[0],
        pred_g.T,
        pred_bg[0, :classes_all],
    )


def solution(mesh):
    split = P("img", "grp", None, None)
    in_specs = (split,) * 5 + (P("img", "grp", None),) * 2 + (split,) + (P(),) * 6
    out_specs = (split,) * 5 + (P(),) * 6
    return jax.shard_map(
        functools.partial(body, mesh.shape["img"], mesh.shape["grp"]),
        mesh=mesh,
        in_specs=in_specs,
        out_specs=out_specs,
        check_vma=False,
    )
```

```python
import functools

import jax
import jax.numpy as jnp
from jax import lax
from jax.experimental import pallas as pl
from jax.experimental.pallas import tpu as pltpu
from jax.sharding import PartitionSpec as P

MESH = pl.DeviceIdType.MESH
POOL = 14
LAYERS = 4
MASK = 28
PIXELS = MASK * MASK
LINE = 896
C = 256
WIDE = 16
TOK = POOL * WIDE
XROWS = 272
DROWS = 288
WIN = 128
CHUNK = 16
GROUP = 4
TEAM = 2
UNIT = 512
MISC = UNIT
DEC = 4 * C
TOP = LAYERS - 1
HEAD_ROWS = 9 * C + DEC
SUM_ROWS = MISC + LAYERS * 9 * C + DEC
SUM_PARTS = tuple((units, "xy") for units in (2, 2, 2, 3, 2, 2, 3, 2, 1, 2))
SUM_GAP = 3
TAIL_GAP = 2
SUM_ENTER = 3
GA = 0.7978845608028654
GB = GA * 0.044715
BF = jnp.bfloat16
F32 = jnp.float32


def dot(a, b):
    return jnp.dot(a, b, preferred_element_type=F32)


def dot_nt(a, b):
    return lax.dot_general(a, b, (((1,), (1,)), ((), ())), preferred_element_type=F32)


def dot_tn(a, b):
    return lax.dot_general(a, b, (((0,), (0,)), ((), ())), preferred_element_type=F32)


def gelu_both(x):
    square = x * x
    gate = 0.5 + 0.5 * jnp.tanh(x * (GA + GB * square))
    value = x * gate
    slope = gate + (value - value * gate) * (2 * GA + 6 * GB * square)
    return value, slope


def exchange_kernel(
    n,
    pair,
    targets,
    picked,
    classes,
    conv_w,
    lines,
    tags,
    conv_wt,
    targets_v,
    picked_v,
    classes_v,
    lines_v,
    tags_v,
    conv_v,
    turned,
    leaving,
    send_sem,
    recv_sem,
    own_sem,
    in_sem,
    w_sem,
    out_sem,
):
    me = lax.axis_index("img")
    grp = lax.axis_index("grp")
    barrier = pltpu.get_barrier_semaphore()
    for k in range(1, n):
        pl.semaphore_signal(barrier, inc=1, device_id=(lax.rem(me + k, n), grp), device_id_type=MESH)
    loads = []
    for k, (source, target) in enumerate(((targets, targets_v), (picked, picked_v), (classes, classes_v))):
        loads.append(pltpu.make_async_copy(source, target, in_sem.at[k]))
    for layer in range(LAYERS):
        loads.append(pltpu.make_async_copy(conv_w.at[layer], conv_v.at[layer], w_sem.at[layer]))
    for load in loads:
        load.start()
    leaving[...] = jnp.zeros_like(leaving)
    for load in loads[:3]:
        load.wait()
    slots, rois = n * pair, targets.shape[0]
    chosen = (lax.broadcasted_iota(jnp.int32, (slots, rois), 0) == picked_v[...]).astype(F32)
    rows = dot(chosen.astype(BF), targets_v[...].astype(F32).astype(BF))
    label = jnp.sum(chosen * classes_v[...].astype(F32), axis=1, keepdims=True)
    flag = jnp.sum(chosen, axis=1, keepdims=True)
    lane = lax.broadcasted_iota(jnp.int32, (slots, 128), 1)
    mark = jnp.where(lane == PIXELS % 128, label, jnp.where(lane == PIXELS % 128 + 1, flag, 0.0))
    whole = PIXELS // 128 * 128
    last = jnp.concatenate([rows[:, whole:], jnp.zeros((slots, LINE - PIXELS), F32)], axis=1) + mark
    for i in range(n):
        leaving[i, 0:pair, 0:whole] = rows[i * pair : (i + 1) * pair, 0:whole]
        leaving[i, 0:pair, whole:LINE] = last[i * pair : (i + 1) * pair]
    own = pltpu.make_async_copy(leaving.at[me], lines_v.at[me], own_sem)
    own.start()
    pl.semaphore_wait(barrier, n - 1)
    copies = []
    for k in range(1, n):
        peer = lax.rem(me + k, n)
        copy = pltpu.make_async_remote_copy(
            src_ref=leaving.at[peer],
            dst_ref=lines_v.at[me],
            send_sem=send_sem.at[k - 1],
            recv_sem=recv_sem.at[k - 1],
            device_id=(peer, grp),
            device_id_type=MESH,
        )
        copy.start()
        copies.append(copy)

    def turn(layer):
        def one(tap, _):
            at = pl.ds(pl.multiple_of(tap * C, C), C)
            turned[layer, at, :] = conv_v[layer, at, :].T
            return 0

        lax.fori_loop(0, 9, one, 0)

    stores = []
    for layer in range(LAYERS):
        loads[3 + layer].wait()
        turn(layer)
        stores.append(pltpu.make_async_copy(turned.at[layer], conv_wt.at[layer], w_sem.at[layer]))
        stores[-1].start()
    own.wait()
    for copy in copies:
        copy.wait()
    for i in range(n):
        tags_v[i * 8 : (i + 1) * 8, :] = lines_v[i, :, whole:LINE].astype(jnp.int32)
    stores.append(pltpu.make_async_copy(lines_v, lines, out_sem.at[0]))
    stores.append(pltpu.make_async_copy(tags_v, tags, out_sem.at[1]))
    for store in stores[LAYERS:]:
        store.start()
    for store in stores:
        store.wait()


def exchange(n, pair, targets, picked, classes, conv_w):
    any_spec = pl.BlockSpec(memory_space=pl.ANY)
    return pl.pallas_call(
        functools.partial(exchange_kernel, n, pair),
        out_shape=(
            jax.ShapeDtypeStruct((n, 8, LINE), F32),
            jax.ShapeDtypeStruct((n * 8, 128), jnp.int32),
            jax.ShapeDtypeStruct(conv_w.shape, BF),
        ),
        in_specs=[any_spec] * 4,
        out_specs=[any_spec] * 3,
        scratch_shapes=[
            pltpu.VMEM(targets.shape, jnp.int32),
            pltpu.VMEM(picked.shape, jnp.int32),
            pltpu.VMEM(classes.shape, jnp.int32),
            pltpu.VMEM((n, 8, LINE), F32),
            pltpu.VMEM((n * 8, 128), jnp.int32),
            pltpu.VMEM(conv_w.shape, BF),
            pltpu.VMEM(conv_w.shape, BF),
            pltpu.VMEM((n, 8, LINE), F32),
            pltpu.SemaphoreType.DMA((n - 1,)),
            pltpu.SemaphoreType.DMA((n - 1,)),
            pltpu.SemaphoreType.DMA,
            pltpu.SemaphoreType.DMA((3,)),
            pltpu.SemaphoreType.DMA((LAYERS,)),
            pltpu.SemaphoreType.DMA((2,)),
        ],
        compiler_params=pltpu.CompilerParams(collective_id=0, has_side_effects=True, vmem_limit_bytes=60 * 2**20),
        name="exchange",
    )(targets, picked, classes, conv_w)


def sum_kernel(
    classes_all,
    xt,
    slope,
    conv_wt,
    small,
    out,
    d_bottom,
    xt_v,
    slope_v,
    wt_v,
    small_v,
    sums,
    leaving,
    mine,
    from_core,
    from_one,
    from_two,
    from_z,
    res,
    in_sem,
    send_sem,
    recv_sem,
    out_sem,
    bottom_sem,
    *held,
):
    img, grp = lax.axis_index("img"), lax.axis_index("grp")
    x, core = grp // 2, grp % 2
    z, y = img // 2, img % 2
    sizes = [UNIT * units for units, kind in SUM_PARTS]
    kinds = [kind for units, kind in SUM_PARTS]
    starts = [SUM_ROWS - sum(sizes[: k + 1]) for k in range(len(sizes))]
    chunks = len(sizes)
    spans = [slice(start, start + size) for start, size in zip(starts, sizes)]
    other_core = (img, x * 2 + 1 - core)
    other_x = (img, (1 - x) * 2 + core)
    other_y = (z * 2 + 1 - y, grp)
    others_z = [(lax.rem(z + k, 4) * 2 + y, grp) for k in range(1, 4)]
    lanes = C // 2
    kept_lanes = pl.ds(pl.multiple_of(core * lanes, lanes), lanes)

    barrier = pltpu.get_barrier_semaphore()
    peers = [other_core, other_x, other_y] + others_z
    for peer in peers:
        pl.semaphore_signal(barrier, inc=1, device_id=peer, device_id_type=MESH)
    load_small = pltpu.make_async_copy(small, small_v, in_sem.at[3 * TOP])
    load_slope, load_wt, load_xt = {}, {}, {}
    for layer in range(TOP):
        load_slope[layer] = pltpu.make_async_copy(slope.at[layer], slope_v.at[layer], in_sem.at[3 * layer])
        load_wt[layer] = pltpu.make_async_copy(conv_wt.at[layer], wt_v.at[layer], in_sem.at[3 * layer + 1])
        load_xt[layer] = pltpu.make_async_copy(xt.at[layer], xt_v.at[layer], in_sem.at[3 * layer + 2])

    def load_layer(layer):
        load_slope[layer].start()
        load_wt[layer].start()
        load_xt[layer].start()

    load_small.start()
    load_layer(TOP - 1)
    frames, dx = held[:GROUP], held[GROUP:]
    blocks = xt.shape[1]
    each = blocks // GROUP
    for frame in frames:
        frame[:, 0:16, :] = jnp.zeros((each, 16, 3 * C), BF)
        frame[:, 16 + TOK : DROWS, :] = jnp.zeros((each, DROWS - 16 - TOK, 3 * C), BF)
    sums[...] = jnp.zeros_like(sums)
    pl.semaphore_wait(barrier, len(peers))

    def remote(k, lane, source, target, peer):
        copy = pltpu.make_async_remote_copy(
            src_ref=source,
            dst_ref=target,
            send_sem=send_sem.at[k, lane],
            recv_sem=recv_sem.at[k, lane],
            device_id=peer,
            device_id_type=MESH,
        )
        copy.start()
        return copy

    bits, across = {"x": (x, y), "y": (y, x)}, {"x": (other_x, other_y), "y": (other_y, other_x)}

    def place(k, s, depth):
        size = sizes[k] // len(kinds[k])
        at = starts[k] + s * size
        for level in range(abs(depth)):
            size = size // 2
            bit = bits[kinds[k][s]][level]
            at = at + (1 - bit if level + 1 == -depth else bit) * size
        return at, size

    def rows_at(k, s, depth):
        at, size = place(k, s, depth)
        return pl.ds(pl.multiple_of(at, 16), size)

    def shard_at(k, s, owner):
        at, size = place(k, s, 2)
        return pl.ds(pl.multiple_of(at + owner * (size // 4), 16), size // 4)

    def landing(k, s, cut, d=0):
        size = sizes[k] // (len(kinds[k]) * cut)
        per = 3 if cut == 16 else 1
        first = starts[k] // cut * per + (per * s + d) * size
        return slice(first, first + size)

    flying = {}

    def arrived(stage, k):
        for copy in flying.pop((stage, k)):
            copy.wait()

    def put(at, value):
        low, high = value[:, :lanes], value[:, lanes:]
        first = core == 0
        mine[at, :] = jnp.where(first, low, high).astype(BF)
        leaving[at, :] = jnp.where(first, high, low).astype(BF)

    def spread(layer, k, q):
        value = slope_v[layer, k * each + q].astype(F32)
        if layer < TOP - 1:
            value = dx[k][q] * value
        frames[k][q, 16 : 16 + TOK, 0:C] = pltpu.roll(value, TOK - 1, 0).astype(BF)
        frames[k][q, 16 : 16 + TOK, C : 2 * C] = value.astype(BF)
        frames[k][q, 16 : 16 + TOK, 2 * C : 3 * C] = pltpu.roll(value, 1, 0).astype(BF)
        return jnp.sum(value.reshape(TOK // 8, 8, C), axis=0)

    def back(layer, k, q):
        wide = jnp.concatenate([frames[k][q, 32 - 16 * ky : 32 - 16 * ky + TOK] for ky in range(3)], axis=1)
        return dot(wide, wt_v[layer])

    def inputs(layer, part):
        def four(q, _):
            total = jnp.zeros((8, C), F32)
            for k in range(GROUP):
                if layer > 0:
                    total += spread(layer, k, q)
                    dx[k][q] = back(layer, k, q)
                else:
                    slope_v[0, k * each + q] = back(0, k, q).astype(BF)
            if layer > 0:
                sums[layer] += total
            return 0

        if part == 0 and layer > 0:
            load_slope[layer].wait()
        if part == 0:
            load_wt[layer].wait()
        if part == 0 and layer > 0:
            load_layer(layer - 1)
        lax.fori_loop(part * each // 2, (part + 1) * each // 2, four, 0)

    def lowest():
        load_slope[0].wait()

        def four(q, _):
            total = jnp.zeros((8, C), F32)
            for k in range(GROUP):
                total += spread(0, k, q)
            sums[0] += total
            return 0

        lax.fori_loop(0, each, four, 0)
        put(slice(0, MISC), small_v[0:MISC, :].astype(F32))
        row = lax.broadcasted_iota(jnp.int32, (16, C), 0)
        first = bias_rows(classes_all)
        biases = small_v[first : first + 16, :].astype(F32)
        for layer in range(TOP):
            biases += jnp.where(row == layer, jnp.sum(sums[layer], axis=0, keepdims=True), 0.0)
        put(slice(first, first + 16), biases)

    def weights(layer, taps):
        if taps[0] == 8:
            load_xt[layer].wait()

        def one(i, _):
            tap = taps[0] - i
            ky, kx = tap // 3, tap % 3
            rows = pl.ds(pl.multiple_of(32 - 16 * ky, 16), C)
            cols = pl.ds(pl.multiple_of(kx * C, C), C)
            lhs = jnp.concatenate([xt_v[layer, n] for n in range(blocks)], axis=1)
            rhs = jnp.concatenate([frames[n // each][n % each, rows, cols] for n in range(blocks)], axis=0)
            at = MISC + (9 * layer + tap) * C
            put(pl.ds(pl.multiple_of(at, C), C), dot(lhs, rhs))
            return 0

        lax.fori_loop(0, len(taps), one, 0)

    def stage_core(k):
        flying[0, k] = [remote(k, 0, leaving.at[spans[k]], from_core.at[spans[k]], other_core)]

    def parts(k):
        return range(len(kinds[k]))

    def stage_one(k):
        arrived(0, k)
        at = spans[k]
        mine[at, :] = (mine[at, :].astype(F32) + from_core[at, :].astype(F32)).astype(BF)
        flying[1, k] = [
            remote(k, 1 + s, mine.at[rows_at(k, s, -1)], from_one.at[landing(k, s, 2)], across[kinds[k][s]][0])
            for s in parts(k)
        ]

    def stage_two(k):
        arrived(1, k)
        copies = []
        for s in parts(k):
            at = rows_at(k, s, 1)
            mine[at, :] = (mine[at, :].astype(F32) + from_one[landing(k, s, 2), :].astype(F32)).astype(BF)
            leave = mine.at[rows_at(k, s, -2)]
            copies.append(remote(k, 3 + s, leave, from_two.at[landing(k, s, 4)], across[kinds[k][s]][1]))
        flying[2, k] = copies

    def stage_three(k):
        arrived(2, k)
        copies = []
        for s in parts(k):
            at = rows_at(k, s, 2)
            mine[at, :] = (mine[at, :].astype(F32) + from_two[landing(k, s, 4), :].astype(F32)).astype(BF)
            for d in range(3):
                leave = mine.at[shard_at(k, s, lax.rem(z + 1 + d, 4))]
                copies.append(remote(k, 5 + 3 * s + d, leave, from_z.at[landing(k, s, 16, d)], others_z[d]))
        flying[3, k] = copies

    def stage_four(k):
        arrived(3, k)
        copies = []
        for s in parts(k):
            at = shard_at(k, s, z)
            total = mine[at, :].astype(F32)
            for d in range(3):
                total += from_z[landing(k, s, 16, d), :].astype(F32)
            res[at, kept_lanes] = total.astype(BF)
            for d in range(3):
                block = res.at[at, kept_lanes]
                copies.append(remote(k, 11 + 3 * s + d, block, block, others_z[d]))
        flying[4, k] = copies

    def stage_five(k):
        arrived(4, k)
        blocks = [res.at[rows_at(k, s, 2), kept_lanes] for s in parts(k)]
        flying[5, k] = [remote(k, 17 + s, blocks[s], blocks[s], across[kinds[k][s]][1]) for s in parts(k)]

    def stage_six(k):
        arrived(5, k)
        blocks = [res.at[rows_at(k, s, 1), kept_lanes] for s in parts(k)]
        flying[6, k] = [remote(k, 19 + s, blocks[s], blocks[s], across[kinds[k][s]][0]) for s in parts(k)]

    def stage_seven(k):
        arrived(6, k)
        block = res.at[spans[k], kept_lanes]
        flying[7, k] = [remote(k, 21, block, block, other_core)]

    outs = []

    def stage_out(k):
        arrived(7, k)
        outs.append(pltpu.make_async_copy(res.at[spans[k]], out.at[spans[k]], out_sem.at[k]))
        outs[-1].start()

    stages = [stage_one, stage_two, stage_three, stage_four, stage_five, stage_six, stage_seven, stage_out]
    work = []
    for layer in reversed(range(TOP)):
        top = MISC + 9 * layer * C
        if layer > 0:
            for part in range(2):
                work.append((functools.partial(inputs, layer, part), None))
        else:
            work.append((lowest, None))
        for taps in ((8, 7), (6, 5), (4, 3), (2, 1, 0)):
            work.append((functools.partial(weights, layer, taps), top + taps[-1] * C))
    work[-1] = (work[-1][0], 0)
    for part in range(2):
        work.append((functools.partial(inputs, 0, part), None))

    load_small.wait()
    put(slice(SUM_ROWS - HEAD_ROWS, SUM_ROWS), small_v[MISC:, :].astype(F32))
    ready = SUM_ROWS - HEAD_ROWS
    due = {}
    step, first = 0, 0
    while len(outs) < chunks or step < len(work):
        gap = SUM_GAP if step < len(work) else TAIL_GAP
        for k in range(chunks):
            if k in due and due[k][1] <= step and due[k][0] < len(stages):
                stages[due[k][0]](k)
                due[k] = (due[k][0] + 1, step + gap)
        for _ in range(SUM_ENTER):
            if first == chunks or starts[first] < ready:
                break
            due[first] = (0, step + gap)
            stage_core(first)
            first += 1
        if step < len(work):
            run, now = work[step]
            run()
            ready = ready if now is None else now
            if step == len(work) - 1:
                bottom = pltpu.make_async_copy(slope_v.at[0], d_bottom, bottom_sem)
                bottom.start()
        step += 1
    bottom.wait()
    for copy in outs:
        copy.wait()


def bias_rows(classes_all):
    return (classes_all + 7) // 8 * 8 + 16


def sum_all(classes_all, xt, slope, conv_w, conv_wt, small):
    blocks = xt.shape[1]
    chunks = len(SUM_PARTS)
    any_spec = pl.BlockSpec(memory_space=pl.ANY)
    return pl.pallas_call(
        functools.partial(sum_kernel, classes_all),
        out_shape=(jax.ShapeDtypeStruct((SUM_ROWS, C), BF), jax.ShapeDtypeStruct(slope.shape[1:], BF)),
        in_specs=[any_spec] * 4,
        out_specs=[any_spec] * 2,
        scratch_shapes=[
            pltpu.VMEM(xt.shape, BF),
            pltpu.VMEM(slope.shape, BF),
            pltpu.VMEM((TOP, 9 * C, C), BF),
            pltpu.VMEM(small.shape, BF),
            pltpu.VMEM((TOP, 8, C), F32),
            pltpu.VMEM((SUM_ROWS, C // 2), BF),
            pltpu.VMEM((SUM_ROWS, C // 2), BF),
            pltpu.VMEM((SUM_ROWS, C // 2), BF),
            pltpu.VMEM((SUM_ROWS // 2, C // 2), BF),
            pltpu.VMEM((SUM_ROWS // 4, C // 2), BF),
            pltpu.VMEM((SUM_ROWS // 16 * 3, C // 2), BF),
            pltpu.VMEM((SUM_ROWS, C), BF),
            pltpu.SemaphoreType.DMA((3 * TOP + 1,)),
            pltpu.SemaphoreType.DMA((chunks, 22)),
            pltpu.SemaphoreType.DMA((chunks, 22)),
            pltpu.SemaphoreType.DMA((chunks,)),
            pltpu.SemaphoreType.DMA,
        ]
        + [pltpu.VMEM((blocks // GROUP, DROWS, 3 * C), BF)] * GROUP
        + [pltpu.VMEM((blocks // GROUP, TOK, C), F32)] * GROUP,
        compiler_params=pltpu.CompilerParams(collective_id=1, has_side_effects=True, vmem_limit_bytes=60 * 2**20),
        name="sum_all",
    )(xt, slope, conv_wt, small)


def sum_plain(classes_all, xt, slope, conv_w, conv_wt, small):
    slots = slope.shape[1]
    chunk = min(CHUNK, slots)

    def some(c, carry):
        weights, biases, bottom = carry
        grad = 1.0
        parts, sums = [], []
        for layer in reversed(range(TOP)):
            d_pre = grad * lax.dynamic_slice_in_dim(slope[layer], c * chunk, chunk).astype(F32)
            sums.insert(0, jnp.sum(d_pre, axis=(0, 1)))
            padded = jnp.pad(d_pre.astype(BF), ((0, 0), (17, 49), (0, 0)))
            held = lax.dynamic_slice_in_dim(xt[layer], c * chunk, chunk)
            grad = 0.0
            taps = []
            for tap in range(9):
                at = 17 - 16 * (tap // 3 - 1) - (tap % 3 - 1)
                moved = padded[:, at : at + C]
                taps.append(jnp.einsum("nct,ntd->cd", held, moved, preferred_element_type=F32))
                kernel = conv_w[layer, tap * C : (tap + 1) * C]
                grad += jnp.einsum("ntd,cd->ntc", moved[:, :TOK], kernel, preferred_element_type=F32)
            parts = taps + parts
        bottom = lax.dynamic_update_slice_in_dim(bottom, grad.astype(BF), c * chunk, 0)
        return weights + jnp.concatenate(parts), biases + jnp.stack(sums), bottom

    carry = (jnp.zeros((TOP * 9 * C, C), F32), jnp.zeros((TOP, C), F32), jnp.zeros(slope.shape[1:], BF))
    weights, biases, bottom = lax.fori_loop(0, slots // chunk, some, carry)
    first = bias_rows(classes_all)
    misc = small[:MISC].astype(F32).at[first : first + TOP].set(biases)
    total = jnp.concatenate([misc, weights, small[MISC:].astype(F32)])
    return lax.psum(total.astype(BF), ("img", "grp")), bottom


class Sampler:
    def __init__(self, boxes, slot):
        level = boxes[0, 0, slot]
        self.level = level
        self.y0, self.x0 = boxes[1, 0, slot], boxes[2, 0, slot]
        self.sy, self.sx = boxes[3, 0, slot], boxes[4, 0, slot]
        self.shift = 6 - level
        self.side = jnp.left_shift(1, self.shift)
        self.offset = jnp.where(level == 0, 0, jnp.where(level == 1, 4096, jnp.where(level == 2, 5120, 5376)))
        self.cell = lax.broadcasted_iota(jnp.int32, (WIDE, WIN), 1)
        self.column = (self.cell & (self.side - 1)).astype(F32)
        self.band = lax.shift_right_logical(self.cell, self.shift)

    def across(self, moved):
        j = lax.broadcasted_iota(jnp.int32, (WIDE, WIN), 0) + moved
        at = jnp.where((j >= 0) & (j < POOL), self.x0 + j * self.sx, -64).astype(F32) * 0.25
        return jnp.maximum(1.0 - jnp.abs(at - self.column), 0.0)

    def down(self, i):
        qy = self.y0 + i * self.sy
        base = self.offset + jnp.left_shift(lax.shift_right_logical(qy, 2), self.shift)
        start = pl.multiple_of(jnp.left_shift(lax.shift_right_logical(base, 4), 4), 16)
        lead = lax.shift_right_logical(base - start, self.shift)
        fraction = (qy & 3).astype(F32) * 0.25
        row = self.band - lead
        return start, jnp.where(row == 0, 1.0 - fraction, jnp.where(row == 1, fraction, 0.0))


def head_kernel(
    slots,
    classes_all,
    images,
    boxes,
    tags,
    lines,
    p2,
    p3,
    p4,
    p5,
    conv_w_h,
    conv_wt_h,
    conv_b,
    dec_w,
    dec_b,
    pred_wt,
    pred_b,
    masks,
    xt_out,
    slope_out,
    small,
    order,
    table,
    xt,
    slope,
    up,
    up_slope,
    dpd,
    x4t,
    acc_dec,
    acc,
    misc,
    dec_sum,
    top_sum,
    bias2,
    bias_d,
    small_v,
    conv_w,
    top_wt,
    moves,
    wanted,
    probs,
    in_sem,
    w_sem,
    out_sem,
    small_sem,
    *frames,
):
    chunk = min(CHUNK, slots)
    chunks = slots // chunk
    pair = slots // images
    cells = p2.shape[0] + p3.shape[0] + p4.shape[0] + p5.shape[0]
    parts = []
    at = 0
    for k, part in enumerate((p2, p3, p4, p5)):
        parts.append(pltpu.make_async_copy(part, table.at[pl.ds(at, part.shape[0])], in_sem.at[k]))
        at += part.shape[0]
    for layer in range(LAYERS):
        parts.append(pltpu.make_async_copy(conv_w_h.at[layer], conv_w.at[layer], w_sem.at[layer]))
    parts.append(pltpu.make_async_copy(conv_wt_h.at[TOP], top_wt, w_sem.at[LAYERS]))
    xw, dpw = frames[:TEAM], frames[TEAM:]
    for part in parts:
        part.start()

    count = processed(slots, pair, tags, order)
    table[cells:, :] = jnp.zeros((table.shape[0] - cells, C), BF)
    probs[...] = jnp.zeros_like(probs)
    for frame in frames:
        frame[...] = jnp.zeros_like(frame)
    dpd[...] = jnp.zeros_like(dpd)
    acc_dec[...] = jnp.zeros_like(acc_dec)
    acc[...] = jnp.zeros_like(acc)
    top_sum[...] = jnp.zeros_like(top_sum)
    misc[...] = jnp.zeros_like(misc)
    dec_sum[...] = jnp.zeros_like(dec_sum)
    col = lax.broadcasted_iota(jnp.int32, (TOK, C), 0) & (WIDE - 1)
    off_block = jnp.where(col < POOL, 0.0, -1e4)
    for layer in range(LAYERS):
        bias2[layer] = off_block + conv_b[layer : layer + 1, :].astype(F32)
    bias_d[...] = off_block + jnp.concatenate([dec_b[0:1, :], dec_b[1:2, :]], axis=1).astype(F32)
    lane_ok = (lax.broadcasted_iota(jnp.int32, (8, TOK), 1) & (WIDE - 1)) < POOL
    row_ok = lax.broadcasted_iota(jnp.int32, (8, TOK), 0) < 4
    live = (lane_ok & row_ok).astype(F32)
    token = lax.broadcasted_iota(jnp.int32, (TOK, LINE), 0)
    pixel = lax.broadcasted_iota(jnp.int32, (TOK, LINE), 1)
    inside = (token & (WIDE - 1)) < POOL
    corner = lax.shift_right_logical(token, 4) * (2 * MASK) + (token & (WIDE - 1)) * 2
    all_lines = lines[...].reshape(images * 8, LINE).astype(BF)
    for ab in range(4):
        moves[ab] = (inside & (pixel == corner + (ab // 2 * MASK + ab % 2))).astype(F32).astype(BF)
        wanted[ab] = dot_nt(all_lines, moves[ab])
    for part in parts:
        part.wait()

    def spread(ref, value, first, last):
        ref[16 : 16 + TOK, C : 2 * C] = value.astype(BF)
        ref[16 : 16 + TOK, first * C : (first + 1) * C] = pltpu.roll(value, 1, 0).astype(BF)
        ref[16 : 16 + TOK, last * C : (last + 1) * C] = pltpu.roll(value, TOK - 1, 0).astype(BF)

    def sends(base, n):
        where = pl.ds(base + n, 1)
        return (
            pltpu.make_async_copy(xt.at[0:TOP, pl.ds(n, 1)], xt_out.at[:, where], out_sem.at[n, 0]),
            pltpu.make_async_copy(slope.at[0:TOP, pl.ds(n, 1)], slope_out.at[:, where], out_sem.at[n, 1]),
        )

    pred_row = (classes_all + 7) // 8 * 8

    def forward(base, first, group):
        def run(q, _):
            at = [first + group * q + k for k in range(group)]
            for k, n in enumerate(at):
                slot = order[base + n]
                sampler = Sampler(boxes, slot)
                across = jnp.concatenate([sampler.across(-1), sampler.across(0), sampler.across(1)], axis=0)
                for i in range(POOL):
                    start, down = sampler.down(i)
                    weights = across * jnp.concatenate([down] * 3, axis=0)
                    sampled = dot(weights.astype(BF), table[pl.ds(start, WIN), :]).astype(BF)
                    for b in range(3):
                        xw[k][16 * (i + 1) : 16 * (i + 2), b * C : (b + 1) * C] = sampled[b * WIDE : (b + 1) * WIDE]
            for layer in range(LAYERS):
                for k, n in enumerate(at):
                    xt[layer, n] = xw[k][16:XROWS, C : 2 * C].T
                    wide = jnp.concatenate([xw[k][16 * ky : 16 * ky + TOK] for ky in range(3)], axis=1)
                    pre = dot(wide, conv_w[layer]) + bias2[layer]
                    value, slope_now = gelu_both(pre)
                    slope[layer, n] = slope_now.astype(BF)
                    spread(xw[k], value, 0, 2)
            for k in range(group):
                x4 = xw[k][16 : 16 + TOK, C : 2 * C]
                x4t[k] = xw[k][16:XROWS, C : 2 * C].T
                for ab in range(4):
                    pre = dot(x4, dec_w[:, ab * C : (ab + 1) * C]) + bias_d[...]
                    value, slope_now = gelu_both(pre)
                    up[k, :, ab * C : (ab + 1) * C] = value.astype(BF)
                    up_slope[k, :, ab * C : (ab + 1) * C] = slope_now.astype(BF)
            row = lax.broadcasted_iota(jnp.int32, (16, C), 0)
            lane = lax.broadcasted_iota(jnp.int32, (1, C), 1)
            class_ids = [tags[line_of(order[base + n], pair), PIXELS % 128] for n in at]
            heads, d_logits = [], []
            for k, n in enumerate(at):
                picks = (lax.broadcasted_iota(jnp.int32, (16, classes_all), 1) == class_ids[k]).astype(F32)
                bias = jnp.sum(picks[0:1] * pred_b[...].astype(F32), axis=1, keepdims=True)
                weight = dot(picks.astype(BF), pred_wt[...])
                blocks = jnp.concatenate([jnp.where(row == ab, weight, 0.0) for ab in range(4)], axis=1).astype(BF)
                heads.append((blocks, bias))
            for k, n in enumerate(at):
                blocks, bias = heads[k]
                index = base + n
                valid = (index < count).astype(F32)
                slot = jnp.where(index < count, order[index], slots)
                line = line_of(order[index], pair)
                logit = dot_nt(blocks, up[k])[0:8] + bias
                prob = 1.0 / (1.0 + jnp.exp(-logit))
                rows = []
                for ab in range(4):
                    probs[ab, pl.ds(slot, 1), :] = prob[ab : ab + 1]
                    rows.append(wanted[ab, pl.ds(line, 1), :])
                target = jnp.concatenate(rows + [jnp.zeros((4, TOK), F32)], axis=0)
                d_logit = ((prob - target) * (valid / (MASK * MASK)) * live).astype(BF)
                d_logits.append(d_logit.astype(F32))
            sixteens = [jnp.concatenate([d, jnp.zeros((8, TOK), F32)], axis=0).astype(BF) for d in d_logits]
            outers = [dot(sixteens[k], up[k]) for k in range(group)]
            dec_total = jnp.zeros((8, C), F32)
            grads = []
            for k in range(group):
                grad = jnp.zeros((TOK, C), F32)
                for ab in range(4):
                    cols = slice(ab * C, (ab + 1) * C)
                    d_up = dot_tn(sixteens[k], heads[k][0][:, cols])
                    d_pre = d_up * up_slope[k, :, cols].astype(F32)
                    dec_total += jnp.sum(d_pre.reshape(TOK // 8, 8, C), axis=0)
                    d_pre = d_pre.astype(BF)
                    dpd[k, 0:TOK, cols] = d_pre
                    grad += dot_nt(d_pre, dec_w[:, cols])
                grads.append(grad)
            dec_sum[...] += dec_total
            top_total = jnp.zeros((8, C), F32)
            for k, n in enumerate(at):
                d_pre = grads[k] * slope[TOP, n].astype(F32)
                top_total += jnp.sum(d_pre.reshape(TOK // 8, 8, C), axis=0)
                spread(dpw[k], d_pre, 2, 0)
                wide = jnp.concatenate([dpw[k][32 - 16 * ky : 32 - 16 * ky + TOK] for ky in range(3)], axis=1)
                slope[TOP - 1, n] = (dot(wide, top_wt[...]) * slope[TOP - 1, n].astype(F32)).astype(BF)
            top_sum[...] += top_total
            for k in range(group):
                gathered = jnp.zeros((16, C), F32)
                for ab in range(4):
                    gathered += jnp.where(row == ab, outers[k][:, ab * C : (ab + 1) * C], 0.0)
                total = jnp.sum(jnp.sum(d_logits[k], axis=1, keepdims=True), axis=0, keepdims=True)
                misc[pl.ds(class_ids[k], 1), :] += jnp.sum(gathered, axis=0, keepdims=True)
                misc[pred_row : pred_row + 1, :] += jnp.where(lane == class_ids[k], total, 0.0)
            lhs = jnp.concatenate([x4t[k] for k in range(group)], axis=1)
            for ab in range(4):
                cols = slice(ab * C, (ab + 1) * C)
                rhs = jnp.concatenate([dpd[k, :, cols] for k in range(group)], axis=0)
                acc_dec[ab] += dot(lhs, rhs)
            lhs = jnp.concatenate([xt[TOP, n] for n in at], axis=1)
            for tap in range(9):
                rows = slice(32 - 16 * (tap // 3), 288 - 16 * (tap // 3))
                cols = slice(tap % 3 * C, (tap % 3 + 1) * C)
                rhs = jnp.concatenate([dpw[k][rows, cols] for k in range(group)], axis=0)
                acc[tap * C : (tap + 1) * C, :] += dot(lhs, rhs)
            for n in at:
                for copy in sends(base, n):
                    copy.start()
            return 0

        return run

    def clear(base):
        def one(n, _):
            for layer in range(TOP):
                xt[layer, n] = jnp.zeros((C, C), BF)
                slope[layer, n] = jnp.zeros((TOK, C), BF)
            for copy in sends(base, n):
                copy.start()
            return 0

        return one

    def wait_for(n, _):
        for copy in sends(0, n):
            copy.wait()
        return 0

    def run_chunk(c, _):
        base = c * chunk
        here = jnp.clip(count - base, 0, chunk)
        steps = (here + TEAM - 1) // TEAM
        lax.fori_loop(steps * TEAM, chunk, clear(base), 0)
        lax.fori_loop(0, steps, forward(base, 0, TEAM), 0)
        lax.fori_loop(0, chunk, wait_for, 0)
        return 0

    if chunks == 1:
        run_chunk(0, 0)
    else:
        lax.fori_loop(0, chunks, run_chunk, 0)

    misc[pred_row + 8 : pred_row + 9, :] = jnp.sum(dec_sum[...], axis=0, keepdims=True)
    first = bias_rows(classes_all) + TOP
    misc[first : first + 1, :] = jnp.sum(top_sum[...], axis=0, keepdims=True)
    small_v[0:MISC, :] = misc[...].astype(BF)
    small_v[MISC : MISC + 9 * C, :] = acc[...].astype(BF)
    for ab in range(4):
        first = MISC + 9 * C + ab * C
        small_v[first : first + C, :] = acc_dec[ab].astype(BF)
    send_small = pltpu.make_async_copy(small_v, small, small_sem)
    send_small.start()
    image = jnp.zeros((slots, LINE), F32)
    for ab in range(4):
        prob = probs[ab, 0:slots, :]
        high = prob.astype(BF)
        low = (prob - high.astype(F32)).astype(BF)
        image += dot(high, moves[ab]) + dot(low, moves[ab])
    masks[...] = image[:, 0:PIXELS]
    send_small.wait()


def processed(slots, pair, tags, order):
    def collect(slot, count):
        order[count] = slot
        return count + tags[line_of(slot, pair), PIXELS % 128 + 1]

    count = lax.fori_loop(0, slots, collect, 0)
    order[count] = 0
    return count


def line_of(slot, pair):
    return slot // pair * 8 + slot % pair


def head(slots, classes_all, boxes, tags, lines, p2, p3, p4, p5, conv_w, conv_wt, *weights):
    chunk = min(CHUNK, slots)
    images = lines.shape[0]
    cells = p2.shape[0] + p3.shape[0] + p4.shape[0] + p5.shape[0]
    any_spec = pl.BlockSpec(memory_space=pl.ANY)
    vmem = pl.BlockSpec(memory_space=pltpu.VMEM)
    smem = pl.BlockSpec(memory_space=pltpu.SMEM)
    return pl.pallas_call(
        functools.partial(head_kernel, slots, classes_all, images),
        out_shape=(
            jax.ShapeDtypeStruct((slots, PIXELS), F32),
            jax.ShapeDtypeStruct((TOP, slots, C, C), BF),
            jax.ShapeDtypeStruct((TOP, slots, TOK, C), BF),
            jax.ShapeDtypeStruct((MISC + HEAD_ROWS, C), BF),
        ),
        in_specs=[smem, smem, vmem] + [any_spec] * 6 + [vmem] * 5,
        out_specs=[vmem] + [any_spec] * 3,
        scratch_shapes=[
            pltpu.SMEM((slots + 2,), jnp.int32),
            pltpu.VMEM((cells + WIN, C), BF),
            pltpu.VMEM((LAYERS, chunk, C, C), BF),
            pltpu.VMEM((LAYERS, chunk, TOK, C), BF),
            pltpu.VMEM((TEAM, TOK, 4 * C), BF),
            pltpu.VMEM((TEAM, TOK, 4 * C), BF),
            pltpu.VMEM((TEAM, C, 4 * C), BF),
            pltpu.VMEM((TEAM, C, C), BF),
            pltpu.VMEM((4, C, C), F32),
            pltpu.VMEM((9 * C, C), F32),
            pltpu.VMEM((MISC, C), F32),
            pltpu.VMEM((8, C), F32),
            pltpu.VMEM((8, C), F32),
            pltpu.VMEM((LAYERS, TOK, C), F32),
            pltpu.VMEM((TOK, C), F32),
            pltpu.VMEM((MISC + HEAD_ROWS, C), BF),
            pltpu.VMEM(conv_w.shape, BF),
            pltpu.VMEM((9 * C, C), BF),
            pltpu.VMEM((4, TOK, LINE), BF),
            pltpu.VMEM((4, images * 8, TOK), F32),
            pltpu.VMEM((4, slots + 8, TOK), F32),
            pltpu.SemaphoreType.DMA((4,)),
            pltpu.SemaphoreType.DMA((LAYERS + 1,)),
            pltpu.SemaphoreType.DMA((chunk, 2)),
            pltpu.SemaphoreType.DMA,
        ]
        + [pltpu.VMEM((XROWS, 3 * C), BF)] * TEAM
        + [pltpu.VMEM((DROWS, 3 * C), BF)] * TEAM,
        compiler_params=pltpu.CompilerParams(vmem_limit_bytes=60 * 2**20),
        name="head",
    )(boxes, tags, lines, p2, p3, p4, p5, conv_w, conv_wt, *weights)


def finish_kernel(
    slots,
    classes_all,
    images,
    boxes,
    tags,
    dx0,
    summed,
    g2,
    g3,
    g4,
    g5,
    conv_g,
    conv_bg,
    dec_g,
    dec_bg,
    pred_g,
    pred_bg,
    order,
    table_grad,
    sum_v,
    conv_v,
    dec_v,
    in_sem,
    conv_sem,
    out_sem,
):
    pieces = LAYERS
    size = 9 * C
    loads = []
    for k in range(pieces):
        at = pl.ds(MISC + k * size, size)
        loads.append(pltpu.make_async_copy(summed.at[at], sum_v.at[at], in_sem.at[k]))
    for k, at in enumerate((pl.ds(0, MISC), pl.ds(SUM_ROWS - DEC, DEC))):
        loads.append(pltpu.make_async_copy(summed.at[at], sum_v.at[at], in_sem.at[pieces + k]))
    for load in loads:
        load.start()
    pair = slots // images
    count = processed(slots, pair, tags, order)
    table_grad[...] = jnp.zeros_like(table_grad)
    stores = []
    for k in range(pieces):
        loads[k].wait()
        conv_v[k] = sum_v[MISC + k * size : MISC + (k + 1) * size, :].astype(F32)
        stores.append(pltpu.make_async_copy(conv_v.at[k], conv_g.at[k], conv_sem.at[k]))
        stores[-1].start()

    for load in loads[pieces:]:
        load.wait()
    for ab in range(4):
        first = SUM_ROWS - DEC + ab * C
        dec_v[:, ab * C : (ab + 1) * C] = sum_v[first : first + C, :].astype(F32)
    stores.append(pltpu.make_async_copy(dec_v, dec_g, conv_sem.at[pieces]))
    stores[-1].start()

    def scatter(n, _):
        sampler = Sampler(boxes, order[n])
        across = sampler.across(0)

        def rows_of(cells):
            def run():
                for i in range(POOL):
                    start, down = sampler.down(i)
                    weights = (across * down).astype(BF)[:, 0:cells]
                    table_grad[pl.ds(start, cells), :] += dot_tn(weights, dx0[n, i * WIDE : (i + 1) * WIDE, :])

            return run

        pl.when(sampler.level == 0)(rows_of(128))
        pl.when(sampler.level == 1)(rows_of(64))
        pl.when(sampler.level >= 2)(rows_of(32))
        return 0

    lax.fori_loop(0, count, scatter, 0)
    at = 0
    for k, part in enumerate((g2, g3, g4, g5)):
        stores.append(pltpu.make_async_copy(table_grad.at[pl.ds(at, part.shape[0])], part, out_sem.at[k]))
        stores[-1].start()
        at += part.shape[0]
    misc = sum_v[0:MISC, :].astype(F32)
    pred_row = (classes_all + 7) // 8 * 8
    bias_row = bias_rows(classes_all)
    pred_g[...] = misc[0:classes_all]
    pred_bg[...] = misc[pred_row : pred_row + 1]
    dec_bg[...] = misc[pred_row + 8 : pred_row + 9]
    conv_bg[...] = misc[bias_row : bias_row + LAYERS]
    for store in stores:
        store.wait()


def finish(slots, classes_all, images, boxes, tags, dx0, summed, levels):
    cells = sum(levels)
    any_spec = pl.BlockSpec(memory_space=pl.ANY)
    vmem = pl.BlockSpec(memory_space=pltpu.VMEM)
    smem = pl.BlockSpec(memory_space=pltpu.SMEM)
    return pl.pallas_call(
        functools.partial(finish_kernel, slots, classes_all, images),
        out_shape=(
            *(jax.ShapeDtypeStruct((level, C), F32) for level in levels),
            jax.ShapeDtypeStruct((LAYERS, 9 * C, C), F32),
            jax.ShapeDtypeStruct((LAYERS, C), F32),
            jax.ShapeDtypeStruct((C, 4 * C), F32),
            jax.ShapeDtypeStruct((1, C), F32),
            jax.ShapeDtypeStruct((classes_all, C), F32),
            jax.ShapeDtypeStruct((1, C), F32),
        ),
        in_specs=[smem, smem, vmem, any_spec],
        out_specs=[any_spec] * 5 + [vmem, any_spec, vmem, vmem, vmem],
        scratch_shapes=[
            pltpu.SMEM((slots + 2,), jnp.int32),
            pltpu.VMEM((cells + WIN, C), F32),
            pltpu.VMEM((SUM_ROWS, C), BF),
            pltpu.VMEM((LAYERS, 9 * C, C), F32),
            pltpu.VMEM((C, 4 * C), F32),
            pltpu.SemaphoreType.DMA((LAYERS + 2,)),
            pltpu.SemaphoreType.DMA((LAYERS + 1,)),
            pltpu.SemaphoreType.DMA((4,)),
        ],
        compiler_params=pltpu.CompilerParams(vmem_limit_bytes=60 * 2**20),
        name="finish",
    )(boxes, tags, dx0, summed)


def body(
    images,
    groups,
    p2,
    p3,
    p4,
    p5,
    roi_boxes,
    recv_index,
    classes,
    targets,
    conv_weights,
    conv_biases,
    deconv_weight,
    deconv_bias,
    predictor_weight,
    predictor_bias,
):
    slots = roi_boxes.shape[-1]
    classes_all = predictor_weight.shape[1]
    boxes = roi_boxes[0].transpose(1, 0, 2)
    lines, tags, conv_wt = exchange(
        images, slots // images, targets[0, 0], recv_index[0], classes[0], conv_weights
    )
    masks, xt, slope, small = head(
        slots,
        classes_all,
        boxes,
        tags,
        lines,
        p2[0, 0],
        p3[0, 0],
        p4[0, 0],
        p5[0, 0],
        conv_weights,
        conv_wt,
        conv_biases,
        deconv_weight,
        deconv_bias.reshape(2, C // 2),
        predictor_weight.T,
        predictor_bias[None, :],
    )
    total = sum_all if images == 8 and groups == 4 else sum_plain
    summed, dx0 = total(classes_all, xt, slope, conv_weights, conv_wt, small)
    levels = [p.shape[2] for p in (p2, p3, p4, p5)]
    g2, g3, g4, g5, conv_g, conv_bg, dec_g, dec_bg, pred_g, pred_bg = finish(
        slots, classes_all, images, boxes, tags, dx0, summed, levels
    )
    return (
        masks[None, None],
        g2[None, None],
        g3[None, None],
        g4[None, None],
        g5[None, None],
        conv_g,
        conv_bg,
        dec_g,
        dec_bg[0],
        pred_g.T,
        pred_bg[0, :classes_all],
    )


def solution(mesh):
    split = P("img", "grp", None, None)
    in_specs = (split,) * 5 + (P("img", "grp", None),) * 2 + (split,) + (P(),) * 6
    out_specs = (split,) * 5 + (P(),) * 6
    return jax.shard_map(
        functools.partial(body, mesh.shape["img"], mesh.shape["grp"]),
        mesh=mesh,
        in_specs=in_specs,
        out_specs=out_specs,
        check_vma=False,
    )
```

```python
import functools

import jax
import jax.numpy as jnp
from jax import lax
from jax.experimental import pallas as pl
from jax.experimental.pallas import tpu as pltpu
from jax.sharding import PartitionSpec as P

MESH = pl.DeviceIdType.MESH
POOL = 14
LAYERS = 4
MASK = 28
PIXELS = MASK * MASK
LINE = 896
C = 256
WIDE = 16
TOK = POOL * WIDE
XROWS = 272
DROWS = 288
WIN = 128
CHUNK = 16
GROUP = 4
TEAM = 2
UNIT = 512
MISC = UNIT
DEC = 4 * C
TOP = LAYERS - 1
HEAD_ROWS = 9 * C + DEC
SUM_ROWS = MISC + LAYERS * 9 * C + DEC
SUM_PARTS = tuple((units, "xy") for units in (2, 2, 2, 3, 2, 2, 3, 2, 1, 2))
SUM_GAP = 3
TAIL_GAP = 2
SUM_ENTER = 3
GA = 0.7978845608028654
GB = GA * 0.044715
BF = jnp.bfloat16
F32 = jnp.float32


def dot(a, b):
    return jnp.dot(a, b, preferred_element_type=F32)


def dot_nt(a, b):
    return lax.dot_general(a, b, (((1,), (1,)), ((), ())), preferred_element_type=F32)


def dot_tn(a, b):
    return lax.dot_general(a, b, (((0,), (0,)), ((), ())), preferred_element_type=F32)


def gelu_both(x):
    square = x * x
    gate = 0.5 + 0.5 * jnp.tanh(x * (GA + GB * square))
    value = x * gate
    slope = gate + (value - value * gate) * (2 * GA + 6 * GB * square)
    return value, slope


def exchange_kernel(
    n,
    pair,
    targets,
    picked,
    classes,
    conv_w,
    lines,
    tags,
    conv_wt,
    targets_v,
    picked_v,
    classes_v,
    lines_v,
    tags_v,
    conv_v,
    turned,
    leaving,
    send_sem,
    recv_sem,
    own_sem,
    in_sem,
    w_sem,
    out_sem,
):
    me = lax.axis_index("img")
    grp = lax.axis_index("grp")
    barrier = pltpu.get_barrier_semaphore()
    for k in range(1, n):
        pl.semaphore_signal(barrier, inc=1, device_id=(lax.rem(me + k, n), grp), device_id_type=MESH)
    loads = []
    for k, (source, target) in enumerate(((targets, targets_v), (picked, picked_v), (classes, classes_v))):
        loads.append(pltpu.make_async_copy(source, target, in_sem.at[k]))
    for layer in range(LAYERS):
        loads.append(pltpu.make_async_copy(conv_w.at[layer], conv_v.at[layer], w_sem.at[layer]))
    for load in loads:
        load.start()
    leaving[...] = jnp.zeros_like(leaving)
    for load in loads[:3]:
        load.wait()
    slots, rois = n * pair, targets.shape[0]
    chosen = (lax.broadcasted_iota(jnp.int32, (slots, rois), 0) == picked_v[...]).astype(F32)
    rows = dot(chosen.astype(BF), targets_v[...].astype(F32).astype(BF))
    label = jnp.sum(chosen * classes_v[...].astype(F32), axis=1, keepdims=True)
    flag = jnp.sum(chosen, axis=1, keepdims=True)
    lane = lax.broadcasted_iota(jnp.int32, (slots, 128), 1)
    mark = jnp.where(lane == PIXELS % 128, label, jnp.where(lane == PIXELS % 128 + 1, flag, 0.0))
    whole = PIXELS // 128 * 128
    last = jnp.concatenate([rows[:, whole:], jnp.zeros((slots, LINE - PIXELS), F32)], axis=1) + mark
    for i in range(n):
        leaving[i, 0:pair, 0:whole] = rows[i * pair : (i + 1) * pair, 0:whole]
        leaving[i, 0:pair, whole:LINE] = last[i * pair : (i + 1) * pair]
    own = pltpu.make_async_copy(leaving.at[me], lines_v.at[me], own_sem)
    own.start()
    pl.semaphore_wait(barrier, n - 1)
    copies = []
    for k in range(1, n):
        peer = lax.rem(me + k, n)
        copy = pltpu.make_async_remote_copy(
            src_ref=leaving.at[peer],
            dst_ref=lines_v.at[me],
            send_sem=send_sem.at[k - 1],
            recv_sem=recv_sem.at[k - 1],
            device_id=(peer, grp),
            device_id_type=MESH,
        )
        copy.start()
        copies.append(copy)

    def turn(layer):
        def one(tap, _):
            at = pl.ds(pl.multiple_of(tap * C, C), C)
            turned[layer, at, :] = conv_v[layer, at, :].T
            return 0

        lax.fori_loop(0, 9, one, 0)

    stores = []
    for layer in range(LAYERS):
        loads[3 + layer].wait()
        turn(layer)
        stores.append(pltpu.make_async_copy(turned.at[layer], conv_wt.at[layer], w_sem.at[layer]))
        stores[-1].start()
    own.wait()
    for copy in copies:
        copy.wait()
    for i in range(n):
        tags_v[i * 8 : (i + 1) * 8, :] = lines_v[i, :, whole:LINE].astype(jnp.int32)
    stores.append(pltpu.make_async_copy(lines_v, lines, out_sem.at[0]))
    stores.append(pltpu.make_async_copy(tags_v, tags, out_sem.at[1]))
    for store in stores[LAYERS:]:
        store.start()
    for store in stores:
        store.wait()


def exchange(n, pair, targets, picked, classes, conv_w):
    any_spec = pl.BlockSpec(memory_space=pl.ANY)
    return pl.pallas_call(
        functools.partial(exchange_kernel, n, pair),
        out_shape=(
            jax.ShapeDtypeStruct((n, 8, LINE), F32),
            jax.ShapeDtypeStruct((n * 8, 128), jnp.int32),
            jax.ShapeDtypeStruct(conv_w.shape, BF),
        ),
        in_specs=[any_spec] * 4,
        out_specs=[any_spec] * 3,
        scratch_shapes=[
            pltpu.VMEM(targets.shape, jnp.int32),
            pltpu.VMEM(picked.shape, jnp.int32),
            pltpu.VMEM(classes.shape, jnp.int32),
            pltpu.VMEM((n, 8, LINE), F32),
            pltpu.VMEM((n * 8, 128), jnp.int32),
            pltpu.VMEM(conv_w.shape, BF),
            pltpu.VMEM(conv_w.shape, BF),
            pltpu.VMEM((n, 8, LINE), F32),
            pltpu.SemaphoreType.DMA((n - 1,)),
            pltpu.SemaphoreType.DMA((n - 1,)),
            pltpu.SemaphoreType.DMA,
            pltpu.SemaphoreType.DMA((3,)),
            pltpu.SemaphoreType.DMA((LAYERS,)),
            pltpu.SemaphoreType.DMA((2,)),
        ],
        compiler_params=pltpu.CompilerParams(collective_id=0, has_side_effects=True, vmem_limit_bytes=60 * 2**20),
        name="exchange",
    )(targets, picked, classes, conv_w)


def sum_kernel(
    classes_all,
    xt,
    slope,
    conv_wt,
    small,
    out,
    d_bottom,
    xt_v,
    slope_v,
    wt_v,
    small_v,
    sums,
    leaving,
    mine,
    from_core,
    from_one,
    from_two,
    from_z,
    res,
    in_sem,
    send_sem,
    recv_sem,
    out_sem,
    bottom_sem,
    *held,
):
    img, grp = lax.axis_index("img"), lax.axis_index("grp")
    x, core = grp // 2, grp % 2
    z, y = img // 2, img % 2
    sizes = [UNIT * units for units, kind in SUM_PARTS]
    kinds = [kind for units, kind in SUM_PARTS]
    starts = [SUM_ROWS - sum(sizes[: k + 1]) for k in range(len(sizes))]
    chunks = len(sizes)
    spans = [slice(start, start + size) for start, size in zip(starts, sizes)]
    other_core = (img, x * 2 + 1 - core)
    other_x = (img, (1 - x) * 2 + core)
    other_y = (z * 2 + 1 - y, grp)
    others_z = [(lax.rem(z + k, 4) * 2 + y, grp) for k in range(1, 4)]
    lanes = C // 2
    kept_lanes = pl.ds(pl.multiple_of(core * lanes, lanes), lanes)

    barrier = pltpu.get_barrier_semaphore()
    peers = [other_core, other_x, other_y] + others_z
    for peer in peers:
        pl.semaphore_signal(barrier, inc=1, device_id=peer, device_id_type=MESH)
    load_small = pltpu.make_async_copy(small, small_v, in_sem.at[3 * TOP])
    load_slope, load_wt, load_xt = {}, {}, {}
    for layer in range(TOP):
        load_slope[layer] = pltpu.make_async_copy(slope.at[layer], slope_v.at[layer], in_sem.at[3 * layer])
        load_wt[layer] = pltpu.make_async_copy(conv_wt.at[layer], wt_v.at[layer], in_sem.at[3 * layer + 1])
        load_xt[layer] = pltpu.make_async_copy(xt.at[layer], xt_v.at[layer], in_sem.at[3 * layer + 2])

    def load_layer(layer):
        load_slope[layer].start()
        load_wt[layer].start()
        load_xt[layer].start()

    load_small.start()
    load_layer(TOP - 1)
    frames, dx = held[:GROUP], held[GROUP:]
    blocks = xt.shape[1]
    each = blocks // GROUP
    for frame in frames:
        frame[:, 0:16, :] = jnp.zeros((each, 16, 3 * C), BF)
        frame[:, 16 + TOK : DROWS, :] = jnp.zeros((each, DROWS - 16 - TOK, 3 * C), BF)
    sums[...] = jnp.zeros_like(sums)
    pl.semaphore_wait(barrier, len(peers))

    def remote(k, lane, source, target, peer):
        copy = pltpu.make_async_remote_copy(
            src_ref=source,
            dst_ref=target,
            send_sem=send_sem.at[k, lane],
            recv_sem=recv_sem.at[k, lane],
            device_id=peer,
            device_id_type=MESH,
        )
        copy.start()
        return copy

    bits, across = {"x": (x, y), "y": (y, x)}, {"x": (other_x, other_y), "y": (other_y, other_x)}

    def place(k, s, depth):
        size = sizes[k] // len(kinds[k])
        at = starts[k] + s * size
        for level in range(abs(depth)):
            size = size // 2
            bit = bits[kinds[k][s]][level]
            at = at + (1 - bit if level + 1 == -depth else bit) * size
        return at, size

    def rows_at(k, s, depth):
        at, size = place(k, s, depth)
        return pl.ds(pl.multiple_of(at, 16), size)

    def shard_at(k, s, owner):
        at, size = place(k, s, 2)
        return pl.ds(pl.multiple_of(at + owner * (size // 4), 16), size // 4)

    def landing(k, s, cut, d=0):
        size = sizes[k] // (len(kinds[k]) * cut)
        per = 3 if cut == 16 else 1
        first = starts[k] // cut * per + (per * s + d) * size
        return slice(first, first + size)

    flying = {}

    def arrived(stage, k):
        for copy in flying.pop((stage, k)):
            copy.wait()

    def put(at, value):
        low, high = value[:, :lanes], value[:, lanes:]
        first = core == 0
        mine[at, :] = jnp.where(first, low, high).astype(BF)
        leaving[at, :] = jnp.where(first, high, low).astype(BF)

    def spread(layer, k, q):
        value = slope_v[layer, k * each + q].astype(F32)
        if layer < TOP - 1:
            value = dx[k][q] * value
        frames[k][q, 16 : 16 + TOK, 0:C] = pltpu.roll(value, TOK - 1, 0).astype(BF)
        frames[k][q, 16 : 16 + TOK, C : 2 * C] = value.astype(BF)
        frames[k][q, 16 : 16 + TOK, 2 * C : 3 * C] = pltpu.roll(value, 1, 0).astype(BF)
        return jnp.sum(value.reshape(TOK // 8, 8, C), axis=0)

    def back(layer, k, q):
        wide = jnp.concatenate([frames[k][q, 32 - 16 * ky : 32 - 16 * ky + TOK] for ky in range(3)], axis=1)
        return dot(wide, wt_v[layer])

    def inputs(layer, part):
        def four(q, _):
            total = jnp.zeros((8, C), F32)
            for k in range(GROUP):
                if layer > 0:
                    total += spread(layer, k, q)
                    dx[k][q] = back(layer, k, q)
                else:
                    slope_v[0, k * each + q] = back(0, k, q).astype(BF)
            if layer > 0:
                sums[layer] += total
            return 0

        if part == 0 and layer > 0:
            load_slope[layer].wait()
        if part == 0:
            load_wt[layer].wait()
        if part == 0 and layer > 0:
            load_layer(layer - 1)
        lax.fori_loop(part * each // 2, (part + 1) * each // 2, four, 0)

    def lowest():
        load_slope[0].wait()

        def four(q, _):
            total = jnp.zeros((8, C), F32)
            for k in range(GROUP):
                total += spread(0, k, q)
            sums[0] += total
            return 0

        lax.fori_loop(0, each, four, 0)
        put(slice(0, MISC), small_v[0:MISC, :].astype(F32))
        row = lax.broadcasted_iota(jnp.int32, (16, C), 0)
        first = bias_rows(classes_all)
        biases = small_v[first : first + 16, :].astype(F32)
        for layer in range(TOP):
            biases += jnp.where(row == layer, jnp.sum(sums[layer], axis=0, keepdims=True), 0.0)
        put(slice(first, first + 16), biases)

    def weights(layer, taps):
        if taps[0] == 8:
            load_xt[layer].wait()

        def one(i, _):
            tap = taps[0] - i
            ky, kx = tap // 3, tap % 3
            rows = pl.ds(pl.multiple_of(32 - 16 * ky, 16), C)
            cols = pl.ds(pl.multiple_of(kx * C, C), C)
            lhs = jnp.concatenate([xt_v[layer, n] for n in range(blocks)], axis=1)
            rhs = jnp.concatenate([frames[n // each][n % each, rows, cols] for n in range(blocks)], axis=0)
            at = MISC + (9 * layer + tap) * C
            put(pl.ds(pl.multiple_of(at, C), C), dot(lhs, rhs))
            return 0

        lax.fori_loop(0, len(taps), one, 0)

    def stage_core(k):
        flying[0, k] = [remote(k, 0, leaving.at[spans[k]], from_core.at[spans[k]], other_core)]

    def parts(k):
        return range(len(kinds[k]))

    def stage_one(k):
        arrived(0, k)
        at = spans[k]
        mine[at, :] = (mine[at, :].astype(F32) + from_core[at, :].astype(F32)).astype(BF)
        flying[1, k] = [
            remote(k, 1 + s, mine.at[rows_at(k, s, -1)], from_one.at[landing(k, s, 2)], across[kinds[k][s]][0])
            for s in parts(k)
        ]

    def stage_two(k):
        arrived(1, k)
        copies = []
        for s in parts(k):
            at = rows_at(k, s, 1)
            mine[at, :] = (mine[at, :].astype(F32) + from_one[landing(k, s, 2), :].astype(F32)).astype(BF)
            leave = mine.at[rows_at(k, s, -2)]
            copies.append(remote(k, 3 + s, leave, from_two.at[landing(k, s, 4)], across[kinds[k][s]][1]))
        flying[2, k] = copies

    def stage_three(k):
        arrived(2, k)
        copies = []
        for s in parts(k):
            at = rows_at(k, s, 2)
            mine[at, :] = (mine[at, :].astype(F32) + from_two[landing(k, s, 4), :].astype(F32)).astype(BF)
            for d in range(3):
                leave = mine.at[shard_at(k, s, lax.rem(z + 1 + d, 4))]
                copies.append(remote(k, 5 + 3 * s + d, leave, from_z.at[landing(k, s, 16, d)], others_z[d]))
        flying[3, k] = copies

    def stage_four(k):
        arrived(3, k)
        copies = []
        for s in parts(k):
            at = shard_at(k, s, z)
            total = mine[at, :].astype(F32)
            for d in range(3):
                total += from_z[landing(k, s, 16, d), :].astype(F32)
            res[at, kept_lanes] = total.astype(BF)
            for d in range(3):
                block = res.at[at, kept_lanes]
                copies.append(remote(k, 11 + 3 * s + d, block, block, others_z[d]))
        flying[4, k] = copies

    def stage_five(k):
        arrived(4, k)
        blocks = [res.at[rows_at(k, s, 2), kept_lanes] for s in parts(k)]
        flying[5, k] = [remote(k, 17 + s, blocks[s], blocks[s], across[kinds[k][s]][1]) for s in parts(k)]

    def stage_six(k):
        arrived(5, k)
        blocks = [res.at[rows_at(k, s, 1), kept_lanes] for s in parts(k)]
        flying[6, k] = [remote(k, 19 + s, blocks[s], blocks[s], across[kinds[k][s]][0]) for s in parts(k)]

    def stage_seven(k):
        arrived(6, k)
        block = res.at[spans[k], kept_lanes]
        flying[7, k] = [remote(k, 21, block, block, other_core)]

    outs = []

    def stage_out(k):
        arrived(7, k)
        outs.append(pltpu.make_async_copy(res.at[spans[k]], out.at[spans[k]], out_sem.at[k]))
        outs[-1].start()

    stages = [stage_one, stage_two, stage_three, stage_four, stage_five, stage_six, stage_seven, stage_out]
    work = []
    for layer in reversed(range(TOP)):
        top = MISC + 9 * layer * C
        if layer > 0:
            for part in range(2):
                work.append((functools.partial(inputs, layer, part), None))
        else:
            work.append((lowest, None))
        for taps in ((8, 7), (6, 5), (4, 3), (2, 1, 0)):
            work.append((functools.partial(weights, layer, taps), top + taps[-1] * C))
    work[-1] = (work[-1][0], 0)
    for part in range(2):
        work.append((functools.partial(inputs, 0, part), None))

    load_small.wait()
    put(slice(SUM_ROWS - HEAD_ROWS, SUM_ROWS), small_v[MISC:, :].astype(F32))
    ready = SUM_ROWS - HEAD_ROWS
    due = {}
    step, first = 0, 0
    while len(outs) < chunks or step < len(work):
        gap = SUM_GAP if step < len(work) else TAIL_GAP
        for k in range(chunks):
            if k in due and due[k][1] <= step and due[k][0] < len(stages):
                stages[due[k][0]](k)
                due[k] = (due[k][0] + 1, step + gap)
        for _ in range(SUM_ENTER):
            if first == chunks or starts[first] < ready:
                break
            due[first] = (0, step + gap)
            stage_core(first)
            first += 1
        if step < len(work):
            run, now = work[step]
            run()
            ready = ready if now is None else now
            if step == len(work) - 1:
                bottom = pltpu.make_async_copy(slope_v.at[0], d_bottom, bottom_sem)
                bottom.start()
        step += 1
    bottom.wait()
    for copy in outs:
        copy.wait()


def bias_rows(classes_all):
    return (classes_all + 7) // 8 * 8 + 16


def sum_all(classes_all, xt, slope, conv_w, conv_wt, small):
    blocks = xt.shape[1]
    chunks = len(SUM_PARTS)
    any_spec = pl.BlockSpec(memory_space=pl.ANY)
    return pl.pallas_call(
        functools.partial(sum_kernel, classes_all),
        out_shape=(jax.ShapeDtypeStruct((SUM_ROWS, C), BF), jax.ShapeDtypeStruct(slope.shape[1:], BF)),
        in_specs=[any_spec] * 4,
        out_specs=[any_spec] * 2,
        scratch_shapes=[
            pltpu.VMEM(xt.shape, BF),
            pltpu.VMEM(slope.shape, BF),
            pltpu.VMEM((TOP, 9 * C, C), BF),
            pltpu.VMEM(small.shape, BF),
            pltpu.VMEM((TOP, 8, C), F32),
            pltpu.VMEM((SUM_ROWS, C // 2), BF),
            pltpu.VMEM((SUM_ROWS, C // 2), BF),
            pltpu.VMEM((SUM_ROWS, C // 2), BF),
            pltpu.VMEM((SUM_ROWS // 2, C // 2), BF),
            pltpu.VMEM((SUM_ROWS // 4, C // 2), BF),
            pltpu.VMEM((SUM_ROWS // 16 * 3, C // 2), BF),
            pltpu.VMEM((SUM_ROWS, C), BF),
            pltpu.SemaphoreType.DMA((3 * TOP + 1,)),
            pltpu.SemaphoreType.DMA((chunks, 22)),
            pltpu.SemaphoreType.DMA((chunks, 22)),
            pltpu.SemaphoreType.DMA((chunks,)),
            pltpu.SemaphoreType.DMA,
        ]
        + [pltpu.VMEM((blocks // GROUP, DROWS, 3 * C), BF)] * GROUP
        + [pltpu.VMEM((blocks // GROUP, TOK, C), F32)] * GROUP,
        compiler_params=pltpu.CompilerParams(collective_id=1, has_side_effects=True, vmem_limit_bytes=60 * 2**20),
        name="sum_all",
    )(xt, slope, conv_wt, small)


def sum_plain(classes_all, xt, slope, conv_w, conv_wt, small):
    slots = slope.shape[1]
    chunk = min(CHUNK, slots)

    def some(c, carry):
        weights, biases, bottom = carry
        grad = 1.0
        parts, sums = [], []
        for layer in reversed(range(TOP)):
            d_pre = grad * lax.dynamic_slice_in_dim(slope[layer], c * chunk, chunk).astype(F32)
            sums.insert(0, jnp.sum(d_pre, axis=(0, 1)))
            padded = jnp.pad(d_pre.astype(BF), ((0, 0), (17, 49), (0, 0)))
            held = lax.dynamic_slice_in_dim(xt[layer], c * chunk, chunk)
            grad = 0.0
            taps = []
            for tap in range(9):
                at = 17 - 16 * (tap // 3 - 1) - (tap % 3 - 1)
                moved = padded[:, at : at + C]
                taps.append(jnp.einsum("nct,ntd->cd", held, moved, preferred_element_type=F32))
                kernel = conv_w[layer, tap * C : (tap + 1) * C]
                grad += jnp.einsum("ntd,cd->ntc", moved[:, :TOK], kernel, preferred_element_type=F32)
            parts = taps + parts
        bottom = lax.dynamic_update_slice_in_dim(bottom, grad.astype(BF), c * chunk, 0)
        return weights + jnp.concatenate(parts), biases + jnp.stack(sums), bottom

    carry = (jnp.zeros((TOP * 9 * C, C), F32), jnp.zeros((TOP, C), F32), jnp.zeros(slope.shape[1:], BF))
    weights, biases, bottom = lax.fori_loop(0, slots // chunk, some, carry)
    first = bias_rows(classes_all)
    misc = small[:MISC].astype(F32).at[first : first + TOP].set(biases)
    total = jnp.concatenate([misc, weights, small[MISC:].astype(F32)])
    return lax.psum(total.astype(BF), ("img", "grp")), bottom


class Sampler:
    def __init__(self, boxes, slot):
        level = boxes[0, 0, slot]
        self.level = level
        self.y0, self.x0 = boxes[1, 0, slot], boxes[2, 0, slot]
        self.sy, self.sx = boxes[3, 0, slot], boxes[4, 0, slot]
        self.shift = 6 - level
        self.side = jnp.left_shift(1, self.shift)
        self.offset = jnp.where(level == 0, 0, jnp.where(level == 1, 4096, jnp.where(level == 2, 5120, 5376)))
        self.cell = lax.broadcasted_iota(jnp.int32, (WIDE, WIN), 1)
        self.column = (self.cell & (self.side - 1)).astype(F32)
        self.band = lax.shift_right_logical(self.cell, self.shift)

    def across(self, moved):
        j = lax.broadcasted_iota(jnp.int32, (WIDE, WIN), 0) + moved
        at = jnp.where((j >= 0) & (j < POOL), self.x0 + j * self.sx, -64).astype(F32) * 0.25
        return jnp.maximum(1.0 - jnp.abs(at - self.column), 0.0)

    def down(self, i):
        qy = self.y0 + i * self.sy
        base = self.offset + jnp.left_shift(lax.shift_right_logical(qy, 2), self.shift)
        start = pl.multiple_of(jnp.left_shift(lax.shift_right_logical(base, 4), 4), 16)
        lead = lax.shift_right_logical(base - start, self.shift)
        fraction = (qy & 3).astype(F32) * 0.25
        row = self.band - lead
        return start, jnp.where(row == 0, 1.0 - fraction, jnp.where(row == 1, fraction, 0.0))


def head_kernel(
    slots,
    classes_all,
    images,
    boxes,
    tags,
    lines,
    p2,
    p3,
    p4,
    p5,
    conv_w_h,
    conv_wt_h,
    conv_b,
    dec_w,
    dec_b,
    pred_wt,
    pred_b,
    masks,
    xt_out,
    slope_out,
    small,
    order,
    table,
    xt,
    slope,
    up,
    up_slope,
    dpd,
    x4t,
    acc_dec,
    acc,
    misc,
    dec_sum,
    top_sum,
    bias2,
    bias_d,
    small_v,
    conv_w,
    top_wt,
    moves,
    wanted,
    probs,
    in_sem,
    w_sem,
    out_sem,
    small_sem,
    *frames,
):
    chunk = min(CHUNK, slots)
    chunks = slots // chunk
    pair = slots // images
    cells = p2.shape[0] + p3.shape[0] + p4.shape[0] + p5.shape[0]
    parts = []
    at = 0
    for k, part in enumerate((p2, p3, p4, p5)):
        parts.append(pltpu.make_async_copy(part, table.at[pl.ds(at, part.shape[0])], in_sem.at[k]))
        at += part.shape[0]
    for layer in range(LAYERS):
        parts.append(pltpu.make_async_copy(conv_w_h.at[layer], conv_w.at[layer], w_sem.at[layer]))
    parts.append(pltpu.make_async_copy(conv_wt_h.at[TOP], top_wt, w_sem.at[LAYERS]))
    xw, dpw = frames[:TEAM], frames[TEAM:]
    for part in parts:
        part.start()

    count = processed(slots, pair, tags, order)
    table[cells:, :] = jnp.zeros((table.shape[0] - cells, C), BF)
    probs[...] = jnp.zeros_like(probs)
    for frame in frames:
        frame[...] = jnp.zeros_like(frame)
    dpd[...] = jnp.zeros_like(dpd)
    acc_dec[...] = jnp.zeros_like(acc_dec)
    acc[...] = jnp.zeros_like(acc)
    top_sum[...] = jnp.zeros_like(top_sum)
    misc[...] = jnp.zeros_like(misc)
    dec_sum[...] = jnp.zeros_like(dec_sum)
    col = lax.broadcasted_iota(jnp.int32, (TOK, C), 0) & (WIDE - 1)
    off_block = jnp.where(col < POOL, 0.0, -1e12)
    for layer in range(LAYERS):
        bias2[layer] = off_block + conv_b[layer : layer + 1, :].astype(F32)
    bias_d[...] = off_block + jnp.concatenate([dec_b[0:1, :], dec_b[1:2, :]], axis=1).astype(F32)
    lane_ok = (lax.broadcasted_iota(jnp.int32, (8, TOK), 1) & (WIDE - 1)) < POOL
    row_ok = lax.broadcasted_iota(jnp.int32, (8, TOK), 0) < 4
    live = (lane_ok & row_ok).astype(F32)
    token = lax.broadcasted_iota(jnp.int32, (TOK, LINE), 0)
    pixel = lax.broadcasted_iota(jnp.int32, (TOK, LINE), 1)
    inside = (token & (WIDE - 1)) < POOL
    corner = lax.shift_right_logical(token, 4) * (2 * MASK) + (token & (WIDE - 1)) * 2
    all_lines = lines[...].reshape(images * 8, LINE).astype(BF)
    for ab in range(4):
        moves[ab] = (inside & (pixel == corner + (ab // 2 * MASK + ab % 2))).astype(F32).astype(BF)
        wanted[ab] = dot_nt(all_lines, moves[ab])
    for part in parts:
        part.wait()

    def spread(ref, value, first, last):
        ref[16 : 16 + TOK, C : 2 * C] = value.astype(BF)
        ref[16 : 16 + TOK, first * C : (first + 1) * C] = pltpu.roll(value, 1, 0).astype(BF)
        ref[16 : 16 + TOK, last * C : (last + 1) * C] = pltpu.roll(value, TOK - 1, 0).astype(BF)

    def sends(base, n):
        where = pl.ds(base + n, 1)
        return (
            pltpu.make_async_copy(xt.at[0:TOP, pl.ds(n, 1)], xt_out.at[:, where], out_sem.at[n, 0]),
            pltpu.make_async_copy(slope.at[0:TOP, pl.ds(n, 1)], slope_out.at[:, where], out_sem.at[n, 1]),
        )

    pred_row = (classes_all + 7) // 8 * 8

    def forward(base, first, group):
        def run(q, _):
            at = [first + group * q + k for k in range(group)]
            for k, n in enumerate(at):
                slot = order[base + n]
                sampler = Sampler(boxes, slot)
                across = jnp.concatenate([sampler.across(-1), sampler.across(0), sampler.across(1)], axis=0)
                for i in range(POOL):
                    start, down = sampler.down(i)
                    weights = across * jnp.concatenate([down] * 3, axis=0)
                    sampled = dot(weights.astype(BF), table[pl.ds(start, WIN), :]).astype(BF)
                    for b in range(3):
                        xw[k][16 * (i + 1) : 16 * (i + 2), b * C : (b + 1) * C] = sampled[b * WIDE : (b + 1) * WIDE]
            for layer in range(LAYERS):
                for k, n in enumerate(at):
                    xt[layer, n] = xw[k][16:XROWS, C : 2 * C].T
                    wide = jnp.concatenate([xw[k][16 * ky : 16 * ky + TOK] for ky in range(3)], axis=1)
                    pre = dot(wide, conv_w[layer]) + bias2[layer]
                    value, slope_now = gelu_both(pre)
                    slope[layer, n] = slope_now.astype(BF)
                    spread(xw[k], value, 0, 2)
            for k in range(group):
                x4 = xw[k][16 : 16 + TOK, C : 2 * C]
                x4t[k] = xw[k][16:XROWS, C : 2 * C].T
                for ab in range(4):
                    pre = dot(x4, dec_w[:, ab * C : (ab + 1) * C]) + bias_d[...]
                    value, slope_now = gelu_both(pre)
                    up[k, :, ab * C : (ab + 1) * C] = value.astype(BF)
                    up_slope[k, :, ab * C : (ab + 1) * C] = slope_now.astype(BF)
            row = lax.broadcasted_iota(jnp.int32, (16, C), 0)
            lane = lax.broadcasted_iota(jnp.int32, (1, C), 1)
            class_ids = [tags[line_of(order[base + n], pair), PIXELS % 128] for n in at]
            heads, d_logits = [], []
            for k, n in enumerate(at):
                picks = (lax.broadcasted_iota(jnp.int32, (16, classes_all), 1) == class_ids[k]).astype(F32)
                bias = jnp.sum(picks[0:1] * pred_b[...].astype(F32), axis=1, keepdims=True)
                weight = dot(picks.astype(BF), pred_wt[...])
                blocks = jnp.concatenate([jnp.where(row == ab, weight, 0.0) for ab in range(4)], axis=1).astype(BF)
                heads.append((blocks, bias))
            for k, n in enumerate(at):
                blocks, bias = heads[k]
                index = base + n
                valid = (index < count).astype(F32)
                slot = jnp.where(index < count, order[index], slots)
                line = line_of(order[index], pair)
                logit = dot_nt(blocks, up[k])[0:8] + bias
                prob = 1.0 / (1.0 + jnp.exp(-logit))
                rows = []
                for ab in range(4):
                    probs[ab, pl.ds(slot, 1), :] = prob[ab : ab + 1]
                    rows.append(wanted[ab, pl.ds(line, 1), :])
                target = jnp.concatenate(rows + [jnp.zeros((4, TOK), F32)], axis=0)
                d_logit = ((prob - target) * (valid / (MASK * MASK)) * live).astype(BF)
                d_logits.append(d_logit.astype(F32))
            sixteens = [jnp.concatenate([d, jnp.zeros((8, TOK), F32)], axis=0).astype(BF) for d in d_logits]
            outers = [dot(sixteens[k], up[k]) for k in range(group)]
            dec_total = jnp.zeros((8, C), F32)
            grads = []
            for k in range(group):
                grad = jnp.zeros((TOK, C), F32)
                for ab in range(4):
                    cols = slice(ab * C, (ab + 1) * C)
                    d_up = dot_tn(sixteens[k], heads[k][0][:, cols])
                    d_pre = d_up * up_slope[k, :, cols].astype(F32)
                    dec_total += jnp.sum(d_pre.reshape(TOK // 8, 8, C), axis=0)
                    d_pre = d_pre.astype(BF)
                    dpd[k, 0:TOK, cols] = d_pre
                    grad += dot_nt(d_pre, dec_w[:, cols])
                grads.append(grad)
            dec_sum[...] += dec_total
            top_total = jnp.zeros((8, C), F32)
            for k, n in enumerate(at):
                d_pre = grads[k] * slope[TOP, n].astype(F32)
                top_total += jnp.sum(d_pre.reshape(TOK // 8, 8, C), axis=0)
                spread(dpw[k], d_pre, 2, 0)
                wide = jnp.concatenate([dpw[k][32 - 16 * ky : 32 - 16 * ky + TOK] for ky in range(3)], axis=1)
                slope[TOP - 1, n] = (dot(wide, top_wt[...]) * slope[TOP - 1, n].astype(F32)).astype(BF)
            top_sum[...] += top_total
            for k in range(group):
                gathered = jnp.zeros((16, C), F32)
                for ab in range(4):
                    gathered += jnp.where(row == ab, outers[k][:, ab * C : (ab + 1) * C], 0.0)
                total = jnp.sum(jnp.sum(d_logits[k], axis=1, keepdims=True), axis=0, keepdims=True)
                misc[pl.ds(class_ids[k], 1), :] += jnp.sum(gathered, axis=0, keepdims=True)
                misc[pred_row : pred_row + 1, :] += jnp.where(lane == class_ids[k], total, 0.0)
            lhs = jnp.concatenate([x4t[k] for k in range(group)], axis=1)
            for ab in range(4):
                cols = slice(ab * C, (ab + 1) * C)
                rhs = jnp.concatenate([dpd[k, :, cols] for k in range(group)], axis=0)
                acc_dec[ab] += dot(lhs, rhs)
            lhs = jnp.concatenate([xt[TOP, n] for n in at], axis=1)
            for tap in range(9):
                rows = slice(32 - 16 * (tap // 3), 288 - 16 * (tap // 3))
                cols = slice(tap % 3 * C, (tap % 3 + 1) * C)
                rhs = jnp.concatenate([dpw[k][rows, cols] for k in range(group)], axis=0)
                acc[tap * C : (tap + 1) * C, :] += dot(lhs, rhs)
            for n in at:
                for copy in sends(base, n):
                    copy.start()
            return 0

        return run

    def clear(base):
        def one(n, _):
            for layer in range(TOP):
                xt[layer, n] = jnp.zeros((C, C), BF)
                slope[layer, n] = jnp.zeros((TOK, C), BF)
            for copy in sends(base, n):
                copy.start()
            return 0

        return one

    def wait_for(n, _):
        for copy in sends(0, n):
            copy.wait()
        return 0

    def run_chunk(c, _):
        base = c * chunk
        here = jnp.clip(count - base, 0, chunk)
        steps = (here + TEAM - 1) // TEAM
        lax.fori_loop(steps * TEAM, chunk, clear(base), 0)
        lax.fori_loop(0, steps, forward(base, 0, TEAM), 0)
        lax.fori_loop(0, chunk, wait_for, 0)
        return 0

    if chunks == 1:
        run_chunk(0, 0)
    else:
        lax.fori_loop(0, chunks, run_chunk, 0)

    misc[pred_row + 8 : pred_row + 9, :] = jnp.sum(dec_sum[...], axis=0, keepdims=True)
    first = bias_rows(classes_all) + TOP
    misc[first : first + 1, :] = jnp.sum(top_sum[...], axis=0, keepdims=True)
    small_v[0:MISC, :] = misc[...].astype(BF)
    small_v[MISC : MISC + 9 * C, :] = acc[...].astype(BF)
    for ab in range(4):
        first = MISC + 9 * C + ab * C
        small_v[first : first + C, :] = acc_dec[ab].astype(BF)
    send_small = pltpu.make_async_copy(small_v, small, small_sem)
    send_small.start()
    image = jnp.zeros((slots, LINE), F32)
    for ab in range(4):
        prob = probs[ab, 0:slots, :]
        high = prob.astype(BF)
        low = (prob - high.astype(F32)).astype(BF)
        image += dot(high, moves[ab]) + dot(low, moves[ab])
    masks[...] = image[:, 0:PIXELS]
    send_small.wait()


def processed(slots, pair, tags, order):
    def collect(slot, count):
        order[count] = slot
        return count + tags[line_of(slot, pair), PIXELS % 128 + 1]

    count = lax.fori_loop(0, slots, collect, 0)
    order[count] = 0
    return count


def line_of(slot, pair):
    return slot // pair * 8 + slot % pair


def head(slots, classes_all, boxes, tags, lines, p2, p3, p4, p5, conv_w, conv_wt, *weights):
    chunk = min(CHUNK, slots)
    images = lines.shape[0]
    cells = p2.shape[0] + p3.shape[0] + p4.shape[0] + p5.shape[0]
    any_spec = pl.BlockSpec(memory_space=pl.ANY)
    vmem = pl.BlockSpec(memory_space=pltpu.VMEM)
    smem = pl.BlockSpec(memory_space=pltpu.SMEM)
    return pl.pallas_call(
        functools.partial(head_kernel, slots, classes_all, images),
        out_shape=(
            jax.ShapeDtypeStruct((slots, PIXELS), F32),
            jax.ShapeDtypeStruct((TOP, slots, C, C), BF),
            jax.ShapeDtypeStruct((TOP, slots, TOK, C), BF),
            jax.ShapeDtypeStruct((MISC + HEAD_ROWS, C), BF),
        ),
        in_specs=[smem, smem, vmem] + [any_spec] * 6 + [vmem] * 5,
        out_specs=[vmem] + [any_spec] * 3,
        scratch_shapes=[
            pltpu.SMEM((slots + 2,), jnp.int32),
            pltpu.VMEM((cells + WIN, C), BF),
            pltpu.VMEM((LAYERS, chunk, C, C), BF),
            pltpu.VMEM((LAYERS, chunk, TOK, C), BF),
            pltpu.VMEM((TEAM, TOK, 4 * C), BF),
            pltpu.VMEM((TEAM, TOK, 4 * C), BF),
            pltpu.VMEM((TEAM, C, 4 * C), BF),
            pltpu.VMEM((TEAM, C, C), BF),
            pltpu.VMEM((4, C, C), F32),
            pltpu.VMEM((9 * C, C), F32),
            pltpu.VMEM((MISC, C), F32),
            pltpu.VMEM((8, C), F32),
            pltpu.VMEM((8, C), F32),
            pltpu.VMEM((LAYERS, TOK, C), F32),
            pltpu.VMEM((TOK, C), F32),
            pltpu.VMEM((MISC + HEAD_ROWS, C), BF),
            pltpu.VMEM(conv_w.shape, BF),
            pltpu.VMEM((9 * C, C), BF),
            pltpu.VMEM((4, TOK, LINE), BF),
            pltpu.VMEM((4, images * 8, TOK), F32),
            pltpu.VMEM((4, slots + 8, TOK), F32),
            pltpu.SemaphoreType.DMA((4,)),
            pltpu.SemaphoreType.DMA((LAYERS + 1,)),
            pltpu.SemaphoreType.DMA((chunk, 2)),
            pltpu.SemaphoreType.DMA,
        ]
        + [pltpu.VMEM((XROWS, 3 * C), BF)] * TEAM
        + [pltpu.VMEM((DROWS, 3 * C), BF)] * TEAM,
        compiler_params=pltpu.CompilerParams(vmem_limit_bytes=60 * 2**20),
        name="head",
    )(boxes, tags, lines, p2, p3, p4, p5, conv_w, conv_wt, *weights)


def finish_kernel(
    slots,
    classes_all,
    images,
    boxes,
    tags,
    dx0,
    summed,
    g2,
    g3,
    g4,
    g5,
    conv_g,
    conv_bg,
    dec_g,
    dec_bg,
    pred_g,
    pred_bg,
    order,
    table_grad,
    sum_v,
    conv_v,
    dec_v,
    in_sem,
    conv_sem,
    out_sem,
):
    pieces = LAYERS
    size = 9 * C
    loads = []
    for k in range(pieces):
        at = pl.ds(MISC + k * size, size)
        loads.append(pltpu.make_async_copy(summed.at[at], sum_v.at[at], in_sem.at[k]))
    for k, at in enumerate((pl.ds(0, MISC), pl.ds(SUM_ROWS - DEC, DEC))):
        loads.append(pltpu.make_async_copy(summed.at[at], sum_v.at[at], in_sem.at[pieces + k]))
    for load in loads:
        load.start()
    pair = slots // images
    count = processed(slots, pair, tags, order)
    table_grad[...] = jnp.zeros_like(table_grad)
    stores = []
    for k in range(pieces):
        loads[k].wait()
        conv_v[k] = sum_v[MISC + k * size : MISC + (k + 1) * size, :].astype(F32)
        stores.append(pltpu.make_async_copy(conv_v.at[k], conv_g.at[k], conv_sem.at[k]))
        stores[-1].start()

    for load in loads[pieces:]:
        load.wait()
    for ab in range(4):
        first = SUM_ROWS - DEC + ab * C
        dec_v[:, ab * C : (ab + 1) * C] = sum_v[first : first + C, :].astype(F32)
    stores.append(pltpu.make_async_copy(dec_v, dec_g, conv_sem.at[pieces]))
    stores[-1].start()

    def scatter(n, _):
        sampler = Sampler(boxes, order[n])
        across = sampler.across(0)

        def rows_of(cells):
            def run():
                for i in range(POOL):
                    start, down = sampler.down(i)
                    weights = (across * down).astype(BF)[:, 0:cells]
                    table_grad[pl.ds(start, cells), :] += dot_tn(weights, dx0[n, i * WIDE : (i + 1) * WIDE, :])

            return run

        pl.when(sampler.level == 0)(rows_of(128))
        pl.when(sampler.level == 1)(rows_of(64))
        pl.when(sampler.level >= 2)(rows_of(32))
        return 0

    lax.fori_loop(0, count, scatter, 0)
    at = 0
    for k, part in enumerate((g2, g3, g4, g5)):
        stores.append(pltpu.make_async_copy(table_grad.at[pl.ds(at, part.shape[0])], part, out_sem.at[k]))
        stores[-1].start()
        at += part.shape[0]
    misc = sum_v[0:MISC, :].astype(F32)
    pred_row = (classes_all + 7) // 8 * 8
    bias_row = bias_rows(classes_all)
    pred_g[...] = misc[0:classes_all]
    pred_bg[...] = misc[pred_row : pred_row + 1]
    dec_bg[...] = misc[pred_row + 8 : pred_row + 9]
    conv_bg[...] = misc[bias_row : bias_row + LAYERS]
    for store in stores:
        store.wait()


def finish(slots, classes_all, images, boxes, tags, dx0, summed, levels):
    cells = sum(levels)
    any_spec = pl.BlockSpec(memory_space=pl.ANY)
    vmem = pl.BlockSpec(memory_space=pltpu.VMEM)
    smem = pl.BlockSpec(memory_space=pltpu.SMEM)
    return pl.pallas_call(
        functools.partial(finish_kernel, slots, classes_all, images),
        out_shape=(
            *(jax.ShapeDtypeStruct((level, C), F32) for level in levels),
            jax.ShapeDtypeStruct((LAYERS, 9 * C, C), F32),
            jax.ShapeDtypeStruct((LAYERS, C), F32),
            jax.ShapeDtypeStruct((C, 4 * C), F32),
            jax.ShapeDtypeStruct((1, C), F32),
            jax.ShapeDtypeStruct((classes_all, C), F32),
            jax.ShapeDtypeStruct((1, C), F32),
        ),
        in_specs=[smem, smem, vmem, any_spec],
        out_specs=[any_spec] * 5 + [vmem, any_spec, vmem, vmem, vmem],
        scratch_shapes=[
            pltpu.SMEM((slots + 2,), jnp.int32),
            pltpu.VMEM((cells + WIN, C), F32),
            pltpu.VMEM((SUM_ROWS, C), BF),
            pltpu.VMEM((LAYERS, 9 * C, C), F32),
            pltpu.VMEM((C, 4 * C), F32),
            pltpu.SemaphoreType.DMA((LAYERS + 2,)),
            pltpu.SemaphoreType.DMA((LAYERS + 1,)),
            pltpu.SemaphoreType.DMA((4,)),
        ],
        compiler_params=pltpu.CompilerParams(vmem_limit_bytes=60 * 2**20),
        name="finish",
    )(boxes, tags, dx0, summed)


def body(
    images,
    groups,
    p2,
    p3,
    p4,
    p5,
    roi_boxes,
    recv_index,
    classes,
    targets,
    conv_weights,
    conv_biases,
    deconv_weight,
    deconv_bias,
    predictor_weight,
    predictor_bias,
):
    slots = roi_boxes.shape[-1]
    classes_all = predictor_weight.shape[1]
    boxes = roi_boxes[0].transpose(1, 0, 2)
    lines, tags, conv_wt = exchange(
        images, slots // images, targets[0, 0], recv_index[0], classes[0], conv_weights
    )
    masks, xt, slope, small = head(
        slots,
        classes_all,
        boxes,
        tags,
        lines,
        p2[0, 0],
        p3[0, 0],
        p4[0, 0],
        p5[0, 0],
        conv_weights,
        conv_wt,
        conv_biases,
        deconv_weight,
        deconv_bias.reshape(2, C // 2),
        predictor_weight.T,
        predictor_bias[None, :],
    )
    total = sum_all if images == 8 and groups == 4 else sum_plain
    summed, dx0 = total(classes_all, xt, slope, conv_weights, conv_wt, small)
    levels = [p.shape[2] for p in (p2, p3, p4, p5)]
    g2, g3, g4, g5, conv_g, conv_bg, dec_g, dec_bg, pred_g, pred_bg = finish(
        slots, classes_all, images, boxes, tags, dx0, summed, levels
    )
    return (
        masks[None, None],
        g2[None, None],
        g3[None, None],
        g4[None, None],
        g5[None, None],
        conv_g,
        conv_bg,
        dec_g,
        dec_bg[0],
        pred_g.T,
        pred_bg[0, :classes_all],
    )


def solution(mesh):
    split = P("img", "grp", None, None)
    in_specs = (split,) * 5 + (P("img", "grp", None),) * 2 + (split,) + (P(),) * 6
    out_specs = (split,) * 5 + (P(),) * 6
    return jax.shard_map(
        functools.partial(body, mesh.shape["img"], mesh.shape["grp"]),
        mesh=mesh,
        in_specs=in_specs,
        out_specs=out_specs,
        check_vma=False,
    )
```
